32 devices in a mesh: dp: 8 (over z, y), tensor: 4 (over x, core).
Axes of the slice: x: 2, y: 2, z: 4, core: 2. Of those that a mesh axis runs over, the one named last changes fastest.
Arguments:
- tokens: bfloat16 [4608, 1024], P('dp'), may hold values from -6 to 6
- cotangent: bfloat16 [4608, 1024], P('dp'), may hold values from -6 to 6
- lengths: int32 [8, 3], P('dp'), may hold values from 1 to 512, 540 in all within a row
- packing: int32 [4608], replicated, may hold values from 0 to 4607, as said below
- w_qkv: float32 [3, 1024, 1024], P(None, None, 'tensor'), may hold values from -0.1875 to 0.1875
- w_out: float32 [1024, 1024], P('tensor'), may hold values from -0.75 to 0.75
- w_up: float32 [1024, 4096], P(None, 'tensor'), may hold values from -0.1875 to 0.1875
- w_down: float32 [4096, 1024], P('tensor'), may hold values from -0.09375 to 0.09375
- bias_qv: float32 [2, 1024], P(None, 'tensor'), may hold values from -1.75 to 1.75
- bias_up: float32 [4096], P('tensor'), may hold values from -1.75 to 1.75
- vectors: float32 [6, 1024], replicated, may hold values from -2.5 to 2.5
- mom_qkv: float32 [3, 1024, 1024], P(None, None, 'tensor'), may hold values from -128 to 128
- mom_out: float32 [1024, 1024], P('tensor'), may hold values from -128 to 128
- mom_up: float32 [1024, 4096], P(None, 'tensor'), may hold values from -128 to 128
- mom_down: float32 [4096, 1024], P('tensor'), may hold values from -128 to 128
- mom_bias_qv: float32 [2, 1024], P(None, 'tensor'), may hold values from -128 to 128
- mom_bias_up: float32 [4096], P('tensor'), may hold values from -128 to 128
- mom_vectors: float32 [6, 1024], replicated, may hold values from -128 to 128
Outputs:
- output: bfloat16 [4608, 1024], P('dp')
- grad_tokens: float32 [4608, 1024], P('dp')
- grad_qkv: float32 [3, 1024, 1024], P(None, None, 'tensor')
- grad_out: float32 [1024, 1024], P('tensor')
- grad_up: float32 [1024, 4096], P(None, 'tensor')
- grad_down: float32 [4096, 1024], P('tensor')
- grad_bias_qv: float32 [2, 1024], P(None, 'tensor')
- grad_bias_up: float32 [4096], P('tensor')
- grad_vectors: float32 [6, 1024], replicated
- moment_qkv: float32 [3, 1024, 1024], P(None, None, 'tensor')
- moment_out: float32 [1024, 1024], P('tensor')
- moment_up: float32 [1024, 4096], P(None, 'tensor')
- moment_down: float32 [4096, 1024], P('tensor')
- moment_bias_qv: float32 [2, 1024], P(None, 'tensor')
- moment_bias_up: float32 [4096], P('tensor')
- moment_vectors: float32 [6, 1024], replicated
- master_qkv: float32 [3, 1024, 1024], P(None, 'dp', 'tensor')
- master_out: float32 [1024, 1024], P('tensor', 'dp')
- master_up: float32 [1024, 4096], P('dp', 'tensor')
- master_down: float32 [4096, 1024], P('tensor', 'dp')
- master_bias_qv: float32 [2, 1024], P(None, 'tensor')
- master_bias_up: float32 [4096], P('tensor')
- master_vectors: float32 [6, 1024], replicated
The draws below stay inside these ranges and needn't reach their ends.
Inputs may be any that keep to these rules, and one draw needn't show every extreme that they name: Each row lists the lengths of the 3 sequences that fill, in order, the first 540 slots of one index of dp; its last 36 slots are padding. `packing`: A permutation of the rows; the slots of one index of dp take the same number of rows, 576 divided by the size of dp, from each index of dp.
All inputs are finite; a program needn't handle non-finite values.
Results may differ from the reference program's by a relative error of at most 0.018.
The reference program's roundings to bfloat16 on the way count: a program that leaves them out, or rounds other values in their place, can miss the bound.
Values may be sent and summed in bfloat16 or wider, within the bound.
A program may use at most 192 MiB of HBM per device.

```python
import math
import jax
import jax.numpy as jnp
import numpy as np
from jax import lax

D = 1024
FF = 4096
HEADS = 16
HEAD = 64
TOK_DEV = 576
SEQ = 512
SEQS_DEV = 3
PAD_DEV = 36
TOKENS = 4608
N_DP = 8


def draw_packing(key, part):
    dp_count = TOKENS // TOK_DEV
    per_peer = TOK_DEV // dp_count

    def source_order(source):
        shuffled = jax.random.permutation(jax.random.fold_in(key, source), TOK_DEV).astype(jnp.int32)
        return (source * TOK_DEV + shuffled).reshape(dp_count, per_peer)
    grouped = jax.vmap(source_order)(jnp.arange(dp_count, dtype=jnp.int32))
    by_target = jnp.transpose(grouped, (1, 0, 2)).reshape(dp_count, TOK_DEV)

    def target_mix(target, entries):
        mixing = jax.random.permutation(jax.random.fold_in(key, 100000 + target), TOK_DEV)
        return entries[mixing]
    mixed = jax.vmap(target_mix)(jnp.arange(dp_count, dtype=jnp.int32), by_target)
    return mixed.reshape(TOKENS).astype(jnp.int32)


def draw_vectors(key, part):
    row_ids = jnp.arange(6, dtype=jnp.int32)[:, None]
    gain_row = (row_ids == 1) | (row_ids == 4)
    noise = jnp.clip(jax.random.normal(key, (6, D), jnp.float32), -4.0, 4.0)
    gains = 1.0 + 0.1 * noise
    shifts = 0.3 * noise
    return jnp.where(gain_row, gains, shifts).astype(jnp.float32)


def levels(key, dims, split, low, top_value):
    def one(axis_at, shards_of):
        heights = jax.random.uniform(jax.random.fold_in(jax.random.fold_in(key, 6), axis_at), (shards_of,), jnp.float32, low / len(split), top_value / len(split))
        return jnp.repeat(jnp.exp(heights), dims[axis_at] // shards_of).reshape((-1,) + (1,) * (len(dims) - axis_at - 1))

    gain = one(*split[0])
    for cut in split[1:]:
        gain = gain * one(*cut)
    return gain


def split_up(count, total, reach, slope):
    weights = [(1 << 20) // math.isqrt(grade ** slope) + 1 for grade in range(2, count + 1)]
    rest, given = total - reach - (count - 1), [1] * (count - 1)
    while rest > 0:
        candidates = [i for i in range(count - 1) if given[i] < reach]
        whole, left = sum([weights[i] for i in candidates]), rest
        for i in candidates:
            extra = min(reach - given[i], max(1, left * weights[i] // whole), rest)
            given[i] = given[i] + extra
            rest = rest - extra
    return np.array([reach] + given)


def uneven(own_key, count, total, most, lean):
    if count == 2:
        one = jax.random.randint(own_key, (), max(1, total - most), min(most, total - 1) + 1)
        return jnp.stack([one, total - one])
    tallies = jnp.asarray(split_up(count, total, most, lean), jnp.int32)
    twos = (count - 1) // 2
    giver, receiver = tallies[1:1 + 2 * twos:2], tallies[2:2 + 2 * twos:2]
    margin = jnp.minimum(giver - 1, most - receiver)
    moved = jax.random.randint(jax.random.fold_in(own_key, 1), (twos,), 0, 1 << 20) % (margin + 1)
    tallies = tallies.at[1:1 + 2 * twos:2].set(giver - moved).at[2:2 + 2 * twos:2].set(receiver + moved)
    return tallies[jax.random.permutation(jax.random.fold_in(own_key, 2), count)]


def bell_draw(own_key, dims, deviation, bound, cuts=(), kind=jnp.bfloat16):
    level = levels(own_key, dims, cuts, -0.22, 0.18) if cuts else 1.0
    values = jax.random.normal(own_key, dims, jnp.float32) * deviation * level
    return jnp.minimum(jnp.maximum(values, -bound), bound).astype(kind)


def setup_inputs(seed: int = 0) -> dict:
    streams_of = jax.random.split(jax.random.key(seed), 19)
    tokens = bell_draw(streams_of[0], (TOKENS, D), 1.0, 6.0, ((0, 8),))
    cotangent = bell_draw(streams_of[1], (TOKENS, D), 1.0, 6.0, ((0, 8),))
    lengths = jax.vmap(lambda own: uneven(own, SEQS_DEV, TOK_DEV - PAD_DEV, SEQ, 2))(jax.random.split(streams_of[2], N_DP)).reshape((N_DP, SEQS_DEV)).astype(jnp.int32)
    packing = draw_packing(jax.random.fold_in(streams_of[18], 71), 0)
    w_qkv = bell_draw(streams_of[4], (3, D, D), D ** -0.5, 0.1875, ((2, 4),), jnp.float32)
    w_out = bell_draw(streams_of[5], (D, D), (D // 16) ** -0.5, 0.75, ((0, 4),), jnp.float32)
    w_up = bell_draw(streams_of[6], (D, FF), D ** -0.5, 0.1875, ((1, 4),), jnp.float32)
    w_down = bell_draw(streams_of[7], (FF, D), FF ** -0.5, 0.09375, ((0, 4),), jnp.float32)
    bias_qv = bell_draw(streams_of[8], (2, D), 0.3, 1.75, ((1, 4),), jnp.float32)
    bias_up = bell_draw(streams_of[9], (FF,), 0.3, 1.75, ((0, 4),), jnp.float32)
    vectors = draw_vectors(jax.random.fold_in(streams_of[18], 71), 0)
    mom_qkv = bell_draw(streams_of[11], (3, D, D), (0.3 * TOKENS ** 0.5), 128.0, ((2, 4),), jnp.float32)
    mom_out = bell_draw(streams_of[12], (D, D), (0.3 * TOKENS ** 0.5), 128.0, ((0, 4),), jnp.float32)
    mom_up = bell_draw(streams_of[13], (D, FF), (0.3 * TOKENS ** 0.5), 128.0, ((1, 4),), jnp.float32)
    mom_down = bell_draw(streams_of[14], (FF, D), (0.3 * TOKENS ** 0.5), 128.0, ((0, 4),), jnp.float32)
    mom_bias_qv = bell_draw(streams_of[15], (2, D), (0.3 * TOKENS ** 0.5), 128.0, ((1, 4),), jnp.float32)
    mom_bias_up = bell_draw(streams_of[16], (FF,), (0.3 * TOKENS ** 0.5), 128.0, ((0, 4),), jnp.float32)
    mom_vectors = bell_draw(streams_of[17], (6, D), (0.3 * TOKENS ** 0.5), 128.0, (), jnp.float32)
    return {"tokens": tokens, "cotangent": cotangent, "lengths": lengths, "packing": packing, "w_qkv": w_qkv, "w_out": w_out, "w_up": w_up, "w_down": w_down, "bias_qv": bias_qv, "bias_up": bias_up, "vectors": vectors, "mom_qkv": mom_qkv, "mom_out": mom_out, "mom_up": mom_up, "mom_down": mom_down, "mom_bias_qv": mom_bias_qv, "mom_bias_up": mom_bias_up, "mom_vectors": mom_vectors}


highest = lax.Precision.HIGHEST
eps_norm = 1e-05
coef_one = 3.4445
coef_two = -4.775
coef_three = 2.0315
momentum_decay = 0.9
rate_matrix = 0.1
masked_score = -1000000000.0

@jax.custom_vjp
def low(v):
    return lax.optimization_barrier(v.astype(jnp.bfloat16)).astype(jnp.float32)

@jax.custom_vjp
def low_back(v):
    return v

def low_keep(v):
    return (low(v), None)

def low_pass(kept, grad):
    return (grad,)

def back_keep(v):
    return (v, None)

def back_low(kept, grad):
    return (low(grad),)
low.defvjp(low_keep, low_pass)
low_back.defvjp(back_keep, back_low)

def segment_layout(length_row, row_count):
    seq_ends = jnp.cumsum(length_row, dtype=jnp.int32)
    position = jnp.arange(row_count, dtype=jnp.int32)
    counted = lax.optimization_barrier(jnp.sum((position[:, None] >= seq_ends[None, :]).astype(jnp.int32), axis=1)).astype(jnp.int32)
    filled = seq_ends[-1]
    beyond = jnp.maximum(position - filled, 0).astype(jnp.int32)
    return ((counted + beyond).astype(jnp.int32), (position < filled).astype(jnp.float32))

def norm_rows(values, gain_row, shift_row):
    average = lax.optimization_barrier(jnp.mean(values, axis=-1, keepdims=True))
    centred = values - average
    variance = lax.optimization_barrier(jnp.mean(centred * centred, axis=-1, keepdims=True))
    return centred * lax.rsqrt(variance + eps_norm) * gain_row + shift_row

def layer_group(lowered, group_x, segments):
    wqkv_b, wout_b, wup_b, wdown_b, bias_pair, bias_hidden, vector_rows = lowered
    row_count = group_x.shape[0]
    projected = jnp.einsum('td,kde->kte', group_x, wqkv_b, precision=highest)
    queries = low_back(low(projected[0] + bias_pair[0])).reshape(row_count, HEADS, HEAD)
    keys_all = low_back(low(projected[1])).reshape(row_count, HEADS, HEAD)
    values_all = low_back(low(projected[2] + bias_pair[1])).reshape(row_count, HEADS, HEAD)
    raw_scores = jnp.einsum('qhd,khd->hqk', queries, keys_all, precision=highest)
    scores = low_back(raw_scores * HEAD ** (-0.5))
    same_seg = segments[:, None] == segments[None, :]
    masked = jnp.where(same_seg[None], scores, masked_score)
    probabilities = low(jax.nn.softmax(masked, axis=-1))
    context = jnp.einsum('hqk,khd->qhd', probabilities, values_all, precision=highest).reshape(row_count, D)
    context = low_back(low(context))
    attn_branch = low_back(jnp.dot(context, wout_b, precision=highest))
    mid_rows = group_x + attn_branch + vector_rows[0]
    hidden = norm_rows(mid_rows, vector_rows[1], vector_rows[2])
    pre_act = low_back(jnp.dot(low(hidden), wup_b, precision=highest) + bias_hidden)
    activated = low(jax.nn.gelu(pre_act, approximate=False))
    mlp_branch = low_back(jnp.dot(activated, wdown_b, precision=highest))
    return norm_rows(hidden + mlp_branch + vector_rows[3], vector_rows[4], vector_rows[5])

def orthogonal(moment):
    row_count, col_count = moment.shape
    current = moment * lax.rsqrt(jnp.sum(moment * moment) + 1e-07)
    if row_count > col_count:
        current = current.T
    for sweep in range(5):
        product = jnp.dot(current, current.T, precision=highest)
        mixing = coef_two * product + coef_three * jnp.dot(product, product, precision=highest)
        current = coef_one * current + jnp.dot(mixing, current, precision=highest)
    if row_count > col_count:
        current = current.T
    return current * (0.2 * math.sqrt(max(row_count, col_count)))

def reference(tokens, cotangent, lengths, packing, w_qkv, w_out, w_up, w_down, bias_qv, bias_up, vectors, mom_qkv, mom_out, mom_up, mom_down, mom_bias_qv, mom_bias_up, mom_vectors):
    packed_rows = tokens.astype(jnp.float32)[packing].reshape(N_DP, TOK_DEV, D)
    packed_grad = cotangent.astype(jnp.float32)[packing].reshape(N_DP, TOK_DEV, D)
    segment_rows, valid_rows = jax.vmap(lambda length_row: segment_layout(length_row, TOK_DEV))(lengths)

    def forward(params, inputs):
        lowered = (low(params[0]), low(params[1]), low(params[2]), low(params[3]), params[4], params[5], params[6])
        checked = jax.checkpoint(layer_group)
        return lax.map(lambda group_pair: checked(lowered, group_pair[0], group_pair[1]), (inputs, segment_rows))
    params = (w_qkv, w_out, w_up, w_down, bias_qv, bias_up, vectors)
    outputs, pullback = jax.vjp(forward, params, packed_rows)
    gradients, grad_packed = pullback(packed_grad * valid_rows[..., None])
    inverse = jnp.argsort(packing).astype(jnp.int32)
    output = outputs.reshape(TOKENS, D)[inverse].astype(jnp.bfloat16)
    grad_tokens = grad_packed.reshape(TOKENS, D)[inverse]
    moments_old = (mom_qkv, mom_out, mom_up, mom_down, mom_bias_qv, mom_bias_up, mom_vectors)
    moments_new = tuple((momentum_decay * old_value + grad_value for old_value, grad_value in zip(moments_old, gradients)))
    steps_matrix = (jax.vmap(orthogonal)(moments_new[0]), orthogonal(moments_new[1]), orthogonal(moments_new[2]), orthogonal(moments_new[3]))
    masters = []
    for position in range(4):
        masters.append(params[position] - rate_matrix * steps_matrix[position])
    rate_vector = 0.2 * TOKENS ** (-0.5)
    for position in range(4, 7):
        masters.append(params[position] - rate_vector * moments_new[position])
    return (output, grad_tokens, gradients[0], gradients[1], gradients[2], gradients[3], gradients[4], gradients[5], gradients[6], moments_new[0], moments_new[1], moments_new[2], moments_new[3], moments_new[4], moments_new[5], moments_new[6], masters[0], masters[1], masters[2], masters[3], masters[4], masters[5], masters[6])
```

```python
import functools
import math

import jax
import jax.numpy as jnp
from jax import lax
from jax.experimental import pallas as pl
from jax.experimental.pallas import tpu as pltpu
from jax.sharding import PartitionSpec as P

D = 1024
HEAD = 64

eps_norm = 1e-05
coef_one = 3.4445
coef_two = -4.775
coef_three = 2.0315
momentum_decay = 0.9
rate_matrix = 0.1
masked_score = -1000000000.0
bf16 = jnp.bfloat16
f32 = jnp.float32


def short(value):
    return value.astype(bf16)


def wide(value):
    return value.astype(f32)


def mm(left, right):
    return jnp.dot(short(left), short(right), preferred_element_type=f32)


def mm_nt(left, right):
    return lax.dot_general(
        short(left), short(right), (((1,), (1,)), ((), ())), preferred_element_type=f32
    )


def mm_tn(left, right):
    return lax.dot_general(
        short(left), short(right), (((0,), (0,)), ((), ())), preferred_element_type=f32
    )


def norm_forward(values, gain_row, shift_row):
    average = jnp.mean(values, axis=-1, keepdims=True)
    centred = values - average
    variance = jnp.mean(centred * centred, axis=-1, keepdims=True)
    inverse = lax.rsqrt(variance + eps_norm)
    normed = centred * inverse
    return (normed, inverse, normed * gain_row + shift_row)


def norm_backward(upstream, normed, inverse, gain_row):
    scaled = upstream * gain_row
    centre_term = jnp.mean(scaled, axis=-1, keepdims=True)
    slope_term = jnp.mean(scaled * normed, axis=-1, keepdims=True)
    return inverse * (scaled - centre_term - normed * slope_term)


class Ring:
    def __init__(self, axes, sizes, digit, members=None):
        self.axes = axes
        self.count = sizes[digit]
        self.below = math.prod(sizes[digit + 1 :])
        self.total = math.prod(sizes)
        self.members = members

    def send(self, value, offset):
        count, below = self.count, self.below
        pairs = []
        for i in range(self.total):
            if self.members is not None and not self.members(i):
                continue
            at = (i // below) % count
            pairs.append((i, i + ((at + offset) % count - at) * below))
        return lax.ppermute(value, self.axes, pairs)

    def place(self, linear):
        return (linear // self.below) % self.count


def cut(value, index, size, axis):
    return lax.dynamic_slice_in_dim(value, index * size, size, axis)


def ring_scatter(value, axis, ring, place):
    size = value.shape[axis] // ring.count
    if ring.count == 1:
        return wide(value)
    total = short(cut(value, (place - 1) % ring.count, size, axis))
    for step in range(ring.count - 1):
        arrived = ring.send(total, 1)
        mine = cut(value, (place - 2 - step) % ring.count, size, axis)
        total = wide(mine) + wide(arrived)
        if step < ring.count - 2:
            total = short(total)
    return total


def ring_gather(piece, axis, ring, place):
    if ring.count == 1:
        return piece
    size = piece.shape[axis]
    shape = list(piece.shape)
    shape[axis] = size * ring.count
    whole = lax.dynamic_update_slice_in_dim(
        jnp.zeros(shape, piece.dtype), piece, place * size, axis
    )
    for step in range(1, ring.count):
        piece = ring.send(piece, 1)
        whole = lax.dynamic_update_slice_in_dim(
            whole, piece, ((place - step) % ring.count) * size, axis
        )
    return whole


def ring_sum_kernel(
    inner, halves, x_ref, small_ref, o_ref, small_sum_ref, got, small_got, send_sems, recv_sems, small_sems
):
    count = lax.axis_size("dp")
    index = lax.axis_index("dp")
    team = lax.axis_index("tensor")
    outer = count // inner
    if inner == 2:
        place = jnp.where(index % 2 == 0, index // 2, count - 1 - index // 2)

        def device(p):
            return jnp.where(p < outer, 2 * p, 2 * (count - 1 - p) + 1)
    else:
        place = index

        def device(p):
            return p

    targets = (device((place + 1) % count), device((place + count - 1) % count))
    barrier = pltpu.get_barrier_semaphore()

    def greet(hop, carry):
        pl.semaphore_signal(
            barrier,
            inc=1,
            device_id=((index + hop) % count, team),
            device_id_type=pl.DeviceIdType.MESH,
        )
        return carry

    lax.fori_loop(1, count, greet, 0)
    pl.semaphore_wait(barrier, count - 1)
    half = x_ref.shape[0] // 2
    chunk = half // count
    sub = chunk // halves
    streams = [(d, h) for h in range(halves) for d in range(2)]

    def rows(d, h, hop):
        at = (place + count - hop) % count if d == 0 else (place + hop) % count
        return pl.ds(pl.multiple_of(d * half + at * chunk + h * sub, 8), sub)

    def copy(d, h, step, src, dst):
        return pltpu.make_async_remote_copy(
            src_ref=src,
            dst_ref=dst,
            send_sem=send_sems.at[step, d, h],
            recv_sem=recv_sems.at[step, d, h],
            device_id=(targets[d], team),
            device_id_type=pl.DeviceIdType.MESH,
        )

    def copies(step):
        made = []
        for d, h in streams:
            if step < count - 1:
                slot = got.at[step, d, pl.ds(h * sub, sub)]
                src = x_ref.at[rows(d, h, 1)] if step == 0 else got.at[step - 1, d, pl.ds(h * sub, sub)]
                made.append(copy(d, h, step, src, slot))
            else:
                at = o_ref.at[rows(d, h, step - (count - 1))]
                made.append(copy(d, h, step, at, at))
        return made

    everything = []
    flying = copies(0)
    for one in flying:
        one.start()
    everything += flying

    def small_copy(hop):
        return pltpu.make_async_remote_copy(
            src_ref=small_ref,
            dst_ref=small_got.at[hop],
            send_sem=small_sems.at[0, hop],
            recv_sem=small_sems.at[1, hop],
            device_id=((index + hop) % count, team),
            device_id_type=pl.DeviceIdType.MESH,
        )

    def small_send(hop, carry):
        small_copy(hop).start()
        return carry

    def small_wait(hop, total):
        one = small_copy(hop)
        one.wait_send()
        one.wait_recv()
        return total + wide(small_got[hop])

    lax.fori_loop(1, count, small_send, 0)
    for step in range(2 * (count - 1)):
        following = copies(step + 1) if step < 2 * count - 3 else [None] * len(streams)
        for (d, h), one, then in zip(streams, flying, following):
            one.wait_recv()
            if step < count - 1:
                total = wide(got[step, d, pl.ds(h * sub, sub)]) + wide(x_ref[rows(d, h, step + 2)])
                if step < count - 2:
                    got[step, d, pl.ds(h * sub, sub)] = short(total)
                else:
                    o_ref[rows(d, h, 0)] = short(total)
            if then is not None:
                then.start()
        flying = following
        everything += [one for one in following if one is not None]
    small_sum_ref[...] = lax.fori_loop(1, count, small_wait, wide(small_ref[...]))
    for one in everything:
        one.wait_send()


def ring_sum(value, small, inner, groups):
    length, columns = value.shape
    halves = 2 if length % (64 * groups) == 0 else 1
    steps = 2 * (groups - 1)
    chunk = length // 2 // groups
    return pl.pallas_call(
        functools.partial(ring_sum_kernel, inner, halves),
        name="ring_sum",
        out_shape=(
            jax.ShapeDtypeStruct(value.shape, bf16),
            jax.ShapeDtypeStruct(small.shape, f32),
        ),
        in_specs=[pl.BlockSpec(memory_space=pltpu.VMEM)] * 2,
        out_specs=[pl.BlockSpec(memory_space=pltpu.VMEM)] * 2,
        scratch_shapes=[
            pltpu.VMEM((groups - 1, 2, chunk, columns), bf16),
            pltpu.VMEM((groups, *small.shape), bf16),
            pltpu.SemaphoreType.DMA((steps, 2, halves)),
            pltpu.SemaphoreType.DMA((steps, 2, halves)),
            pltpu.SemaphoreType.DMA((2, groups)),
        ],
        compiler_params=pltpu.CompilerParams(
            collective_id=0, has_side_effects=True, vmem_limit_bytes=40 * 2**20
        ),
        cost_estimate=pl.CostEstimate(
            flops=length * columns, bytes_accessed=4 * length * columns, transcendentals=0
        ),
    )(value, small)


def dot(left, right):
    return jnp.dot(left, right, preferred_element_type=f32)

def dot_nt(left, right):
    return lax.dot_general(left, right, (((1,), (1,)), ((), ())), preferred_element_type=f32)

def polar_kernel(block, m_ref, o_ref, x_ref, gram_ref, low_ref):
    size = m_ref.shape[0]
    keep = o_ref.shape[1]
    blocks = size // block

    def rows(i):
        return pl.ds(pl.multiple_of(i * block, block), block)

    def norm_step(i, total):
        part = wide(m_ref[rows(i), :])
        return total + jnp.sum(part * part, axis=0, keepdims=True)

    total = lax.fori_loop(0, blocks, norm_step, jnp.zeros((1, m_ref.shape[1]), f32))
    scale = lax.rsqrt(jnp.sum(total, axis=1, keepdims=True) + 1e-07)

    def scale_step(i, carry):
        x_ref[0, rows(i), :] = short(wide(m_ref[rows(i), :]) * scale)
        return carry

    lax.fori_loop(0, blocks, scale_step, 0)

    def sweep(now, last):
        x = x_ref.at[now]

        def gram_step(i, carry):
            gram = dot_nt(x[rows(i), :], x[...])
            gram_ref[rows(i), :] = gram
            low_ref[rows(i), :] = short(gram)
            return carry

        lax.fori_loop(0, blocks, gram_step, 0)

        def mix_step(i, carry):
            mixing = coef_two * gram_ref[rows(i), :] + coef_three * dot(low_ref[rows(i), :], low_ref[...])
            if last:
                o_ref[rows(i), :] = short(coef_one * wide(x[rows(i), :keep]) + dot(short(mixing), x[:, :keep]))
            else:
                x_ref[1 - now, rows(i), :] = short(coef_one * wide(x[rows(i), :]) + dot(short(mixing), x[...]))
            return carry

        lax.fori_loop(0, blocks, mix_step, 0)

    def two(k, carry):
        sweep(0, False)
        sweep(1, False)
        return carry

    lax.fori_loop(0, 2, two, 0)
    sweep(0, True)

def polar_columns(matrix, keep):
    size = matrix.shape[0]
    return pl.pallas_call(
        functools.partial(polar_kernel, 512),
        name="polar",
        out_shape=jax.ShapeDtypeStruct((size, keep), bf16),
        in_specs=[pl.BlockSpec(memory_space=pltpu.VMEM)],
        out_specs=pl.BlockSpec(memory_space=pltpu.VMEM),
        scratch_shapes=[
            pltpu.VMEM((2, size, matrix.shape[1]), bf16),
            pltpu.VMEM((size, size), f32),
            pltpu.VMEM((size, size), bf16),
        ],
        compiler_params=pltpu.CompilerParams(vmem_limit_bytes=32 * 2**20),
    )(matrix)


def factor_kernel(block, g_ref, o_ref, cur_ref, high_ref, low_ref, poly_ref, factor_ref):
    tile = g_ref.shape[1]
    tiles = cur_ref.shape[1] // tile
    size = cur_ref.shape[1]
    blocks = size // block
    keep = o_ref.shape[1]
    first = lax.axis_index("tensor") * keep
    k = 0
    trace = jnp.zeros((1, 1), f32)
    eye = (lax.broadcasted_iota(jnp.int32, (tile, tile), 0) == lax.broadcasted_iota(jnp.int32, (tile, tile), 1))
    for i in range(tiles):
        for j in range(i, tiles):
            part = g_ref[k]
            cur_ref[0, i*tile:(i+1)*tile, j*tile:(j+1)*tile] = part
            if i != j:
                cur_ref[0, j*tile:(j+1)*tile, i*tile:(i+1)*tile] = part.T
            else:
                diag = jnp.where(eye, part, 0.0)
                trace = trace + jnp.sum(jnp.sum(diag, axis=0, keepdims=True), axis=1, keepdims=True)
            k += 1
    scale = lax.rsqrt(trace + 1e-07)
    scale_two = scale * scale

    def rows(i):
        return pl.ds(pl.multiple_of(i * block, block), block)

    def scale_step(i, carry):
        cur_ref[0, rows(i), :] = cur_ref[0, rows(i), :] * scale_two
        return carry

    lax.fori_loop(0, blocks, scale_step, 0)

    def sweep(k, exact, finer):
        now = k % 2
        cur = cur_ref.at[now]

        def split_step(i, carry):
            value = cur[rows(i), :]
            high = short(value)
            high_ref[rows(i), :] = high
            if exact or finer:
                low_ref[rows(i), :] = short(value - wide(high))
            return carry

        lax.fori_loop(0, blocks, split_step, 0)

        def poly_step(i, carry):
            r = lax.broadcasted_iota(jnp.int32, (block, size), 0) + i * block
            c = lax.broadcasted_iota(jnp.int32, (block, size), 1)
            power = dot(high_ref[rows(i), :], high_ref[...])
            if finer:
                power = power + dot(high_ref[rows(i), :], low_ref[...])
            poly = coef_two * cur[rows(i), :] + coef_three * power
            poly = poly + jnp.where(r == c, coef_one, 0.0)
            poly_ref[rows(i), :] = short(poly)
            return carry

        lax.fori_loop(0, blocks, poly_step, 0)

        def next_step(i, carry):
            half = dot(poly_ref[rows(i), :], high_ref[...])
            if exact:
                half = half + dot(poly_ref[rows(i), :], low_ref[...])
            half_high = short(half)
            new = dot(half_high, poly_ref[...])
            if exact:
                new = new + dot(short(half - wide(half_high)), poly_ref[...])
            cur_ref[1 - now, rows(i), :] = new
            return carry

        if k < 4:
            lax.fori_loop(0, blocks, next_step, 0)

        def factor_step(i, carry):
            if k == 0:
                columns = pl.ds(pl.multiple_of(first, 128), keep)
                factor_ref[0, rows(i), :] = poly_ref[rows(i), columns]
            else:
                before = factor_ref[1 - now]
                new = dot(poly_ref[rows(i), :], before)
                if k < 4:
                    factor_ref[now, rows(i), :] = short(new)
                else:
                    o_ref[rows(i), :] = short(new * scale)
            return carry

        lax.fori_loop(0, blocks, factor_step, 0)

    for k in range(5):
        sweep(k, k < 2, k > 2)

def factor_columns(tiles, size, keep):
    return pl.pallas_call(
        functools.partial(factor_kernel, 512),
        name="factor",
        out_shape=jax.ShapeDtypeStruct((size, keep), bf16),
        in_specs=[pl.BlockSpec(memory_space=pltpu.VMEM)],
        out_specs=pl.BlockSpec(memory_space=pltpu.VMEM),
        scratch_shapes=[
            pltpu.VMEM((2, size, size), f32),
            pltpu.VMEM((size, size), bf16),
            pltpu.VMEM((size, size), bf16),
            pltpu.VMEM((size, size), bf16),
            pltpu.VMEM((2, size, keep), bf16),
        ],
        compiler_params=pltpu.CompilerParams(vmem_limit_bytes=40 * 2**20),
    )(tiles)


def body(
    layout,
    tokens,
    cotangent,
    lengths,
    packing,
    w_qkv,
    w_out,
    w_up,
    w_down,
    bias_qv,
    bias_up,
    vectors,
    mom_qkv,
    mom_out,
    mom_up,
    mom_down,
    mom_bias_qv,
    mom_bias_up,
    mom_vectors,
):
    inner, cores = layout
    groups = lax.axis_size("dp")
    teams = lax.axis_size("tensor")
    group = lax.axis_index("dp")
    team = lax.axis_index("tensor")
    outer, wides = groups // inner, teams // cores
    count = tokens.shape[0]
    per_peer = count // groups
    share = count // teams
    width = D // teams
    all_tokens = count * groups

    outer_ring = Ring("dp", (outer, inner), 0)
    inner_ring = Ring("dp", (outer, inner), 1)
    outer_at, inner_at = outer_ring.place(group), inner_ring.place(group)
    x_ring = Ring("tensor", (wides, cores), 0)
    core_ring = Ring("tensor", (wides, cores), 1)
    x_at, core_at = x_ring.place(team), core_ring.place(team)

    def team_of(rank):
        return ((x_at + rank % wides) % wides) * cores + (core_at + rank // wides) % cores

    def to_relative(value, size, axis=0):
        return jnp.concatenate([cut(value, team_of(r), size, axis) for r in range(teams)], axis)

    def to_given(value, size, axis=0):
        parts = []
        for other in range(teams):
            rank = ((other % cores - core_at) % cores) * wides + (other // cores - x_at) % wides
            parts.append(cut(value, rank, size, axis))
        return jnp.concatenate(parts, axis)

    def spread_list(piece, ring_x=x_ring, ring_core=core_ring):
        line = [piece]
        for _ in range(wides - 1):
            line.append(ring_x.send(line[-1], -1))
        pieces = list(line)
        for hop in range(1, cores):
            pieces += [ring_core.send(p, -hop) for p in line]
        return pieces

    def spread_rows(piece):
        return jnp.concatenate(spread_list(piece), 0)

    def spread_columns(piece):
        return to_given(jnp.concatenate(spread_list(piece), 1), piece.shape[1], 1)

    def reduce_rows(partial):
        block = wides * share
        held = partial[:block]
        for hop in range(1, cores):
            held = held + wide(core_ring.send(short(partial[hop * block : (hop + 1) * block]), hop))
        total = held[(wides - 1) * share :]
        for i in range(wides - 2, -1, -1):
            total = held[i * share : (i + 1) * share] + wide(x_ring.send(short(total), 1))
        return total

    def own_rows(value):
        return cut(value, team, share, 0)

    position = jnp.arange(count, dtype=jnp.int32)
    peer = jnp.arange(groups, dtype=jnp.int32)
    packed = packing.reshape(groups, count)
    source = packed // count
    source_mine = lax.dynamic_index_in_dim(source, group, 0, keepdims=False)
    masks = jnp.concatenate([source == group, source_mine[None, :] == peer[:, None]], 0)
    before = (position[:, None] < position[None, :]).astype(bf16)
    rank = mm(masks.astype(bf16), before).astype(jnp.int32)
    key = jnp.where(masks, rank, -1)
    value = jnp.concatenate(
        [packed % count, jnp.broadcast_to(position[None, :], (groups, count))], 0
    )
    slot_in_message = jnp.arange(per_peer, dtype=jnp.int32)
    picked = jnp.sum(
        jnp.where(key[:, None, :] == slot_in_message[None, :, None], value[:, None, :], 0), axis=-1
    )
    rows_sent = picked[:groups].reshape(count)
    slots = picked[groups:].reshape(count)
    choose = (rows_sent[:, None] == position[None, :]).astype(bf16)

    length_row = lengths[0]
    end_one = length_row[0]
    end_two = end_one + length_row[1]
    end_all = end_two + length_row[2]
    segments = (
        (slots >= end_one).astype(jnp.int32)
        + (slots >= end_two).astype(jnp.int32)
        + (slots >= end_all).astype(jnp.int32)
        + jnp.maximum(slots - end_all, 0)
    )
    valid_own = own_rows((slots < end_all).astype(f32))
    segments = to_relative(segments, share)

    def fetch(rows):
        sent = short(mm(choose, cut(rows, team, width, 1))).reshape(groups, per_peer, width)
        got = lax.all_to_all(sent, "dp", split_axis=0, concat_axis=0, tiled=True)
        return got.reshape(count, width)

    def give_back(rows):
        parts = len(rows)
        both = jnp.concatenate([r.reshape(share, teams, width) for r in rows], 2)
        columns = lax.all_to_all(
            both.reshape(share, teams * parts * width), "tensor", split_axis=1, concat_axis=0, tiled=True
        )
        got = lax.all_to_all(
            columns.reshape(groups, per_peer, parts * width), "dp", split_axis=0, concat_axis=0, tiled=True
        )
        pieces = spread_list(short(mm_tn(choose, got.reshape(count, parts * width))))
        return [
            to_given(jnp.concatenate([p[:, k * width : (k + 1) * width] for p in pieces], 1), width, 1)
            for k in range(parts)
        ]

    packed_x = to_relative(spread_columns(fetch(tokens)), share)
    grad_rows = lax.all_to_all(
        fetch(cotangent), "tensor", split_axis=0, concat_axis=1, tiled=True
    )

    wqkv_low = short(w_qkv)
    wout_low = short(w_out)
    wup_low = short(w_up)
    wdown_low = short(w_down)
    heads = width // HEAD
    score_scale = HEAD ** (-0.5)
    queries = short(mm(packed_x, wqkv_low[0]) + bias_qv[0]).reshape(count, heads, HEAD)
    keys = short(mm(packed_x, wqkv_low[1])).reshape(count, heads, HEAD)
    values = short(mm(packed_x, wqkv_low[2]) + bias_qv[1]).reshape(count, heads, HEAD)
    raw = jnp.einsum("qhd,khd->hqk", queries, keys, preferred_element_type=f32)
    same = segments[:, None] == segments[None, :]
    masked = jnp.where(same[None], raw * score_scale, masked_score)
    exponent = jnp.exp(masked - jnp.max(masked, axis=-1, keepdims=True))
    probs = exponent / jnp.sum(exponent, axis=-1, keepdims=True)
    probs_low = short(probs)
    context = short(
        jnp.einsum("hqk,khd->qhd", probs_low, values, preferred_element_type=f32)
    ).reshape(count, width)
    mid = wide(packed_x[:share]) + reduce_rows(mm(context, wout_low)) + vectors[0]
    normed_one, inverse_one, hidden = norm_forward(mid, vectors[1], vectors[2])
    hidden_low = spread_rows(short(hidden))
    pre_act = mm(hidden_low, wup_low) + bias_up
    phi = 0.5 * lax.erfc(-pre_act * math.sqrt(0.5))
    act_low = short(pre_act * phi)
    slope = phi + pre_act * jnp.exp(-0.5 * pre_act * pre_act) * (1.0 / math.sqrt(2.0 * math.pi))
    normed_two, inverse_two, result = norm_forward(
        hidden + reduce_rows(mm(act_low, wdown_low)) + vectors[3], vectors[4], vectors[5]
    )

    grad_result = wide(grad_rows) * valid_own[:, None]
    grad_z = norm_backward(grad_result, normed_two, inverse_two, vectors[4])
    grad_z_low = spread_rows(short(grad_z))
    grad_pre = short(mm_nt(grad_z_low, wdown_low) * slope)
    grad_hidden = grad_z + reduce_rows(mm_nt(grad_pre, wup_low))
    grad_down = short(mm_tn(act_low, grad_z_low))
    grad_up = short(mm_tn(hidden_low, grad_pre))
    grad_bias_up = jnp.sum(grad_pre, axis=0, dtype=f32)
    grad_mid = norm_backward(grad_hidden, normed_one, inverse_one, vectors[1])
    vector_part = jnp.stack(
        [
            jnp.sum(grad_mid, axis=0),
            jnp.sum(grad_hidden * normed_one, axis=0),
            jnp.sum(grad_hidden, axis=0),
            jnp.sum(grad_z, axis=0),
            jnp.sum(grad_result * normed_two, axis=0),
            jnp.sum(grad_result, axis=0),
        ]
    )
    extra = 16
    joined = jnp.concatenate(
        [short(grad_mid), short(vector_part), jnp.zeros((extra - 6, D), bf16)], 0
    )
    pieces = spread_list(joined)
    grad_mid_low = jnp.concatenate([p[:share] for p in pieces], 0)
    vector_part = sum(wide(p[share : share + 6]) for p in pieces)
    grad_out_t = short(mm_tn(grad_mid_low, context))
    grad_context = short(mm_nt(grad_mid_low, wout_low)).reshape(count, heads, HEAD)
    grad_probs = jnp.einsum("qhd,khd->hqk", grad_context, values, preferred_element_type=f32)
    weighted = jnp.sum(probs * grad_probs, axis=-1, keepdims=True)
    grad_scores = short(probs * (grad_probs - weighted))
    grad_values = short(
        jnp.einsum("hqk,qhd->khd", probs_low, grad_context, preferred_element_type=f32)
    ).reshape(count, width)
    grad_keys = short(
        jnp.einsum("hqk,qhd->khd", grad_scores, queries, preferred_element_type=f32) * score_scale
    ).reshape(count, width)
    grad_queries = short(
        jnp.einsum("hqk,khd->qhd", grad_scores, keys, preferred_element_type=f32) * score_scale
    ).reshape(count, width)
    grad_bias_pair = jnp.stack(
        [jnp.sum(grad_queries, axis=0, dtype=f32), jnp.sum(grad_values, axis=0, dtype=f32)]
    )
    grad_qkvo = jnp.concatenate(
        [
            short(mm_tn(packed_x, jnp.concatenate([grad_queries, grad_keys, grad_values], 1))),
            grad_out_t,
        ],
        1,
    )
    input_part = (
        mm_nt(grad_queries, wqkv_low[0])
        + mm_nt(grad_keys, wqkv_low[1])
        + mm_nt(grad_values, wqkv_low[2])
    )
    columns = D
    small = jnp.concatenate(
        [vector_part.reshape(-1), grad_bias_pair.reshape(-1), grad_bias_up.reshape(-1)]
    )
    parts = [
        grad_down.reshape(-1, columns),
        grad_up.reshape(-1, columns),
        grad_qkvo.reshape(-1, columns),
    ]
    rows_small = -(-small.size // (16 * columns)) * 16
    small = jnp.pad(short(small), (0, rows_small * columns - small.size)).reshape(rows_small, columns)
    total, small_sum = ring_sum(jnp.concatenate(parts, 0), small, inner, groups)
    sums, start = [], 0
    for part in parts:
        sums.append(total[start : start + part.shape[0]])
        start += part.shape[0]
    down_sum = sums[0].reshape(grad_down.shape)
    up_sum = sums[1].reshape(grad_up.shape)
    qkvo_sum = wide(sums[2].reshape(grad_qkvo.shape))
    small_sum = small_sum.reshape(-1)
    gradients = (
        jnp.stack([qkvo_sum[:, k * width : (k + 1) * width] for k in range(3)]),
        qkvo_sum[:, 3 * width :].T,
        wide(up_sum),
        wide(down_sum),
        small_sum[6 * D : 6 * D + 2 * width].reshape(2, width),
        small_sum[6 * D + 2 * width : 6 * D + 2 * width + bias_up.shape[0]],
        small_sum[: 6 * D].reshape(6, D),
    )
    moments_old = (mom_qkv, mom_out, mom_up, mom_down, mom_bias_qv, mom_bias_up, mom_vectors)
    moments = tuple(
        momentum_decay * old + grad for old, grad in zip(moments_old, gradients)
    )

    everyone = ("dp", "tensor")
    radices = (groups, wides, cores)

    def ring_within(digit, low, high):
        return Ring(everyone, radices, digit, lambda i: low <= i // teams < high)

    square_mine = lax.switch(
        jnp.minimum(group, 3),
        [
            lambda: short(moments[0][0]),
            lambda: short(moments[0][1]),
            lambda: short(moments[0][2]),
            lambda: short(moments[1]).T,
        ],
    )
    square = jnp.concatenate(
        spread_list(square_mine, ring_within(1, 0, 4), ring_within(2, 0, 4)), 1
    )

    up_low, down_low = short(moments[2]), short(moments[3])
    tile = D // 4
    pairs = [(i, j) for i in range(4) for j in range(i, 4)]

    def pack(gram):
        return jnp.concatenate(
            [gram[i * tile : (i + 1) * tile, j * tile : (j + 1) * tile] for i, j in pairs], 0
        )

    packed_gram = lax.switch(
        jnp.clip(group - 3, 0, 3),
        [
            lambda: jnp.zeros((len(pairs) * tile, tile), f32),
            lambda: pack(mm_nt(up_low, up_low)),
            lambda: pack(mm_tn(down_low, down_low)),
            lambda: jnp.zeros((len(pairs) * tile, tile), f32),
        ],
    )
    gram_x, gram_core = ring_within(1, 4, 6), ring_within(2, 4, 6)
    part_rows = len(pairs) * tile // cores
    held = cut(packed_gram, core_at, part_rows, 0)
    for hop in range(1, cores):
        held = held + gram_core.send(cut(packed_gram, (core_at + hop) % cores, part_rows, 0), hop)
    passing, total = held, held
    for _ in range(wides - 1):
        passing = gram_x.send(passing, 1)
        total = total + passing
    packed_gram = ring_gather(total, 0, gram_core, core_at)

    def no_work(square, blocks):
        return jnp.zeros((D, width), bf16)

    def square_work(square, blocks):
        return polar_columns(square, width)

    def gram_work(square, blocks):
        return factor_columns(blocks.reshape(len(pairs), tile, tile), D, width)

    stepped = lax.switch(
        (group >= 4).astype(jnp.int32) + (group >= 6).astype(jnp.int32),
        [square_work, gram_work, no_work],
        square,
        packed_gram,
    )
    dp_rows = D // groups
    steps = lax.all_to_all(
        stepped.reshape(groups, dp_rows, width), "dp", split_axis=0, concat_axis=0, tiled=True
    )
    factors = spread_columns(steps[4:6].reshape(2 * dp_rows, width))

    def mine(values_, dim):
        return lax.dynamic_slice_in_dim(values_, group * dp_rows, dp_rows, dim)

    short_rate = rate_matrix * 0.2 * math.sqrt(D)
    long_rate = rate_matrix * 0.2 * math.sqrt(w_up.shape[1] * teams)
    masters = [
        mine(w_qkv, 1) - short_rate * wide(steps[:3]),
        mine(w_out, 1) - short_rate * wide(steps[3]).T,
        mine(w_up, 0) - long_rate * mm(factors[:dp_rows], up_low),
        mine(w_down, 1) - long_rate * mm_nt(down_low, factors[dp_rows:]),
    ]
    rate_vector = 0.2 / math.sqrt(all_tokens)
    for param, moment in zip((bias_qv, bias_up, vectors), moments[4:]):
        masters.append(param - rate_vector * moment)

    output, grad_tokens = give_back(
        [short(result), short(grad_mid + reduce_rows(input_part))]
    )
    grad_tokens = wide(grad_tokens)
    return (output, grad_tokens, *gradients, *moments, *masters)


def axis_layout(mesh):
    grid = mesh.devices
    groups, teams = grid.shape
    places = [getattr(d, "coords", None) for d in grid[:, 0]]
    inner = 2 if groups % 2 == 0 else 1
    if places[0] is not None:
        moved = [k for k in range(3) if places[0][k] != places[1][k]]
        fixed = [k for k in range(3) if k not in moved]
        inner = 1
        while inner < groups and all(places[inner][k] == places[0][k] for k in fixed):
            inner += 1
        if groups % inner:
            inner = 1
    return inner, (2 if teams % 2 == 0 else 1)


def solution(mesh):
    grads = (
        P(None, None, "tensor"),
        P("tensor", None),
        P(None, "tensor"),
        P("tensor", None),
        P(None, "tensor"),
        P("tensor"),
        P(),
    )
    rows = P("dp", None)
    return jax.shard_map(
        functools.partial(body, axis_layout(mesh)),
        mesh=mesh,
        in_specs=(rows, rows, rows, P(), *grads, *grads),
        out_specs=(
            rows,
            rows,
            *grads,
            *grads,
            P(None, "dp", "tensor"),
            P("tensor", "dp"),
            P("dp", "tensor"),
            P("tensor", "dp"),
            P(None, "tensor"),
            P("tensor"),
            P(),
        ),
        check_vma=False,
    )
```

```python
import functools
import math

import jax
import jax.numpy as jnp
from jax import lax
from jax.experimental import pallas as pl
from jax.experimental.pallas import tpu as pltpu
from jax.sharding import PartitionSpec as P

D = 1024
HEAD = 64

eps_norm = 1e-05
coef_one = 3.4445
coef_two = -4.775
coef_three = 2.0315
momentum_decay = 0.9
rate_matrix = 0.1
masked_score = -1000000000.0
bf16 = jnp.bfloat16
f32 = jnp.float32


def short(value):
    return value.astype(bf16)


def wide(value):
    return value.astype(f32)


def mm(left, right):
    return jnp.dot(short(left), short(right), preferred_element_type=f32)


def mm_nt(left, right):
    return lax.dot_general(
        short(left), short(right), (((1,), (1,)), ((), ())), preferred_element_type=f32
    )


def mm_tn(left, right):
    return lax.dot_general(
        short(left), short(right), (((0,), (0,)), ((), ())), preferred_element_type=f32
    )


def norm_forward(values, gain_row, shift_row):
    average = jnp.mean(values, axis=-1, keepdims=True)
    centred = values - average
    variance = jnp.mean(centred * centred, axis=-1, keepdims=True)
    inverse = lax.rsqrt(variance + eps_norm)
    normed = centred * inverse
    return (normed, inverse, normed * gain_row + shift_row)


def norm_backward(upstream, normed, inverse, gain_row):
    scaled = upstream * gain_row
    centre_term = jnp.mean(scaled, axis=-1, keepdims=True)
    slope_term = jnp.mean(scaled * normed, axis=-1, keepdims=True)
    return inverse * (scaled - centre_term - normed * slope_term)


class Ring:
    def __init__(self, axes, sizes, digit, members=None):
        self.axes = axes
        self.count = sizes[digit]
        self.below = math.prod(sizes[digit + 1 :])
        self.total = math.prod(sizes)
        self.members = members

    def send(self, value, offset):
        count, below = self.count, self.below
        pairs = []
        for i in range(self.total):
            if self.members is not None and not self.members(i):
                continue
            at = (i // below) % count
            pairs.append((i, i + ((at + offset) % count - at) * below))
        return lax.ppermute(value, self.axes, pairs)

    def place(self, linear):
        return (linear // self.below) % self.count


def cut(value, index, size, axis):
    return lax.dynamic_slice_in_dim(value, index * size, size, axis)


def tile_pairs(tiles):
    return [(i, j) for i in range(tiles) for j in range(i, tiles)]


def pick(options, index):
    chosen = jnp.int32(options[0])
    for k in range(1, len(options)):
        chosen = jnp.where(index == k, jnp.int32(options[k]), chosen)
    return chosen


def sum_kernel(
    inner,
    tile,
    down_ref,
    up_ref,
    qkvo_ref,
    small_ref,
    mom_qkv_ref,
    mom_out_ref,
    mom_up_ref,
    mom_down_ref,
    down_sum_ref,
    up_sum_ref,
    qkvo_sum_ref,
    small_sum_ref,
    square_ref,
    tiles_ref,
    got_down,
    got_up,
    got_low,
    got_high,
    small_got,
    mom_up,
    mom_down,
    mom_column,
    mom_row,
    up_low,
    down_low,
    part,
    core_got,
    chip_sum,
    x_got,
    ring_sems,
    late_sems,
    small_sems,
    load_sem,
    core_sems,
    x_sems,
    back_sems,
    square_x_sems,
    square_core_sems,
):
    mesh_type = pl.DeviceIdType.MESH
    count = lax.axis_size("dp")
    index = lax.axis_index("dp")
    team = lax.axis_index("tensor")
    wides = lax.axis_size("tensor") // 2
    x_at, core = team // 2, team % 2
    outer = count // inner
    if inner == 2:
        place = jnp.where(index % 2 == 0, index // 2, count - 1 - index // 2)

        def device(p):
            return jnp.where(p < outer, 2 * p, 2 * (count - 1 - p) + 1)
    else:
        place = index

        def device(p):
            return p

    ring_next = ((device((place + 1) % count), team), (device((place + count - 1) % count), team))
    core_next = (index, x_at * 2 + 1 - core)
    x_up = (index, ((x_at + 1) % wides) * 2 + core)
    x_down = (index, ((x_at + wides - 1) % wides) * 2 + core)

    barrier = pltpu.get_barrier_semaphore()

    def greet(hop, carry):
        pl.semaphore_signal(
            barrier, inc=1, device_id=((index + hop) % count, team), device_id_type=mesh_type
        )
        return carry

    lax.fori_loop(1, count, greet, 0)
    others = [core_next, x_up] + ([x_down] if wides > 2 else [])
    for other in others:
        pl.semaphore_signal(barrier, inc=1, device_id=other, device_id_type=mesh_type)
    pl.semaphore_wait(barrier, count - 1 + len(others))

    def remote(src, dst, sems, at, target):
        return pltpu.make_async_remote_copy(
            src_ref=src,
            dst_ref=dst,
            send_sem=sems.at[(0, *at)],
            recv_sem=sems.at[(1, *at)],
            device_id=target,
            device_id_type=mesh_type,
        )

    sent = []

    def ring(lanes, sems):
        streams = []
        for d, (x_ref, o_ref, first, length, got) in enumerate(lanes):
            chunk = length // count
            halves = 2 if chunk % 32 == 0 else 1
            sub = chunk // halves
            for h in range(halves):
                streams.append((d, h, x_ref, o_ref, first, chunk, sub, got))
        streams.sort(key=lambda one: one[1])

        def rows(stream, hop):
            d, h, _, _, first, chunk, sub, _ = stream
            at = (place + count - hop) % count if d == 0 else (place + hop) % count
            return pl.ds(pl.multiple_of(first + at * chunk + h * sub, 16), sub)

        def copy(stream, step):
            d, h, x_ref, o_ref, _, _, sub, got = stream
            if step < count - 1:
                slot = pl.ds(h * sub, sub)
                src = x_ref.at[rows(stream, 1)] if step == 0 else got.at[step - 1, slot]
                dst = got.at[step, slot]
            else:
                src = dst = o_ref.at[rows(stream, step - (count - 1))]
            return remote(src, dst, sems, (step, d, h), ring_next[d])

        for stream in streams:
            copy(stream, 0).start()
        yield 0
        for step in range(2 * (count - 1)):
            for stream in streams:
                _, h, x_ref, o_ref, _, _, sub, got = stream
                one = copy(stream, step)
                one.wait_recv()
                sent.append(one)
                if step < count - 1:
                    slot = pl.ds(h * sub, sub)
                    total = wide(got[step, slot]) + wide(x_ref[rows(stream, step + 2)])
                    if step < count - 2:
                        got[step, slot] = short(total)
                    else:
                        o_ref[rows(stream, 0)] = short(total)
                if step < 2 * count - 3:
                    copy(stream, step + 1).start()
                yield step

    half = qkvo_ref.shape[0] // 2
    first_ring = ring(
        [
            (down_ref, down_sum_ref, 0, down_ref.shape[0], got_down),
            (up_ref, up_sum_ref, 0, up_ref.shape[0], got_up),
        ],
        ring_sems,
    )
    second_ring = ring(
        [(qkvo_ref, qkvo_sum_ref, 0, half, got_low), (qkvo_ref, qkvo_sum_ref, half, half, got_high)],
        late_sems,
    )

    is_up, is_down = index == 4, index == 5
    is_gram = jnp.logical_or(is_up, is_down)
    size = up_ref.shape[0]
    pairs = tile_pairs(size // tile)
    share = len(pairs) // 2
    load_up = pltpu.make_async_copy(mom_up_ref, mom_up, load_sem.at[0])
    load_down = pltpu.make_async_copy(mom_down_ref, mom_down, load_sem.at[0])

    def gram_tasks():
        for ref, mom, total, low, load, mine in (
            (mom_up_ref, mom_up, up_sum_ref, up_low, load_up, is_up),
            (mom_down_ref, mom_down, down_sum_ref, down_low, load_down, is_down),
        ):

            @pl.when(mine)
            def _():
                load.wait()

            for start in range(0, ref.shape[0], 256):

                @pl.when(mine)
                def _():
                    rows = pl.ds(start, 256)
                    low[rows, :] = short(momentum_decay * mom[rows, :] + wide(total[rows, :]))

            yield

        def compute(k):
            row = pl.ds(pl.multiple_of(pick([p[0] for p in pairs], k) * tile, tile), tile)
            column = pl.ds(pl.multiple_of(pick([p[1] for p in pairs], k) * tile, tile), tile)

            @pl.when(is_up)
            def _():
                part[k] = mm_nt(up_low[row, :], up_low[column, :])

            @pl.when(is_down)
            def _():
                part[k] = mm_tn(down_low[:, row], down_low[:, column])

        def to_core(i):
            return remote(part.at[(1 - core) * share + i], core_got.at[i], core_sems, (i,), core_next)

        def to_x(i, hop):
            src = chip_sum.at[i] if hop == 0 else x_got.at[hop - 1, i]
            return remote(src, x_got.at[hop, i], x_sems, (hop, i), x_up)

        def to_back(i):
            at = tiles_ref.at[core * share + i]
            return remote(at, at, back_sems, (i,), core_next)

        for i in range(share):
            compute((1 - core) * share + i)

            @pl.when(is_gram)
            def _():
                to_core(i).start()

            yield
        for i in range(share):
            compute(core * share + i)
            yield
        for i in range(share):

            @pl.when(is_gram)
            def _():
                to_core(i).wait_recv()
                chip_sum[i] = part[core * share + i] + core_got[i]
                to_x(i, 0).start()

            yield
        yield "late"
        for hop in range(wides - 1):
            for i in range(share):

                @pl.when(is_gram)
                def _():
                    to_x(i, hop).wait_recv()
                    before = chip_sum[i] if hop == 0 else tiles_ref[core * share + i]
                    tiles_ref[core * share + i] = before + x_got[hop, i]
                    if hop < wides - 2:
                        to_x(i, hop + 1).start()
                    else:
                        to_back(i).start()

        @pl.when(is_gram)
        def _():
            for i in range(share):
                to_back(i).wait_recv()
                to_core(i).wait_send()
                to_back(i).wait_send()
                for hop in range(wides - 1):
                    to_x(i, hop).wait_send()

    def small_copy(hop):
        return remote(
            small_ref, small_got.at[hop], small_sems, (hop,), ((index + hop) % count, team)
        )

    def small_send(hop, carry):
        small_copy(hop).start()
        return carry

    def small_wait(hop, total):
        one = small_copy(hop)
        one.wait_send()
        one.wait_recv()
        return total + wide(small_got[hop])

    is_column, is_row = index < 3, index == 3
    is_square = index < 4
    width = square_ref.shape[2]
    load_column = pltpu.make_async_copy(
        mom_qkv_ref.at[jnp.minimum(index, 2)], mom_column, load_sem.at[0]
    )
    load_row = pltpu.make_async_copy(mom_out_ref, mom_row, load_sem.at[0])
    square_rows = square_ref.shape[1]
    block = 256
    blocks = square_rows // block

    def square_x(hop, b):
        rows = pl.ds(b * block, block)
        return remote(
            square_ref.at[hop, rows], square_ref.at[hop + 1, rows], square_x_sems, (hop, b), x_down
        )

    def square_core(hop, b):
        rows = pl.ds(b * block, block)
        return remote(
            square_ref.at[hop, rows], square_ref.at[wides + hop, rows], square_core_sems, (hop, b), core_next
        )

    def square_work():
        columns = pl.ds(pl.multiple_of(jnp.minimum(index, 3) * width, 128), width)
        for b in range(blocks):
            rows = pl.ds(b * block, block)
            fresh = wide(qkvo_sum_ref[rows, columns])

            @pl.when(is_column)
            def _():
                if b == 0:
                    load_column.wait()
                square_ref[0, rows] = short(momentum_decay * mom_column[rows, :] + fresh)

            @pl.when(is_row)
            def _():
                if b == 0:
                    load_row.wait()
                square_ref[0, rows] = short(momentum_decay * mom_row[:, rows].T + fresh)

            square_x(0, b).start()
            square_core(0, b).start()
        for hop in range(1, wides):
            for b in range(blocks):
                square_x(hop - 1, b).wait_recv()
                if hop < wides - 1:
                    square_x(hop, b).start()
                square_core(hop, b).start()
        for hop in range(wides):
            for b in range(blocks):
                square_core(hop, b).wait_recv()
        for hop in range(wides):
            for b in range(blocks):
                square_core(hop, b).wait_send()
                if hop < wides - 1:
                    square_x(hop, b).wait_send()

    next(first_ring)
    lax.fori_loop(1, count, small_send, 0)
    for one, mine in (
        (load_up, is_up),
        (load_down, is_down),
        (load_column, is_column),
        (load_row, is_row),
    ):

        @pl.when(mine)
        def _():
            one.start()

    begun = False
    for step in first_ring:
        if step == 2 * count - 4 and not begun:
            next(second_ring)
            begun = True
    side = gram_tasks()
    late = False
    for _ in second_ring:
        if not late:
            late = next(side) == "late"
    while not late:
        late = next(side) == "late"
    pl.when(is_square)(square_work)
    for _ in side:
        pass
    small_sum_ref[...] = lax.fori_loop(1, count, small_wait, wide(small_ref[...]))
    for one in sent:
        one.wait_send()


def sums_over_dp(inner, down, up, qkvo, small, moments_old):
    groups, teams = lax.axis_size("dp"), lax.axis_size("tensor")
    wides = teams // 2
    size, width = qkvo.shape[0], qkvo.shape[1] // 4
    tile = size // 4
    pairs = len(tile_pairs(4))
    steps = 2 * (groups - 1)
    mom_qkv, mom_out, mom_up, mom_down = moments_old
    dma = pltpu.SemaphoreType.DMA
    vmem = pl.BlockSpec(memory_space=pltpu.VMEM)
    length = down.size + up.size + qkvo.size
    return pl.pallas_call(
        functools.partial(sum_kernel, inner, tile),
        name="sums_over_dp",
        out_shape=(
            jax.ShapeDtypeStruct(down.shape, bf16),
            jax.ShapeDtypeStruct(up.shape, bf16),
            jax.ShapeDtypeStruct(qkvo.shape, bf16),
            jax.ShapeDtypeStruct(small.shape, f32),
            jax.ShapeDtypeStruct((teams, size, width), bf16),
            jax.ShapeDtypeStruct((pairs, tile, tile), f32),
        ),
        in_specs=[vmem] * 4 + [pl.BlockSpec(memory_space=pl.ANY)] * 4,
        out_specs=[vmem] * 6,
        scratch_shapes=[
            pltpu.VMEM((groups - 1, down.shape[0] // groups, down.shape[1]), bf16),
            pltpu.VMEM((groups - 1, up.shape[0] // groups, up.shape[1]), bf16),
            pltpu.VMEM((groups - 1, size // 2 // groups, qkvo.shape[1]), bf16),
            pltpu.VMEM((groups - 1, size // 2 // groups, qkvo.shape[1]), bf16),
            pltpu.VMEM((groups, *small.shape), bf16),
            pltpu.VMEM(up.shape, f32),
            pltpu.VMEM(down.shape, f32),
            pltpu.VMEM((size, width), f32),
            pltpu.VMEM((width, size), f32),
            pltpu.VMEM(up.shape, bf16),
            pltpu.VMEM(down.shape, bf16),
            pltpu.VMEM((pairs, tile, tile), f32),
            pltpu.VMEM((pairs // 2, tile, tile), f32),
            pltpu.VMEM((pairs // 2, tile, tile), f32),
            pltpu.VMEM((wides - 1, pairs // 2, tile, tile), f32),
            dma((2, steps, 2, 2)),
            dma((2, steps, 2, 2)),
            dma((2, groups)),
            dma((1,)),
            dma((2, pairs // 2)),
            dma((2, wides - 1, pairs // 2)),
            dma((2, pairs // 2)),
            dma((2, wides - 1, size // 256)),
            dma((2, wides, size // 256)),
        ],
        compiler_params=pltpu.CompilerParams(
            collective_id=0, has_side_effects=True, vmem_limit_bytes=52 * 2**20
        ),
        cost_estimate=pl.CostEstimate(
            flops=length, bytes_accessed=4 * length, transcendentals=0
        ),
    )(down, up, qkvo, small, mom_qkv, mom_out, mom_up, mom_down)


def dot(left, right):
    return jnp.dot(left, right, preferred_element_type=f32)

def dot_nt(left, right):
    return lax.dot_general(left, right, (((1,), (1,)), ((), ())), preferred_element_type=f32)

def polar_kernel(block, m_ref, o_ref, x_ref, gram_ref, low_ref):
    teams, size, width = m_ref.shape
    keep = o_ref.shape[1]
    blocks = size // block

    def rows(i):
        return pl.ds(pl.multiple_of(i * block, block), block)

    def norm_step(i, total):
        for r in range(teams):
            part = wide(m_ref[r, rows(i), :])
            total = total + jnp.sum(part * part, axis=0, keepdims=True)
        return total

    total = lax.fori_loop(0, blocks, norm_step, jnp.zeros((1, width), f32))
    scale = lax.rsqrt(jnp.sum(total, axis=1, keepdims=True) + 1e-07)

    def scale_step(i, carry):
        for r in range(teams):
            x_ref[0, rows(i), r * width : (r + 1) * width] = short(wide(m_ref[r, rows(i), :]) * scale)
        return carry

    lax.fori_loop(0, blocks, scale_step, 0)

    def sweep(now, last):
        x = x_ref.at[now]

        def gram_step(i, carry):
            gram = dot_nt(x[rows(i), :], x[...])
            gram_ref[rows(i), :] = gram
            low_ref[rows(i), :] = short(gram)
            return carry

        lax.fori_loop(0, blocks, gram_step, 0)

        def mix_step(i, carry):
            mixing = coef_two * gram_ref[rows(i), :] + coef_three * dot(low_ref[rows(i), :], low_ref[...])
            if last:
                o_ref[rows(i), :] = short(coef_one * wide(x[rows(i), :keep]) + dot(short(mixing), x[:, :keep]))
            else:
                x_ref[1 - now, rows(i), :] = short(coef_one * wide(x[rows(i), :]) + dot(short(mixing), x[...]))
            return carry

        lax.fori_loop(0, blocks, mix_step, 0)

    def two(k, carry):
        sweep(0, False)
        sweep(1, False)
        return carry

    lax.fori_loop(0, 2, two, 0)
    sweep(0, True)

def polar_columns(matrix):
    teams, size, width = matrix.shape
    return pl.pallas_call(
        functools.partial(polar_kernel, 512),
        name="polar",
        out_shape=jax.ShapeDtypeStruct((size, width), bf16),
        in_specs=[pl.BlockSpec(memory_space=pltpu.VMEM)],
        out_specs=pl.BlockSpec(memory_space=pltpu.VMEM),
        scratch_shapes=[
            pltpu.VMEM((2, size, teams * width), bf16),
            pltpu.VMEM((size, size), f32),
            pltpu.VMEM((size, size), bf16),
        ],
        compiler_params=pltpu.CompilerParams(vmem_limit_bytes=32 * 2**20),
    )(matrix)


def factor_kernel(block, g_ref, o_ref, cur_ref, high_ref, low_ref, poly_ref, factor_ref):
    tile = g_ref.shape[1]
    tiles = cur_ref.shape[1] // tile
    size = cur_ref.shape[1]
    blocks = size // block
    keep = o_ref.shape[1]
    first = lax.axis_index("tensor") * keep
    k = 0
    trace = jnp.zeros((1, 1), f32)
    eye = (lax.broadcasted_iota(jnp.int32, (tile, tile), 0) == lax.broadcasted_iota(jnp.int32, (tile, tile), 1))
    for i in range(tiles):
        for j in range(i, tiles):
            part = g_ref[k]
            cur_ref[0, i*tile:(i+1)*tile, j*tile:(j+1)*tile] = part
            if i != j:
                cur_ref[0, j*tile:(j+1)*tile, i*tile:(i+1)*tile] = part.T
            else:
                diag = jnp.where(eye, part, 0.0)
                trace = trace + jnp.sum(jnp.sum(diag, axis=0, keepdims=True), axis=1, keepdims=True)
            k += 1
    scale = lax.rsqrt(trace + 1e-07)
    scale_two = scale * scale

    def rows(i):
        return pl.ds(pl.multiple_of(i * block, block), block)

    def scale_step(i, carry):
        cur_ref[0, rows(i), :] = cur_ref[0, rows(i), :] * scale_two
        return carry

    lax.fori_loop(0, blocks, scale_step, 0)

    def sweep(k, exact, finer):
        now = k % 2
        cur = cur_ref.at[now]

        def split_step(i, carry):
            value = cur[rows(i), :]
            high = short(value)
            high_ref[rows(i), :] = high
            if exact or finer:
                low_ref[rows(i), :] = short(value - wide(high))
            return carry

        lax.fori_loop(0, blocks, split_step, 0)

        def poly_step(i, carry):
            r = lax.broadcasted_iota(jnp.int32, (block, size), 0) + i * block
            c = lax.broadcasted_iota(jnp.int32, (block, size), 1)
            power = dot(high_ref[rows(i), :], high_ref[...])
            if finer:
                power = power + dot(high_ref[rows(i), :], low_ref[...])
            poly = coef_two * cur[rows(i), :] + coef_three * power
            poly = poly + jnp.where(r == c, coef_one, 0.0)
            poly_ref[rows(i), :] = short(poly)
            return carry

        lax.fori_loop(0, blocks, poly_step, 0)

        def next_step(i, carry):
            half = dot(poly_ref[rows(i), :], high_ref[...])
            if exact:
                half = half + dot(poly_ref[rows(i), :], low_ref[...])
            half_high = short(half)
            new = dot(half_high, poly_ref[...])
            if exact:
                new = new + dot(short(half - wide(half_high)), poly_ref[...])
            cur_ref[1 - now, rows(i), :] = new
            return carry

        if k < 4:
            lax.fori_loop(0, blocks, next_step, 0)

        def factor_step(i, carry):
            if k == 0:
                columns = pl.ds(pl.multiple_of(first, 128), keep)
                factor_ref[0, rows(i), :] = poly_ref[rows(i), columns]
            else:
                before = factor_ref[1 - now]
                new = dot(poly_ref[rows(i), :], before)
                if k < 4:
                    factor_ref[now, rows(i), :] = short(new)
                else:
                    o_ref[rows(i), :] = short(new * scale)
            return carry

        lax.fori_loop(0, blocks, factor_step, 0)

    for k in range(5):
        sweep(k, k < 2, k > 2)

def factor_columns(tiles, size, keep):
    return pl.pallas_call(
        functools.partial(factor_kernel, 512),
        name="factor",
        out_shape=jax.ShapeDtypeStruct((size, keep), bf16),
        in_specs=[pl.BlockSpec(memory_space=pltpu.VMEM)],
        out_specs=pl.BlockSpec(memory_space=pltpu.VMEM),
        scratch_shapes=[
            pltpu.VMEM((2, size, size), f32),
            pltpu.VMEM((size, size), bf16),
            pltpu.VMEM((size, size), bf16),
            pltpu.VMEM((size, size), bf16),
            pltpu.VMEM((2, size, keep), bf16),
        ],
        compiler_params=pltpu.CompilerParams(vmem_limit_bytes=40 * 2**20),
    )(tiles)


def body(
    layout,
    tokens,
    cotangent,
    lengths,
    packing,
    w_qkv,
    w_out,
    w_up,
    w_down,
    bias_qv,
    bias_up,
    vectors,
    mom_qkv,
    mom_out,
    mom_up,
    mom_down,
    mom_bias_qv,
    mom_bias_up,
    mom_vectors,
):
    inner, cores = layout
    groups = lax.axis_size("dp")
    teams = lax.axis_size("tensor")
    group = lax.axis_index("dp")
    team = lax.axis_index("tensor")
    outer, wides = groups // inner, teams // cores
    count = tokens.shape[0]
    per_peer = count // groups
    share = count // teams
    width = D // teams
    all_tokens = count * groups

    outer_ring = Ring("dp", (outer, inner), 0)
    inner_ring = Ring("dp", (outer, inner), 1)
    outer_at, inner_at = outer_ring.place(group), inner_ring.place(group)
    x_ring = Ring("tensor", (wides, cores), 0)
    core_ring = Ring("tensor", (wides, cores), 1)
    x_at, core_at = x_ring.place(team), core_ring.place(team)

    def team_of(rank):
        return ((x_at + rank % wides) % wides) * cores + (core_at + rank // wides) % cores

    def to_relative(value, size, axis=0):
        return jnp.concatenate([cut(value, team_of(r), size, axis) for r in range(teams)], axis)

    def to_given(value, size, axis=0):
        parts = []
        for other in range(teams):
            rank = ((other % cores - core_at) % cores) * wides + (other // cores - x_at) % wides
            parts.append(cut(value, rank, size, axis))
        return jnp.concatenate(parts, axis)

    def spread_list(piece, ring_x=x_ring, ring_core=core_ring):
        line = [piece]
        for _ in range(wides - 1):
            line.append(ring_x.send(line[-1], -1))
        pieces = list(line)
        for hop in range(1, cores):
            pieces += [ring_core.send(p, -hop) for p in line]
        return pieces

    def spread_rows(piece):
        return jnp.concatenate(spread_list(piece), 0)

    def spread_columns(piece):
        return to_given(jnp.concatenate(spread_list(piece), 1), piece.shape[1], 1)

    def reduce_rows(partial):
        block = wides * share
        held = partial[:block]
        for hop in range(1, cores):
            held = held + wide(core_ring.send(short(partial[hop * block : (hop + 1) * block]), hop))
        total = held[(wides - 1) * share :]
        for i in range(wides - 2, -1, -1):
            total = held[i * share : (i + 1) * share] + wide(x_ring.send(short(total), 1))
        return total

    def own_rows(value):
        return cut(value, team, share, 0)

    position = jnp.arange(count, dtype=jnp.int32)
    peer = jnp.arange(groups, dtype=jnp.int32)
    packed = packing.reshape(groups, count)
    source = packed // count
    source_mine = lax.dynamic_index_in_dim(source, group, 0, keepdims=False)
    masks = jnp.concatenate([source == group, source_mine[None, :] == peer[:, None]], 0)
    before = (position[:, None] < position[None, :]).astype(bf16)
    rank = mm(masks.astype(bf16), before).astype(jnp.int32)
    key = jnp.where(masks, rank, -1)
    value = jnp.concatenate(
        [packed % count, jnp.broadcast_to(position[None, :], (groups, count))], 0
    )
    slot_in_message = jnp.arange(per_peer, dtype=jnp.int32)
    picked = jnp.sum(
        jnp.where(key[:, None, :] == slot_in_message[None, :, None], value[:, None, :], 0), axis=-1
    )
    rows_sent = picked[:groups].reshape(count)
    slots = picked[groups:].reshape(count)
    choose = (rows_sent[:, None] == position[None, :]).astype(bf16)

    length_row = lengths[0]
    end_one = length_row[0]
    end_two = end_one + length_row[1]
    end_all = end_two + length_row[2]
    segments = (
        (slots >= end_one).astype(jnp.int32)
        + (slots >= end_two).astype(jnp.int32)
        + (slots >= end_all).astype(jnp.int32)
        + jnp.maximum(slots - end_all, 0)
    )
    valid_own = own_rows((slots < end_all).astype(f32))
    segments = to_relative(segments, share)

    def fetch(rows):
        sent = short(mm(choose, cut(rows, team, width, 1))).reshape(groups, per_peer, width)
        got = lax.all_to_all(sent, "dp", split_axis=0, concat_axis=0, tiled=True)
        return got.reshape(count, width)

    def give_back(rows):
        parts = len(rows)
        both = jnp.concatenate([r.reshape(share, teams, width) for r in rows], 2)
        columns = lax.all_to_all(
            both.reshape(share, teams * parts * width), "tensor", split_axis=1, concat_axis=0, tiled=True
        )
        got = lax.all_to_all(
            columns.reshape(groups, per_peer, parts * width), "dp", split_axis=0, concat_axis=0, tiled=True
        )
        pieces = spread_list(short(mm_tn(choose, got.reshape(count, parts * width))))
        return [
            to_given(jnp.concatenate([p[:, k * width : (k + 1) * width] for p in pieces], 1), width, 1)
            for k in range(parts)
        ]

    packed_x = to_relative(spread_columns(fetch(tokens)), share)
    grad_rows = lax.all_to_all(
        fetch(cotangent), "tensor", split_axis=0, concat_axis=1, tiled=True
    )

    wqkv_low = short(w_qkv)
    wout_low = short(w_out)
    wup_low = short(w_up)
    wdown_low = short(w_down)
    heads = width // HEAD
    score_scale = HEAD ** (-0.5)
    queries = short(mm(packed_x, wqkv_low[0]) + bias_qv[0]).reshape(count, heads, HEAD)
    keys = short(mm(packed_x, wqkv_low[1])).reshape(count, heads, HEAD)
    values = short(mm(packed_x, wqkv_low[2]) + bias_qv[1]).reshape(count, heads, HEAD)
    raw = jnp.einsum("qhd,khd->hqk", queries, keys, preferred_element_type=f32)
    same = segments[:, None] == segments[None, :]
    masked = jnp.where(same[None], raw * score_scale, masked_score)
    exponent = jnp.exp(masked - jnp.max(masked, axis=-1, keepdims=True))
    probs = exponent / jnp.sum(exponent, axis=-1, keepdims=True)
    probs_low = short(probs)
    context = short(
        jnp.einsum("hqk,khd->qhd", probs_low, values, preferred_element_type=f32)
    ).reshape(count, width)
    mid = wide(packed_x[:share]) + reduce_rows(mm(context, wout_low)) + vectors[0]
    normed_one, inverse_one, hidden = norm_forward(mid, vectors[1], vectors[2])
    hidden_low = spread_rows(short(hidden))
    pre_act = mm(hidden_low, wup_low) + bias_up
    phi = 0.5 * lax.erfc(-pre_act * math.sqrt(0.5))
    act_low = short(pre_act * phi)
    slope = phi + pre_act * jnp.exp(-0.5 * pre_act * pre_act) * (1.0 / math.sqrt(2.0 * math.pi))
    normed_two, inverse_two, result = norm_forward(
        hidden + reduce_rows(mm(act_low, wdown_low)) + vectors[3], vectors[4], vectors[5]
    )

    grad_result = wide(grad_rows) * valid_own[:, None]
    grad_z = norm_backward(grad_result, normed_two, inverse_two, vectors[4])
    grad_z_low = spread_rows(short(grad_z))
    grad_pre = short(mm_nt(grad_z_low, wdown_low) * slope)
    grad_hidden = grad_z + reduce_rows(mm_nt(grad_pre, wup_low))
    grad_down = short(mm_tn(act_low, grad_z_low))
    grad_up = short(mm_tn(hidden_low, grad_pre))
    grad_bias_up = jnp.sum(grad_pre, axis=0, dtype=f32)
    grad_mid = norm_backward(grad_hidden, normed_one, inverse_one, vectors[1])
    vector_part = jnp.stack(
        [
            jnp.sum(grad_mid, axis=0),
            jnp.sum(grad_hidden * normed_one, axis=0),
            jnp.sum(grad_hidden, axis=0),
            jnp.sum(grad_z, axis=0),
            jnp.sum(grad_result * normed_two, axis=0),
            jnp.sum(grad_result, axis=0),
        ]
    )
    extra = 16
    joined = jnp.concatenate(
        [short(grad_mid), short(vector_part), jnp.zeros((extra - 6, D), bf16)], 0
    )
    pieces = spread_list(joined)
    grad_mid_low = jnp.concatenate([p[:share] for p in pieces], 0)
    vector_part = sum(wide(p[share : share + 6]) for p in pieces)
    grad_out_t = short(mm_tn(grad_mid_low, context))
    grad_context = short(mm_nt(grad_mid_low, wout_low)).reshape(count, heads, HEAD)
    grad_probs = jnp.einsum("qhd,khd->hqk", grad_context, values, preferred_element_type=f32)
    weighted = jnp.sum(probs * grad_probs, axis=-1, keepdims=True)
    grad_scores = short(probs * (grad_probs - weighted))
    grad_values = short(
        jnp.einsum("hqk,qhd->khd", probs_low, grad_context, preferred_element_type=f32)
    ).reshape(count, width)
    grad_keys = short(
        jnp.einsum("hqk,qhd->khd", grad_scores, queries, preferred_element_type=f32) * score_scale
    ).reshape(count, width)
    grad_queries = short(
        jnp.einsum("hqk,khd->qhd", grad_scores, keys, preferred_element_type=f32) * score_scale
    ).reshape(count, width)
    grad_bias_pair = jnp.stack(
        [jnp.sum(grad_queries, axis=0, dtype=f32), jnp.sum(grad_values, axis=0, dtype=f32)]
    )
    grad_qkvo = jnp.concatenate(
        [
            short(mm_tn(packed_x, jnp.concatenate([grad_queries, grad_keys, grad_values], 1))),
            grad_out_t,
        ],
        1,
    )
    input_part = (
        mm_nt(grad_queries, wqkv_low[0])
        + mm_nt(grad_keys, wqkv_low[1])
        + mm_nt(grad_values, wqkv_low[2])
    )
    columns = D
    small = jnp.concatenate(
        [vector_part.reshape(-1), grad_bias_pair.reshape(-1), grad_bias_up.reshape(-1)]
    )
    rows_small = -(-small.size // (16 * columns)) * 16
    small = jnp.pad(short(small), (0, rows_small * columns - small.size)).reshape(rows_small, columns)
    down_sum, up_sum, qkvo_sum, small_sum, square, gram_tiles = sums_over_dp(
        inner, grad_down, grad_up, grad_qkvo, small, (mom_qkv, mom_out, mom_up, mom_down)
    )
    qkvo_sum = wide(qkvo_sum)
    small_sum = small_sum.reshape(-1)
    gradients = (
        jnp.stack([qkvo_sum[:, k * width : (k + 1) * width] for k in range(3)]),
        qkvo_sum[:, 3 * width :].T,
        wide(up_sum),
        wide(down_sum),
        small_sum[6 * D : 6 * D + 2 * width].reshape(2, width),
        small_sum[6 * D + 2 * width : 6 * D + 2 * width + bias_up.shape[0]],
        small_sum[: 6 * D].reshape(6, D),
    )
    moments_old = (mom_qkv, mom_out, mom_up, mom_down, mom_bias_qv, mom_bias_up, mom_vectors)
    moments = tuple(
        momentum_decay * old + grad for old, grad in zip(moments_old, gradients)
    )

    up_low, down_low = short(moments[2]), short(moments[3])

    def no_work(square, blocks):
        return jnp.zeros((D, width), bf16)

    def square_work(square, blocks):
        return polar_columns(square)

    def gram_work(square, blocks):
        return factor_columns(blocks, D, width)

    stepped = lax.switch(
        (group >= 4).astype(jnp.int32) + (group >= 6).astype(jnp.int32),
        [square_work, gram_work, no_work],
        square,
        gram_tiles,
    )
    dp_rows = D // groups
    steps = lax.all_to_all(
        stepped.reshape(groups, dp_rows, width), "dp", split_axis=0, concat_axis=0, tiled=True
    )
    factors = spread_columns(steps[4:6].reshape(2 * dp_rows, width))

    def mine(values_, dim):
        return lax.dynamic_slice_in_dim(values_, group * dp_rows, dp_rows, dim)

    short_rate = rate_matrix * 0.2 * math.sqrt(D)
    long_rate = rate_matrix * 0.2 * math.sqrt(w_up.shape[1] * teams)
    masters = [
        mine(w_qkv, 1) - short_rate * wide(steps[:3]),
        mine(w_out, 1) - short_rate * wide(steps[3]).T,
        mine(w_up, 0) - long_rate * mm(factors[:dp_rows], up_low),
        mine(w_down, 1) - long_rate * mm_nt(down_low, factors[dp_rows:]),
    ]
    rate_vector = 0.2 / math.sqrt(all_tokens)
    for param, moment in zip((bias_qv, bias_up, vectors), moments[4:]):
        masters.append(param - rate_vector * moment)

    output, grad_tokens = give_back(
        [short(result), short(grad_mid + reduce_rows(input_part))]
    )
    grad_tokens = wide(grad_tokens)
    return (output, grad_tokens, *gradients, *moments, *masters)


def axis_layout(mesh):
    grid = mesh.devices
    groups, teams = grid.shape
    places = [getattr(d, "coords", None) for d in grid[:, 0]]
    inner = 2 if groups % 2 == 0 else 1
    if places[0] is not None:
        moved = [k for k in range(3) if places[0][k] != places[1][k]]
        fixed = [k for k in range(3) if k not in moved]
        inner = 1
        while inner < groups and all(places[inner][k] == places[0][k] for k in fixed):
            inner += 1
        if groups % inner:
            inner = 1
    return inner, (2 if teams % 2 == 0 else 1)


def solution(mesh):
    grads = (
        P(None, None, "tensor"),
        P("tensor", None),
        P(None, "tensor"),
        P("tensor", None),
        P(None, "tensor"),
        P("tensor"),
        P(),
    )
    rows = P("dp", None)
    return jax.shard_map(
        functools.partial(body, axis_layout(mesh)),
        mesh=mesh,
        in_specs=(rows, rows, rows, P(), *grads, *grads),
        out_specs=(
            rows,
            rows,
            *grads,
            *grads,
            P(None, "dp", "tensor"),
            P("tensor", "dp"),
            P("dp", "tensor"),
            P("tensor", "dp"),
            P(None, "tensor"),
            P("tensor"),
            P(),
        ),
        check_vma=False,
    )
```

```python
import functools
import math

import jax
import jax.numpy as jnp
from jax import lax
from jax.experimental import pallas as pl
from jax.experimental.pallas import tpu as pltpu
from jax.sharding import PartitionSpec as P

D = 1024
HEAD = 64

eps_norm = 1e-05
coef_one = 3.4445
coef_two = -4.775
coef_three = 2.0315
momentum_decay = 0.9
rate_matrix = 0.1
masked_score = -1000000000.0
bf16 = jnp.bfloat16
f32 = jnp.float32


def short(value):
    return value.astype(bf16)


def wide(value):
    return value.astype(f32)


def mm(left, right):
    return jnp.dot(short(left), short(right), preferred_element_type=f32)


def mm_nt(left, right):
    return lax.dot_general(
        short(left), short(right), (((1,), (1,)), ((), ())), preferred_element_type=f32
    )


def mm_tn(left, right):
    return lax.dot_general(
        short(left), short(right), (((0,), (0,)), ((), ())), preferred_element_type=f32
    )


def norm_forward(values, gain_row, shift_row):
    average = jnp.mean(values, axis=-1, keepdims=True)
    centred = values - average
    variance = jnp.mean(centred * centred, axis=-1, keepdims=True)
    inverse = lax.rsqrt(variance + eps_norm)
    normed = centred * inverse
    return (normed, inverse, normed * gain_row + shift_row)


def norm_backward(upstream, normed, inverse, gain_row):
    scaled = upstream * gain_row
    centre_term = jnp.mean(scaled, axis=-1, keepdims=True)
    slope_term = jnp.mean(scaled * normed, axis=-1, keepdims=True)
    return inverse * (scaled - centre_term - normed * slope_term)


class Ring:
    def __init__(self, axes, sizes, digit, members=None):
        self.axes = axes
        self.count = sizes[digit]
        self.below = math.prod(sizes[digit + 1 :])
        self.total = math.prod(sizes)
        self.members = members

    def send(self, value, offset):
        count, below = self.count, self.below
        pairs = []
        for i in range(self.total):
            if self.members is not None and not self.members(i):
                continue
            at = (i // below) % count
            pairs.append((i, i + ((at + offset) % count - at) * below))
        return lax.ppermute(value, self.axes, pairs)

    def place(self, linear):
        return (linear // self.below) % self.count


def cut(value, index, size, axis):
    return lax.dynamic_slice_in_dim(value, index * size, size, axis)


def tile_pairs(tiles):
    return [(i, j) for i in range(tiles) for j in range(i, tiles)]


def pick(options, index):
    chosen = jnp.int32(options[0])
    for k in range(1, len(options)):
        chosen = jnp.where(index == k, jnp.int32(options[k]), chosen)
    return chosen


def sum_kernel(
    inner,
    tile,
    down_ref,
    up_ref,
    qkvo_ref,
    small_ref,
    input_ref,
    mid_ref,
    result_ref,
    mom_qkv_ref,
    mom_out_ref,
    mom_up_ref,
    mom_down_ref,
    down_sum_ref,
    up_sum_ref,
    qkvo_sum_ref,
    small_sum_ref,
    square_ref,
    tiles_ref,
    given_ref,
    got_down,
    got_up,
    got_low,
    got_high,
    small_got,
    mom_up,
    mom_down,
    mom_column,
    mom_row,
    up_low,
    down_low,
    part,
    core_got,
    chip_sum,
    x_got,
    ring_sems,
    late_sems,
    small_sems,
    load_sem,
    core_sems,
    x_sems,
    back_sems,
    square_x_sems,
    square_core_sems,
    input_core,
    input_x,
    input_out,
    input_own,
    stage,
    back,
    input_core_sems,
    input_x_sems,
    stage_sems,
    given_sems,
):
    mesh_type = pl.DeviceIdType.MESH
    count = lax.axis_size("dp")
    index = lax.axis_index("dp")
    team = lax.axis_index("tensor")
    wides = lax.axis_size("tensor") // 2
    x_at, core = team // 2, team % 2
    outer = count // inner
    if inner == 2:
        place = jnp.where(index % 2 == 0, index // 2, count - 1 - index // 2)

        def device(p):
            return jnp.where(p < outer, 2 * p, 2 * (count - 1 - p) + 1)
    else:
        place = index

        def device(p):
            return p

    ring_next = ((device((place + 1) % count), team), (device((place + count - 1) % count), team))
    core_next = (index, x_at * 2 + 1 - core)
    x_up = (index, ((x_at + 1) % wides) * 2 + core)
    x_down = (index, ((x_at + wides - 1) % wides) * 2 + core)

    barrier = pltpu.get_barrier_semaphore()

    def greet(hop, carry):
        pl.semaphore_signal(
            barrier, inc=1, device_id=((index + hop) % count, team), device_id_type=mesh_type
        )
        return carry

    lax.fori_loop(1, count, greet, 0)
    for hop in range(1, 2 * wides):
        pl.semaphore_signal(
            barrier,
            inc=1,
            device_id=(index, (team + hop) % (2 * wides)),
            device_id_type=mesh_type,
        )
    pl.semaphore_wait(barrier, count - 1 + 2 * wides - 1)

    def remote(src, dst, sems, at, target):
        return pltpu.make_async_remote_copy(
            src_ref=src,
            dst_ref=dst,
            send_sem=sems.at[(0, *at)],
            recv_sem=sems.at[(1, *at)],
            device_id=target,
            device_id_type=mesh_type,
        )

    sent = []

    def ring(lanes, sems):
        streams = []
        for d, (x_ref, o_ref, first, length, got) in enumerate(lanes):
            chunk = length // count
            halves = 2 if chunk % 32 == 0 else 1
            sub = chunk // halves
            for h in range(halves):
                streams.append((d, h, x_ref, o_ref, first, chunk, sub, got))
        streams.sort(key=lambda one: one[1])

        def rows(stream, hop):
            d, h, _, _, first, chunk, sub, _ = stream
            at = (place + count - hop) % count if d == 0 else (place + hop) % count
            return pl.ds(pl.multiple_of(first + at * chunk + h * sub, 16), sub)

        def copy(stream, step):
            d, h, x_ref, o_ref, _, _, sub, got = stream
            if step < count - 1:
                slot = pl.ds(h * sub, sub)
                src = x_ref.at[rows(stream, 1)] if step == 0 else got.at[step - 1, slot]
                dst = got.at[step, slot]
            else:
                src = dst = o_ref.at[rows(stream, step - (count - 1))]
            return remote(src, dst, sems, (step, d, h), ring_next[d])

        for stream in streams:
            copy(stream, 0).start()
        yield 0
        for step in range(2 * (count - 1)):
            for stream in streams:
                _, h, x_ref, o_ref, _, _, sub, got = stream
                one = copy(stream, step)
                one.wait_recv()
                sent.append(one)
                if step < count - 1:
                    slot = pl.ds(h * sub, sub)
                    total = wide(got[step, slot]) + wide(x_ref[rows(stream, step + 2)])
                    if step < count - 2:
                        got[step, slot] = short(total)
                    else:
                        o_ref[rows(stream, 0)] = short(total)
                if step < 2 * count - 3:
                    copy(stream, step + 1).start()
                yield step

    half = qkvo_ref.shape[0] // 2
    first_ring = ring(
        [
            (down_ref, down_sum_ref, 0, down_ref.shape[0], got_down),
            (up_ref, up_sum_ref, 0, up_ref.shape[0], got_up),
        ],
        ring_sems,
    )
    second_ring = ring(
        [(qkvo_ref, qkvo_sum_ref, 0, half, got_low), (qkvo_ref, qkvo_sum_ref, half, half, got_high)],
        late_sems,
    )

    teams = 2 * wides
    peers = count // teams

    def input_tasks():

        def over_core(i):
            return remote(input_ref.at[wides + i], input_core.at[i], input_core_sems, (i,), core_next)

        def over_x(hop):
            return remote(input_out.at[hop], input_x.at[hop], input_x_sems, (hop,), x_up)

        def over_teams(hop):
            target = (team + hop) % teams
            mine = back.at[pl.ds(team * peers, peers)]
            return remote(stage.at[hop], mine, stage_sems, (hop,), (index, target))

        for i in range(wides - 1, -1, -1):
            over_core(i).start()
        for _ in range(5):
            yield
        for hop in range(wides):
            i = wides - 1 - hop
            over_core(i).wait_recv()
            total = wide(input_ref[i]) + wide(input_core[i])
            if hop > 0:
                over_x(hop - 1).wait_recv()
                total = total + wide(input_x[hop - 1])
            if i > 0:
                input_out[hop] = short(total)
                over_x(hop).start()
                for _ in range(8):
                    yield
            else:
                input_own[...] = short(total + mid_ref[...])
        yield
        part_width = result_ref.shape[2] // teams
        for hop in range(teams):
            columns = pl.ds(pl.multiple_of((team + hop) % teams * part_width, 128), part_width)
            for k, rows_ref in enumerate((result_ref, input_own)):
                stage[hop, :, :, k * part_width : (k + 1) * part_width] = rows_ref[:, :, columns]
            if hop > 0:
                over_teams(hop).start()
            else:
                back[pl.ds(team * peers, peers)] = stage[0]
            yield
        for _ in range(8):
            yield
        for i in range(wides):
            over_core(i).wait_send()
        for hop in range(wides - 1):
            over_x(hop).wait_send()
        for hop in range(1, teams):
            over_teams(hop).wait_recv()
            over_teams(hop).wait_send()

    def give(hop):
        target = (index + hop) % count
        return remote(back.at[target], given_ref.at[index], given_sems, (hop,), (target, team))

    def give_start(hop, carry):
        give(hop).start()
        return carry

    def give_wait(hop, carry):
        give(hop).wait_recv()
        give(hop).wait_send()
        return carry

    is_up, is_down = index == 4, index == 5
    is_gram = jnp.logical_or(is_up, is_down)
    size = up_ref.shape[0]
    pairs = tile_pairs(size // tile)
    share = len(pairs) // 2
    load_up = pltpu.make_async_copy(mom_up_ref, mom_up, load_sem.at[0])
    load_down = pltpu.make_async_copy(mom_down_ref, mom_down, load_sem.at[0])

    def gram_tasks():
        for ref, mom, total, low, load, mine in (
            (mom_up_ref, mom_up, up_sum_ref, up_low, load_up, is_up),
            (mom_down_ref, mom_down, down_sum_ref, down_low, load_down, is_down),
        ):

            @pl.when(mine)
            def _():
                load.wait()

            for start in range(0, ref.shape[0], 256):

                @pl.when(mine)
                def _():
                    rows = pl.ds(start, 256)
                    low[rows, :] = short(momentum_decay * mom[rows, :] + wide(total[rows, :]))

            yield

        def compute(k):
            row = pl.ds(pl.multiple_of(pick([p[0] for p in pairs], k) * tile, tile), tile)
            column = pl.ds(pl.multiple_of(pick([p[1] for p in pairs], k) * tile, tile), tile)

            @pl.when(is_up)
            def _():
                part[k] = mm_nt(up_low[row, :], up_low[column, :])

            @pl.when(is_down)
            def _():
                part[k] = mm_tn(down_low[:, row], down_low[:, column])

        def to_core(i):
            return remote(part.at[(1 - core) * share + i], core_got.at[i], core_sems, (i,), core_next)

        def to_x(i, hop):
            src = chip_sum.at[i] if hop == 0 else x_got.at[hop - 1, i]
            return remote(src, x_got.at[hop, i], x_sems, (hop, i), x_up)

        def to_back(i):
            at = tiles_ref.at[core * share + i]
            return remote(at, at, back_sems, (i,), core_next)

        for i in range(share):
            compute((1 - core) * share + i)

            @pl.when(is_gram)
            def _():
                to_core(i).start()

            yield
        for i in range(share):
            compute(core * share + i)
            yield
        for i in range(share):

            @pl.when(is_gram)
            def _():
                to_core(i).wait_recv()
                chip_sum[i] = part[core * share + i] + core_got[i]
                to_x(i, 0).start()

            yield
        for _ in range(12):
            yield
        for hop in range(wides - 1):
            for i in range(share):

                @pl.when(is_gram)
                def _():
                    to_x(i, hop).wait_recv()
                    before = chip_sum[i] if hop == 0 else tiles_ref[core * share + i]
                    tiles_ref[core * share + i] = before + x_got[hop, i]
                    if hop < wides - 2:
                        to_x(i, hop + 1).start()
                    else:
                        to_back(i).start()

                for _ in range(2):
                    yield

        @pl.when(is_gram)
        def _():
            for i in range(share):
                to_back(i).wait_recv()
                to_core(i).wait_send()
                to_back(i).wait_send()
                for hop in range(wides - 1):
                    to_x(i, hop).wait_send()

    def small_copy(hop):
        return remote(
            small_ref, small_got.at[hop], small_sems, (hop,), ((index + hop) % count, team)
        )

    def small_send(hop, carry):
        small_copy(hop).start()
        return carry

    def small_wait(hop, total):
        one = small_copy(hop)
        one.wait_send()
        one.wait_recv()
        return total + wide(small_got[hop])

    is_column, is_row = index < 3, index == 3
    is_square = index < 4
    width = square_ref.shape[2]
    load_column = pltpu.make_async_copy(
        mom_qkv_ref.at[jnp.minimum(index, 2)], mom_column, load_sem.at[0]
    )
    load_row = pltpu.make_async_copy(mom_out_ref, mom_row, load_sem.at[0])
    square_rows = square_ref.shape[1]
    block = 256
    blocks = square_rows // block

    def square_x(hop, b):
        rows = pl.ds(b * block, block)
        return remote(
            square_ref.at[hop, rows], square_ref.at[hop + 1, rows], square_x_sems, (hop, b), x_down
        )

    def square_core(hop, b):
        rows = pl.ds(b * block, block)
        return remote(
            square_ref.at[hop, rows], square_ref.at[wides + hop, rows], square_core_sems, (hop, b), core_next
        )

    def square_work():
        columns = pl.ds(pl.multiple_of(jnp.minimum(index, 3) * width, 128), width)
        for b in range(blocks):
            rows = pl.ds(b * block, block)
            fresh = wide(qkvo_sum_ref[rows, columns])

            @pl.when(is_column)
            def _():
                if b == 0:
                    load_column.wait()
                square_ref[0, rows] = short(momentum_decay * mom_column[rows, :] + fresh)

            @pl.when(is_row)
            def _():
                if b == 0:
                    load_row.wait()
                square_ref[0, rows] = short(momentum_decay * mom_row[:, rows].T + fresh)

            square_x(0, b).start()
            square_core(0, b).start()
        for hop in range(1, wides):
            for b in range(blocks):
                square_x(hop - 1, b).wait_recv()
                if hop < wides - 1:
                    square_x(hop, b).start()
                square_core(hop, b).start()
        for hop in range(wides):
            for b in range(blocks):
                square_core(hop, b).wait_recv()
        for hop in range(wides):
            for b in range(blocks):
                square_core(hop, b).wait_send()
                if hop < wides - 1:
                    square_x(hop, b).wait_send()

    next(first_ring)
    lax.fori_loop(1, count, small_send, 0)
    for one, mine in (
        (load_up, is_up),
        (load_down, is_down),
        (load_column, is_column),
        (load_row, is_row),
    ):

        @pl.when(mine)
        def _():
            one.start()

    beside = input_tasks()
    for step in first_ring:
        next(beside, None)
        if step >= 2 * count - 6:
            next(second_ring, None)
    for _ in beside:
        pass
    side = gram_tasks()
    for _ in second_ring:
        next(side, None)
    lax.fori_loop(1, count, give_start, 0)
    given_ref[index] = back[index]
    pl.when(is_square)(square_work)
    for _ in side:
        pass
    lax.fori_loop(1, count, give_wait, 0)
    small_sum_ref[...] = lax.fori_loop(1, count, small_wait, wide(small_ref[...]))
    for one in sent:
        one.wait_send()


def sums_over_dp(inner, down, up, qkvo, small, input_part, grad_mid, result, moments_old):
    groups, teams = lax.axis_size("dp"), lax.axis_size("tensor")
    wides = teams // 2
    size, width = qkvo.shape[0], qkvo.shape[1] // 4
    tile = size // 4
    pairs = len(tile_pairs(4))
    steps = 2 * (groups - 1)
    mom_qkv, mom_out, mom_up, mom_down = moments_old
    dma = pltpu.SemaphoreType.DMA
    vmem = pl.BlockSpec(memory_space=pltpu.VMEM)
    length = down.size + up.size + qkvo.size
    peers, rows, model = result.shape
    return pl.pallas_call(
        functools.partial(sum_kernel, inner, tile),
        name="sums_over_dp",
        out_shape=(
            jax.ShapeDtypeStruct(down.shape, bf16),
            jax.ShapeDtypeStruct(up.shape, bf16),
            jax.ShapeDtypeStruct(qkvo.shape, bf16),
            jax.ShapeDtypeStruct(small.shape, f32),
            jax.ShapeDtypeStruct((teams, size, width), bf16),
            jax.ShapeDtypeStruct((pairs, tile, tile), f32),
            jax.ShapeDtypeStruct((groups, rows, 2 * (model // teams)), bf16),
        ),
        in_specs=[vmem] * 7 + [pl.BlockSpec(memory_space=pl.ANY)] * 4,
        out_specs=[vmem] * 7,
        scratch_shapes=[
            pltpu.VMEM((groups - 1, down.shape[0] // groups, down.shape[1]), bf16),
            pltpu.VMEM((groups - 1, up.shape[0] // groups, up.shape[1]), bf16),
            pltpu.VMEM((groups - 1, size // 2 // groups, qkvo.shape[1]), bf16),
            pltpu.VMEM((groups - 1, size // 2 // groups, qkvo.shape[1]), bf16),
            pltpu.VMEM((groups, *small.shape), bf16),
            pltpu.VMEM(up.shape, f32),
            pltpu.VMEM(down.shape, f32),
            pltpu.VMEM((size, width), f32),
            pltpu.VMEM((width, size), f32),
            pltpu.VMEM(up.shape, bf16),
            pltpu.VMEM(down.shape, bf16),
            pltpu.VMEM((pairs, tile, tile), f32),
            pltpu.VMEM((pairs // 2, tile, tile), f32),
            pltpu.VMEM((pairs // 2, tile, tile), f32),
            pltpu.VMEM((wides - 1, pairs // 2, tile, tile), f32),
            dma((2, steps, 2, 2)),
            dma((2, steps, 2, 2)),
            dma((2, groups)),
            dma((1,)),
            dma((2, pairs // 2)),
            dma((2, wides - 1, pairs // 2)),
            dma((2, pairs // 2)),
            dma((2, wides - 1, size // 256)),
            dma((2, wides, size // 256)),
            pltpu.VMEM((wides, peers, rows, model), bf16),
            pltpu.VMEM((wides - 1, peers, rows, model), bf16),
            pltpu.VMEM((wides - 1, peers, rows, model), bf16),
            pltpu.VMEM((peers, rows, model), bf16),
            pltpu.VMEM((teams, peers, rows, 2 * (model // teams)), bf16),
            pltpu.VMEM((groups, rows, 2 * (model // teams)), bf16),
            dma((2, wides)),
            dma((2, wides - 1)),
            dma((2, teams)),
            dma((2, groups)),
        ],
        compiler_params=pltpu.CompilerParams(
            collective_id=0, has_side_effects=True, vmem_limit_bytes=52 * 2**20
        ),
        cost_estimate=pl.CostEstimate(
            flops=length, bytes_accessed=4 * length, transcendentals=0
        ),
    )(
        down, up, qkvo, small, input_part, grad_mid, result, mom_qkv, mom_out, mom_up, mom_down
    )


def dot(left, right):
    return jnp.dot(left, right, preferred_element_type=f32)

def dot_nt(left, right):
    return lax.dot_general(left, right, (((1,), (1,)), ((), ())), preferred_element_type=f32)

def middle_kernel(
    context_ref,
    x_ref,
    out_ref,
    up_ref,
    down_ref,
    bias_ref,
    vectors_ref,
    upstream_ref,
    valid_ref,
    hidden_ref,
    act_ref,
    grad_z_ref,
    grad_pre_ref,
    grad_mid_ref,
    own_grad_mid_ref,
    result_ref,
    vector_sum_ref,
    grad_down_ref,
    grad_up_ref,
    slope,
    held,
    core_out,
    core_got,
    x_out,
    x_got,
    normed_one,
    own_hidden,
    normed_two,
    own_grad_z,
    vector_own,
    vector_got,
    core_sems,
    x_sems,
    spread_x_sems,
    spread_core_sems,
    vector_sems,
):
    mesh_type = pl.DeviceIdType.MESH
    index = lax.axis_index("dp")
    team = lax.axis_index("tensor")
    teams = lax.axis_size("tensor")
    wides = teams // 2
    x_at, core = team // 2, team % 2
    core_next = (index, x_at * 2 + 1 - core)
    x_up = (index, ((x_at + 1) % wides) * 2 + core)
    x_down = (index, ((x_at + wides - 1) % wides) * 2 + core)
    barrier = pltpu.get_barrier_semaphore()
    for hop in range(1, teams):
        pl.semaphore_signal(
            barrier, inc=1, device_id=(index, (team + hop) % teams), device_id_type=mesh_type
        )
    pl.semaphore_wait(barrier, teams - 1)
    sent = []

    def remote(src, dst, sems, at, target):
        return pltpu.make_async_remote_copy(
            src_ref=src,
            dst_ref=dst,
            send_sem=sems.at[(0, *at)],
            recv_sem=sems.at[(1, *at)],
            device_id=target,
            device_id_type=mesh_type,
        )

    def start(one):
        one.start()
        sent.append(one)

    def over_core(s, i):
        return remote(core_out.at[s, i], core_got.at[s, i], core_sems, (s, i), core_next)

    def over_x(s, hop):
        return remote(x_out.at[s, hop], x_got.at[s, hop], x_sems, (s, hop), x_up)

    def finish(s, filler):
        for hop in range(wides):
            i = wides - 1 - hop
            over_core(s, i).wait_recv()
            total = held[i] + wide(core_got[s, i])
            if hop > 0:
                if filler is not None:
                    filler()
                    filler = None
                over_x(s, hop - 1).wait_recv()
                total = total + wide(x_got[s, hop - 1])
            if i > 0:
                x_out[s, hop] = short(total)
                start(over_x(s, hop))
        return total

    def along_x(s, ref, i):
        return remote(ref.at[i], ref.at[i + 1], spread_x_sems, (s, i), x_down)

    def across(s, ref, i):
        return remote(ref.at[i], ref.at[wides + i], spread_core_sems, (s, i), core_next)

    def spread(s, ref):
        start(along_x(s, ref, 0))
        start(across(s, ref, 0))

    def arrive(s, ref, i):
        if i > 0:
            along_x(s, ref, i - 1).wait_recv()
            start(across(s, ref, i))
            if i < wides - 1:
                start(along_x(s, ref, i))
        across(s, ref, i).wait_recv()

    share = x_ref.shape[0]

    def pair(ref, i):
        return jnp.concatenate([ref[i], ref[wides + i]], 0)

    def put_pair(ref, i, value):
        ref[i] = value[:share]
        ref[wides + i] = value[share:]

    def keep(s, i, partial):
        core_out[s, i] = short(partial[share:])
        start(over_core(s, i))
        held[i] = partial[:share]

    def sums(value):
        return jnp.sum(value, axis=0, keepdims=True)

    for i in range(wides - 1, -1, -1):
        keep(0, i, dot(pair(context_ref, i), out_ref[...]))
    mid = wide(x_ref[...]) + finish(0, None) + vectors_ref[0:1, :]
    normed, inverse_one, hidden = norm_forward(mid, vectors_ref[1:2, :], vectors_ref[2:3, :])
    normed_one[...] = normed
    own_hidden[...] = hidden
    hidden_ref[0] = short(hidden)
    spread(0, hidden_ref)

    units = up_ref.shape[1]
    step = min(units, 512)
    for i in range(wides):
        arrive(0, hidden_ref, i)
        rows = pair(hidden_ref, i)
        for c in range(0, units, step):
            at = slice(c, c + step)
            pre = dot(rows, up_ref[:, at]) + bias_ref[:, at]
            phi = 0.5 + 0.5 * lax.erf(pre * math.sqrt(0.5))
            act = short(pre * phi)
            bend = phi + pre * jnp.exp(-0.5 * pre * pre) * (1.0 / math.sqrt(2.0 * math.pi))
            for r, part in ((i, slice(0, share)), (wides + i, slice(share, 2 * share))):
                act_ref[r, :, at] = act[part]
                slope[r, :, at] = bend[part]
        keep(1, i, dot(pair(act_ref, i), down_ref[...]))
    summed = own_hidden[...] + finish(1, None) + vectors_ref[3:4, :]
    gain_two = vectors_ref[4:5, :]
    normed, inverse_two, result = norm_forward(summed, gain_two, vectors_ref[5:6, :])
    result_ref[...] = short(result)
    upstream = wide(upstream_ref[...]) * valid_ref[...]
    grad_z = norm_backward(upstream, normed, inverse_two, gain_two)
    own_grad_z[...] = grad_z
    grad_z_ref[0] = short(grad_z)
    spread(1, grad_z_ref)
    vector_own[...] = jnp.zeros_like(vector_own)
    vector_own[3:4, :] = sums(grad_z)
    vector_own[4:5, :] = sums(upstream * normed)
    vector_own[5:6, :] = sums(upstream)

    for i in range(wides):
        arrive(1, grad_z_ref, i)
        rows = pair(grad_z_ref, i)
        for c in range(0, units, step):
            at = slice(c, c + step)
            grad = dot_nt(rows, down_ref[at, :])
            for r, part in ((i, slice(0, share)), (wides + i, slice(share, 2 * share))):
                grad_pre_ref[r, :, at] = short(grad[part] * slope[r, :, at])
        keep(2, i, dot_nt(pair(grad_pre_ref, i), up_ref[...]))

    def every(ref, at):
        return jnp.concatenate([ref[r, :, at] for r in range(teams)], 0)

    def down_filler():
        def one(k, carry):
            at = pl.ds(pl.multiple_of(k * 128, 128), 128)
            grad_down_ref[at, :] = short(mm_tn(every(act_ref, at), every(grad_z_ref, slice(None))))
            return carry

        lax.fori_loop(0, units // 128, one, 0)

    grad_hidden = own_grad_z[...] + finish(2, down_filler)
    grad_mid = norm_backward(grad_hidden, normed_one[...], inverse_one, vectors_ref[1:2, :])
    own_grad_mid_ref[...] = grad_mid
    grad_mid_ref[0] = short(grad_mid)
    spread(2, grad_mid_ref)
    vector_own[0:1, :] = sums(grad_mid)
    vector_own[1:2, :] = sums(grad_hidden * normed_one[...])
    vector_own[2:3, :] = sums(grad_hidden)

    def to_team(hop):
        return remote(
            vector_own, vector_got.at[hop], vector_sems, (hop,), (index, (team + hop) % teams)
        )

    for hop in range(1, teams):
        start(to_team(hop))

    def up_filler(k, carry):
        at = pl.ds(pl.multiple_of(k * 128, 128), 128)
        grad_up_ref[at, :] = short(mm_tn(every(hidden_ref, at), every(grad_pre_ref, slice(None))))
        return carry

    lax.fori_loop(0, hidden_ref.shape[2] // 128, up_filler, 0)
    for i in range(wides):
        arrive(2, grad_mid_ref, i)
    total = vector_own[...]
    for hop in range(1, teams):
        to_team(hop).wait_recv()
        total = total + vector_got[hop]
    vector_sum_ref[...] = total
    for one in sent:
        one.wait_send()


def middle(context, x_own, w_out, w_up, w_down, bias_up, vectors, upstream, valid):
    teams, share, width = context.shape
    model, units = w_up.shape
    wides = teams // 2
    dma = pltpu.SemaphoreType.DMA
    vmem = pl.BlockSpec(memory_space=pltpu.VMEM)
    rows = jax.ShapeDtypeStruct((teams, share, model), bf16)
    inner = jax.ShapeDtypeStruct((teams, share, units), bf16)
    own = pltpu.VMEM((share, model), f32)
    return pl.pallas_call(
        middle_kernel,
        name="middle",
        out_shape=(
            rows,
            inner,
            rows,
            inner,
            rows,
            jax.ShapeDtypeStruct((share, model), f32),
            jax.ShapeDtypeStruct((share, model), bf16),
            jax.ShapeDtypeStruct((8, model), f32),
            jax.ShapeDtypeStruct((units, model), bf16),
            jax.ShapeDtypeStruct((model, units), bf16),
        ),
        in_specs=[vmem] * 9,
        out_specs=[vmem] * 10,
        scratch_shapes=[
            pltpu.VMEM((teams, share, units), f32),
            pltpu.VMEM((wides, share, model), f32),
            pltpu.VMEM((3, wides, share, model), bf16),
            pltpu.VMEM((3, wides, share, model), bf16),
            pltpu.VMEM((3, wides - 1, share, model), bf16),
            pltpu.VMEM((3, wides - 1, share, model), bf16),
            own,
            own,
            own,
            own,
            pltpu.VMEM((8, model), f32),
            pltpu.VMEM((teams, 8, model), f32),
            dma((2, 3, wides)),
            dma((2, 3, wides - 1)),
            dma((2, 3, wides - 1)),
            dma((2, 3, wides)),
            dma((2, teams)),
        ],
        compiler_params=pltpu.CompilerParams(
            collective_id=1, has_side_effects=True, vmem_limit_bytes=48 * 2**20
        ),
        cost_estimate=pl.CostEstimate(
            flops=12 * teams * share * model * units,
            bytes_accessed=8 * model * units,
            transcendentals=0,
        ),
    )(context, x_own, w_out, w_up, w_down, bias_up.reshape(1, units), vectors, upstream, valid)


def polar_kernel(block, m_ref, o_ref, x_ref, gram_ref, low_ref, mix_ref):
    teams, size, width = m_ref.shape
    keep = o_ref.shape[1]
    bits = 256

    def rows(i):
        return pl.ds(pl.multiple_of(i * bits, bits), bits)

    def columns(j):
        return pl.ds(pl.multiple_of(j * block, block), block)

    def norm_step(i, total):
        for r in range(teams):
            part = wide(m_ref[r, rows(i), :])
            total = total + jnp.sum(part * part, axis=0, keepdims=True)
        return total

    total = lax.fori_loop(0, size // bits, norm_step, jnp.zeros((1, width), f32))
    scale = lax.rsqrt(jnp.sum(total, axis=1, keepdims=True) + 1e-07)

    def scale_step(i, carry):
        for r in range(teams):
            x_ref[0, rows(i), r * width : (r + 1) * width] = short(wide(m_ref[r, rows(i), :]) * scale)
        return carry

    lax.fori_loop(0, size // bits, scale_step, 0)

    def sweep(k, carry):
        now = k % 2
        x = x_ref.at[now]

        def gram_step(j, carry):
            gram = dot_nt(x[...], x[columns(j), :])
            gram_ref[:, columns(j)] = gram
            low_ref[:, columns(j)] = short(gram)
            return carry

        def mix_step(j, carry):
            power = dot(low_ref[...], low_ref[:, columns(j)])
            mix_ref[:, columns(j)] = short(coef_two * gram_ref[:, columns(j)] + coef_three * power)
            return carry

        def next_step(j, carry):
            mixed = dot(mix_ref[...], x[:, columns(j)])
            x_ref[1 - now, :, columns(j)] = short(coef_one * wide(x[:, columns(j)]) + mixed)
            return carry

        lax.fori_loop(0, size // block, gram_step, 0)
        lax.fori_loop(0, size // block, mix_step, 0)
        lax.fori_loop(0, jnp.where(k < 4, size // block, -(-keep // block)), next_step, 0)
        return carry

    lax.fori_loop(0, 5, sweep, 0)
    o_ref[...] = x_ref[1, :, :keep]


def factor_kernel(block, g_ref, o_ref, current_ref, poly_ref, half_ref, factor_ref):
    size = poly_ref.shape[0]
    tile = g_ref.shape[1]
    tiles = size // tile
    keep = o_ref.shape[1]
    first = lax.axis_index("tensor") * keep
    eye = lax.broadcasted_iota(jnp.int32, (tile, tile), 0) == lax.broadcasted_iota(
        jnp.int32, (tile, tile), 1
    )
    trace = jnp.zeros((1, 1), f32)
    for k, (i, j) in enumerate(tile_pairs(tiles)):
        if i == j:
            diagonal = jnp.where(eye, g_ref[k], 0.0)
            trace = trace + jnp.sum(jnp.sum(diagonal, axis=0, keepdims=True), axis=1, keepdims=True)
    scale = lax.rsqrt(trace + 1e-07)
    scale_two = scale * scale

    def store(slot, rows, columns, value):
        high = short(value)
        current_ref[slot, 0, rows, columns] = high
        current_ref[slot, 1, rows, columns] = short(value - wide(high))

    def span(i):
        return slice(i * tile, (i + 1) * tile)

    for k, (i, j) in enumerate(tile_pairs(tiles)):
        part = g_ref[k] * scale_two
        store(0, span(i), span(j), part)
        if i != j:
            store(0, span(j), span(i), part.T)

    def cols(j):
        return pl.ds(pl.multiple_of(j * block, block), block)

    def sweep(k, exact, last):
        now = k % 2
        high_ref, low_ref = current_ref.at[now, 0], current_ref.at[now, 1]

        def poly_step(j, carry):
            power = dot(high_ref[...], high_ref[:, cols(j)])
            if not exact:
                power = power + dot(high_ref[...], low_ref[:, cols(j)])
            r = lax.broadcasted_iota(jnp.int32, (size, block), 0)
            c = lax.broadcasted_iota(jnp.int32, (size, block), 1) + j * block
            present = wide(high_ref[:, cols(j)]) + wide(low_ref[:, cols(j)])
            poly = coef_two * present + coef_three * power
            poly_ref[:, cols(j)] = short(poly + jnp.where(r == c, coef_one, 0.0))
            return carry

        def half_step(j, carry):
            half = dot(poly_ref[...], high_ref[:, cols(j)])
            if exact:
                half = half + dot(poly_ref[...], low_ref[:, cols(j)])
            high = short(half)
            half_ref[0, :, cols(j)] = high
            if exact:
                half_ref[1, :, cols(j)] = short(half - wide(high))
            return carry

        def next_step(j, carry):
            new = dot(half_ref[0], poly_ref[:, cols(j)])
            if exact:
                new = new + dot(half_ref[1], poly_ref[:, cols(j)])
            store(1 - now, slice(None), cols(j), new)
            return carry

        lax.fori_loop(0, size // block, poly_step, 0)
        if not last:
            lax.fori_loop(0, size // block, half_step, 0)
            lax.fori_loop(0, size // block, next_step, 0)

    def exact_sweep(k, carry):
        sweep(k, True, False)

        @pl.when(k == 0)
        def _():
            factor_ref[...] = poly_ref[:, pl.ds(pl.multiple_of(first, 128), keep)]

        @pl.when(k > 0)
        def _():
            factor_ref[...] = short(dot(poly_ref[...], factor_ref[...]))

        return carry

    def plain_sweep(k, carry):
        sweep(k, False, False)
        factor_ref[...] = short(dot(poly_ref[...], factor_ref[...]))
        return carry

    lax.fori_loop(0, 2, exact_sweep, 0)
    lax.fori_loop(2, 4, plain_sweep, 0)
    sweep(4, False, True)
    o_ref[...] = short(dot(poly_ref[...], factor_ref[...]) * scale)


def step_kernel(
    block,
    square_ref,
    tiles_ref,
    o_ref,
    x_ref,
    gram_ref,
    low_ref,
    mix_ref,
    current_ref,
    poly_ref,
    half_ref,
    factor_ref,
):
    index = lax.axis_index("dp")

    @pl.when(index < 4)
    def _():
        polar_kernel(block, square_ref, o_ref, x_ref, gram_ref, low_ref, mix_ref)

    @pl.when(jnp.logical_or(index == 4, index == 5))
    def _():
        factor_kernel(block, tiles_ref, o_ref, current_ref, poly_ref, half_ref, factor_ref)

    @pl.when(index > 5)
    def _():
        o_ref[...] = jnp.zeros_like(o_ref)


def orthogonal_columns(square, tiles):
    teams, size, width = square.shape
    vmem = pl.BlockSpec(memory_space=pltpu.VMEM)
    return pl.pallas_call(
        functools.partial(step_kernel, 512),
        name="orthogonal_columns",
        out_shape=jax.ShapeDtypeStruct((size, width), bf16),
        in_specs=[vmem] * 2,
        out_specs=vmem,
        scratch_shapes=[
            pltpu.VMEM((2, size, teams * width), bf16),
            pltpu.VMEM((size, size), f32),
            pltpu.VMEM((size, size), bf16),
            pltpu.VMEM((size, size), bf16),
            pltpu.VMEM((2, 2, size, size), bf16),
            pltpu.VMEM((size, size), bf16),
            pltpu.VMEM((2, size, size), bf16),
            pltpu.VMEM((size, width), bf16),
        ],
        compiler_params=pltpu.CompilerParams(vmem_limit_bytes=48 * 2**20),
        cost_estimate=pl.CostEstimate(
            flops=40 * size**3, bytes_accessed=8 * size * size, transcendentals=0
        ),
    )(square, tiles)


def body(
    layout,
    tokens,
    cotangent,
    lengths,
    packing,
    w_qkv,
    w_out,
    w_up,
    w_down,
    bias_qv,
    bias_up,
    vectors,
    mom_qkv,
    mom_out,
    mom_up,
    mom_down,
    mom_bias_qv,
    mom_bias_up,
    mom_vectors,
):
    inner, cores = layout
    groups = lax.axis_size("dp")
    teams = lax.axis_size("tensor")
    group = lax.axis_index("dp")
    team = lax.axis_index("tensor")
    outer, wides = groups // inner, teams // cores
    count = tokens.shape[0]
    per_peer = count // groups
    share = count // teams
    width = D // teams
    all_tokens = count * groups

    outer_ring = Ring("dp", (outer, inner), 0)
    inner_ring = Ring("dp", (outer, inner), 1)
    outer_at, inner_at = outer_ring.place(group), inner_ring.place(group)
    x_ring = Ring("tensor", (wides, cores), 0)
    core_ring = Ring("tensor", (wides, cores), 1)
    x_at, core_at = x_ring.place(team), core_ring.place(team)

    def team_of(rank):
        return ((x_at + rank % wides) % wides) * cores + (core_at + rank // wides) % cores

    def to_relative(value, size, axis=0):
        return jnp.concatenate([cut(value, team_of(r), size, axis) for r in range(teams)], axis)

    def to_given(value, size, axis=0):
        parts = []
        for other in range(teams):
            rank = ((other % cores - core_at) % cores) * wides + (other // cores - x_at) % wides
            parts.append(cut(value, rank, size, axis))
        return jnp.concatenate(parts, axis)

    def spread_list(piece, ring_x=x_ring, ring_core=core_ring):
        line = [piece]
        for _ in range(wides - 1):
            line.append(ring_x.send(line[-1], -1))
        pieces = list(line)
        for hop in range(1, cores):
            pieces += [ring_core.send(p, -hop) for p in line]
        return pieces

    def spread_columns(piece):
        return to_given(jnp.concatenate(spread_list(piece), 1), piece.shape[1], 1)

    def own_rows(value):
        return cut(value, team, share, 0)

    position = jnp.arange(count, dtype=jnp.int32)
    peer = jnp.arange(groups, dtype=jnp.int32)
    packed = packing.reshape(groups, count)
    source = packed // count
    source_mine = lax.dynamic_index_in_dim(source, group, 0, keepdims=False)
    masks = jnp.concatenate([source == group, source_mine[None, :] == peer[:, None]], 0)
    before = (position[:, None] < position[None, :]).astype(bf16)
    rank = mm(masks.astype(bf16), before).astype(jnp.int32)
    key = jnp.where(masks, rank, -1)
    value = jnp.concatenate(
        [packed % count, jnp.broadcast_to(position[None, :], (groups, count))], 0
    )
    slot_in_message = jnp.arange(per_peer, dtype=jnp.int32)
    picked = jnp.sum(
        jnp.where(key[:, None, :] == slot_in_message[None, :, None], value[:, None, :], 0), axis=-1
    )
    rows_sent = picked[:groups].reshape(count)
    slots = picked[groups:].reshape(count)
    choose = (rows_sent[:, None] == position[None, :]).astype(bf16)

    length_row = lengths[0]
    end_one = length_row[0]
    end_two = end_one + length_row[1]
    end_all = end_two + length_row[2]
    segments = (
        (slots >= end_one).astype(jnp.int32)
        + (slots >= end_two).astype(jnp.int32)
        + (slots >= end_all).astype(jnp.int32)
        + jnp.maximum(slots - end_all, 0)
    )
    valid_own = own_rows((slots < end_all).astype(f32))
    segments = to_relative(segments, share)

    own_columns = jnp.concatenate([cut(tokens, team, width, 1), cut(cotangent, team, width, 1)], 1)
    sent = short(mm(choose, own_columns)).reshape(groups, per_peer, 2 * width)
    got = lax.all_to_all(sent, "dp", split_axis=0, concat_axis=0, tiled=True)
    got = got.reshape(count, 2 * width)

    packed_x = to_relative(spread_columns(got[:, :width]), share)
    turns = []
    for hop in range(teams):
        block = cut(got[:, width:], (team + hop) % teams, share, 0)
        if hop > 0:
            block = lax.ppermute(block, "tensor", [(i, (i + hop) % teams) for i in range(teams)])
        turns.append(block)
    turns = jnp.concatenate(turns, 1)
    grad_rows = jnp.concatenate(
        [cut(turns, (team - other) % teams, width, 1) for other in range(teams)], 1
    )

    wqkv_low = short(w_qkv)
    wout_low = short(w_out)
    wup_low = short(w_up)
    wdown_low = short(w_down)
    heads = width // HEAD
    score_scale = HEAD ** (-0.5)
    queries = short(mm(packed_x, wqkv_low[0]) + bias_qv[0]).reshape(count, heads, HEAD)
    keys = short(mm(packed_x, wqkv_low[1])).reshape(count, heads, HEAD)
    values = short(mm(packed_x, wqkv_low[2]) + bias_qv[1]).reshape(count, heads, HEAD)
    raw = jnp.einsum("qhd,khd->hqk", queries, keys, preferred_element_type=f32)
    same = segments[:, None] == segments[None, :]
    masked = jnp.where(same[None], raw * score_scale, masked_score)
    exponent = jnp.exp(masked - jnp.max(masked, axis=-1, keepdims=True))
    probs = exponent / jnp.sum(exponent, axis=-1, keepdims=True)
    probs_low = short(probs)
    context = short(
        jnp.einsum("hqk,khd->qhd", probs_low, values, preferred_element_type=f32)
    ).reshape(count, width)
    (
        hidden_low,
        act_low,
        grad_z_low,
        grad_pre,
        grad_mid_low,
        grad_mid,
        result,
        vector_part,
        grad_down,
        grad_up,
    ) = middle(
        context.reshape(teams, share, width),
        packed_x[:share],
        wout_low,
        wup_low,
        wdown_low,
        bias_up,
        vectors,
        grad_rows,
        valid_own[:, None],
    )
    grad_bias_up = jnp.sum(grad_pre, axis=(0, 1), dtype=f32)
    grad_mid_low = grad_mid_low.reshape(count, D)
    vector_part = vector_part[:6]
    grad_out_t = short(mm_tn(grad_mid_low, context))
    grad_context = short(mm_nt(grad_mid_low, wout_low)).reshape(count, heads, HEAD)
    grad_probs = jnp.einsum("qhd,khd->hqk", grad_context, values, preferred_element_type=f32)
    weighted = jnp.sum(probs * grad_probs, axis=-1, keepdims=True)
    grad_scores = short(probs * (grad_probs - weighted))
    grad_values = short(
        jnp.einsum("hqk,qhd->khd", probs_low, grad_context, preferred_element_type=f32)
    ).reshape(count, width)
    grad_keys = short(
        jnp.einsum("hqk,qhd->khd", grad_scores, queries, preferred_element_type=f32) * score_scale
    ).reshape(count, width)
    grad_queries = short(
        jnp.einsum("hqk,khd->qhd", grad_scores, keys, preferred_element_type=f32) * score_scale
    ).reshape(count, width)
    grad_bias_pair = jnp.stack(
        [jnp.sum(grad_queries, axis=0, dtype=f32), jnp.sum(grad_values, axis=0, dtype=f32)]
    )
    grad_qkvo = jnp.concatenate(
        [
            short(mm_tn(packed_x, jnp.concatenate([grad_queries, grad_keys, grad_values], 1))),
            grad_out_t,
        ],
        1,
    )
    input_part = (
        mm_nt(grad_queries, wqkv_low[0])
        + mm_nt(grad_keys, wqkv_low[1])
        + mm_nt(grad_values, wqkv_low[2])
    )
    columns = D
    small = jnp.concatenate(
        [vector_part.reshape(-1), grad_bias_pair.reshape(-1), grad_bias_up.reshape(-1)]
    )
    rows_small = -(-small.size // (16 * columns)) * 16
    small = jnp.pad(short(small), (0, rows_small * columns - small.size)).reshape(rows_small, columns)
    down_sum, up_sum, qkvo_sum, small_sum, square, gram_tiles, given = sums_over_dp(
        inner,
        grad_down,
        grad_up,
        grad_qkvo,
        small,
        short(input_part).reshape(teams, groups // teams, per_peer, D),
        grad_mid.reshape(groups // teams, per_peer, D),
        result.reshape(groups // teams, per_peer, D),
        (mom_qkv, mom_out, mom_up, mom_down),
    )
    pieces = spread_list(short(mm_tn(choose, given.reshape(count, 2 * width))))
    output = to_given(jnp.concatenate([p[:, :width] for p in pieces], 1), width, 1)
    grad_tokens = wide(to_given(jnp.concatenate([p[:, width:] for p in pieces], 1), width, 1))

    qkvo_sum = wide(qkvo_sum)
    small_sum = small_sum.reshape(-1)
    gradients = (
        jnp.stack([qkvo_sum[:, k * width : (k + 1) * width] for k in range(3)]),
        qkvo_sum[:, 3 * width :].T,
        wide(up_sum),
        wide(down_sum),
        small_sum[6 * D : 6 * D + 2 * width].reshape(2, width),
        small_sum[6 * D + 2 * width : 6 * D + 2 * width + bias_up.shape[0]],
        small_sum[: 6 * D].reshape(6, D),
    )
    moments_old = (mom_qkv, mom_out, mom_up, mom_down, mom_bias_qv, mom_bias_up, mom_vectors)
    moments = tuple(
        momentum_decay * old + grad for old, grad in zip(moments_old, gradients)
    )

    up_low, down_low = short(moments[2]), short(moments[3])

    stepped = orthogonal_columns(square, gram_tiles)
    dp_rows = D // groups
    steps = lax.all_to_all(
        stepped.reshape(groups, dp_rows, width), "dp", split_axis=0, concat_axis=0, tiled=True
    )
    factors = spread_columns(steps[4:6].reshape(2 * dp_rows, width))

    def mine(values_, dim):
        return lax.dynamic_slice_in_dim(values_, group * dp_rows, dp_rows, dim)

    short_rate = rate_matrix * 0.2 * math.sqrt(D)
    long_rate = rate_matrix * 0.2 * math.sqrt(w_up.shape[1] * teams)
    masters = [
        mine(w_qkv, 1) - short_rate * wide(steps[:3]),
        mine(w_out, 1) - short_rate * wide(steps[3]).T,
        mine(w_up, 0) - long_rate * mm(factors[:dp_rows], up_low),
        mine(w_down, 1) - long_rate * mm_nt(down_low, factors[dp_rows:]),
    ]
    rate_vector = 0.2 / math.sqrt(all_tokens)
    for param, moment in zip((bias_qv, bias_up, vectors), moments[4:]):
        masters.append(param - rate_vector * moment)

    return (output, grad_tokens, *gradients, *moments, *masters)


def axis_layout(mesh):
    grid = mesh.devices
    groups, teams = grid.shape
    places = [getattr(d, "coords", None) for d in grid[:, 0]]
    inner = 2 if groups % 2 == 0 else 1
    if places[0] is not None:
        moved = [k for k in range(3) if places[0][k] != places[1][k]]
        fixed = [k for k in range(3) if k not in moved]
        inner = 1
        while inner < groups and all(places[inner][k] == places[0][k] for k in fixed):
            inner += 1
        if groups % inner:
            inner = 1
    return inner, (2 if teams % 2 == 0 else 1)


def solution(mesh):
    grads = (
        P(None, None, "tensor"),
        P("tensor", None),
        P(None, "tensor"),
        P("tensor", None),
        P(None, "tensor"),
        P("tensor"),
        P(),
    )
    rows = P("dp", None)
    return jax.shard_map(
        functools.partial(body, axis_layout(mesh)),
        mesh=mesh,
        in_specs=(rows, rows, rows, P(), *grads, *grads),
        out_specs=(
            rows,
            rows,
            *grads,
            *grads,
            P(None, "dp", "tensor"),
            P("tensor", "dp"),
            P("dp", "tensor"),
            P("tensor", "dp"),
            P(None, "tensor"),
            P("tensor"),
            P(),
        ),
        check_vma=False,
    )
```

```python
import functools
import math

import jax
import jax.numpy as jnp
from jax import lax
from jax.experimental import pallas as pl
from jax.experimental.pallas import tpu as pltpu
from jax.sharding import PartitionSpec as P

D = 1024
HEAD = 64

eps_norm = 1e-05
coef_one = 3.4445
coef_two = -4.775
coef_three = 2.0315
momentum_decay = 0.9
rate_matrix = 0.1
masked_score = -1000000000.0
bf16 = jnp.bfloat16
f32 = jnp.float32


def short(value):
    return value.astype(bf16)


def wide(value):
    return value.astype(f32)


def mm(left, right):
    return jnp.dot(short(left), short(right), preferred_element_type=f32)


def mm_nt(left, right):
    return lax.dot_general(
        short(left), short(right), (((1,), (1,)), ((), ())), preferred_element_type=f32
    )


def mm_tn(left, right):
    return lax.dot_general(
        short(left), short(right), (((0,), (0,)), ((), ())), preferred_element_type=f32
    )


def norm_forward(values, gain_row, shift_row):
    average = jnp.mean(values, axis=-1, keepdims=True)
    centred = values - average
    variance = jnp.mean(centred * centred, axis=-1, keepdims=True)
    inverse = lax.rsqrt(variance + eps_norm)
    normed = centred * inverse
    return (normed, inverse, normed * gain_row + shift_row)


def norm_backward(upstream, normed, inverse, gain_row):
    scaled = upstream * gain_row
    centre_term = jnp.mean(scaled, axis=-1, keepdims=True)
    slope_term = jnp.mean(scaled * normed, axis=-1, keepdims=True)
    return inverse * (scaled - centre_term - normed * slope_term)


class Ring:
    def __init__(self, axes, sizes, digit, members=None):
        self.axes = axes
        self.count = sizes[digit]
        self.below = math.prod(sizes[digit + 1 :])
        self.total = math.prod(sizes)
        self.members = members

    def send(self, value, offset):
        count, below = self.count, self.below
        pairs = []
        for i in range(self.total):
            if self.members is not None and not self.members(i):
                continue
            at = (i // below) % count
            pairs.append((i, i + ((at + offset) % count - at) * below))
        return lax.ppermute(value, self.axes, pairs)

    def place(self, linear):
        return (linear // self.below) % self.count


def cut(value, index, size, axis):
    return lax.dynamic_slice_in_dim(value, index * size, size, axis)


def tile_pairs(tiles):
    return [(i, j) for i in range(tiles) for j in range(i, tiles)]


def pick(options, index):
    chosen = jnp.int32(options[0])
    for k in range(1, len(options)):
        chosen = jnp.where(index == k, jnp.int32(options[k]), chosen)
    return chosen


def sum_kernel(
    inner,
    tile,
    down_ref,
    up_ref,
    qkvo_ref,
    small_ref,
    input_ref,
    mid_ref,
    result_ref,
    mom_qkv_ref,
    mom_out_ref,
    mom_up_ref,
    mom_down_ref,
    down_sum_ref,
    up_sum_ref,
    qkvo_sum_ref,
    small_sum_ref,
    square_ref,
    tiles_ref,
    given_ref,
    got_down,
    got_up,
    got_low,
    got_high,
    small_got,
    mom_up,
    mom_down,
    mom_column,
    mom_row,
    up_low,
    down_low,
    part,
    core_got,
    chip_sum,
    x_got,
    ring_sems,
    late_sems,
    small_sems,
    load_sem,
    core_sems,
    x_sems,
    back_sems,
    square_x_sems,
    square_core_sems,
    input_core,
    input_x,
    input_out,
    input_own,
    stage,
    back,
    input_core_sems,
    input_x_sems,
    stage_sems,
    given_sems,
):
    mesh_type = pl.DeviceIdType.MESH
    count = lax.axis_size("dp")
    index = lax.axis_index("dp")
    team = lax.axis_index("tensor")
    wides = lax.axis_size("tensor") // 2
    x_at, core = team // 2, team % 2
    outer = count // inner
    if inner == 2:
        place = jnp.where(index % 2 == 0, index // 2, count - 1 - index // 2)

        def device(p):
            return jnp.where(p < outer, 2 * p, 2 * (count - 1 - p) + 1)
    else:
        place = index

        def device(p):
            return p

    ring_next = ((device((place + 1) % count), team), (device((place + count - 1) % count), team))
    core_next = (index, x_at * 2 + 1 - core)
    x_up = (index, ((x_at + 1) % wides) * 2 + core)
    x_down = (index, ((x_at + wides - 1) % wides) * 2 + core)

    barrier = pltpu.get_barrier_semaphore()

    def greet(hop, carry):
        pl.semaphore_signal(
            barrier, inc=1, device_id=((index + hop) % count, team), device_id_type=mesh_type
        )
        return carry

    lax.fori_loop(1, count, greet, 0)
    for hop in range(1, 2 * wides):
        pl.semaphore_signal(
            barrier,
            inc=1,
            device_id=(index, (team + hop) % (2 * wides)),
            device_id_type=mesh_type,
        )
    pl.semaphore_wait(barrier, count - 1 + 2 * wides - 1)

    def remote(src, dst, sems, at, target):
        return pltpu.make_async_remote_copy(
            src_ref=src,
            dst_ref=dst,
            send_sem=sems.at[(0, *at)],
            recv_sem=sems.at[(1, *at)],
            device_id=target,
            device_id_type=mesh_type,
        )

    sent = []

    def ring(lanes, sems):
        streams = []
        for d, (x_ref, o_ref, first, length, got) in enumerate(lanes):
            chunk = length // count
            halves = 2 if chunk % 32 == 0 else 1
            sub = chunk // halves
            for h in range(halves):
                streams.append((d, h, x_ref, o_ref, first, chunk, sub, got))
        streams.sort(key=lambda one: one[1])

        def rows(stream, hop):
            d, h, _, _, first, chunk, sub, _ = stream
            at = (place + count - hop) % count if d == 0 else (place + hop) % count
            return pl.ds(pl.multiple_of(first + at * chunk + h * sub, 16), sub)

        def copy(stream, step):
            d, h, x_ref, o_ref, _, _, sub, got = stream
            if step < count - 1:
                slot = pl.ds(h * sub, sub)
                src = x_ref.at[rows(stream, 1)] if step == 0 else got.at[step - 1, slot]
                dst = got.at[step, slot]
            else:
                src = dst = o_ref.at[rows(stream, step - (count - 1))]
            return remote(src, dst, sems, (step, d, h), ring_next[d])

        for stream in streams:
            copy(stream, 0).start()
        yield 0
        for step in range(2 * (count - 1)):
            for stream in streams:
                _, h, x_ref, o_ref, _, _, sub, got = stream
                one = copy(stream, step)
                one.wait_recv()
                sent.append(one)
                if step < count - 1:
                    slot = pl.ds(h * sub, sub)
                    total = wide(got[step, slot]) + wide(x_ref[rows(stream, step + 2)])
                    if step < count - 2:
                        got[step, slot] = short(total)
                    else:
                        o_ref[rows(stream, 0)] = short(total)
                if step < 2 * count - 3:
                    copy(stream, step + 1).start()
                yield step

    half = qkvo_ref.shape[0] // 2
    first_ring = ring(
        [
            (down_ref, down_sum_ref, 0, down_ref.shape[0], got_down),
            (up_ref, up_sum_ref, 0, up_ref.shape[0], got_up),
        ],
        ring_sems,
    )
    second_ring = ring(
        [(qkvo_ref, qkvo_sum_ref, 0, half, got_low), (qkvo_ref, qkvo_sum_ref, half, half, got_high)],
        late_sems,
    )

    teams = 2 * wides
    peers = count // teams

    def input_tasks():

        def over_core(i):
            return remote(input_ref.at[wides + i], input_core.at[i], input_core_sems, (i,), core_next)

        def over_x(hop):
            return remote(input_out.at[hop], input_x.at[hop], input_x_sems, (hop,), x_up)

        def over_teams(hop):
            target = (team + hop) % teams
            mine = back.at[pl.ds(team * peers, peers)]
            return remote(stage.at[hop], mine, stage_sems, (hop,), (index, target))

        for i in range(wides - 1, -1, -1):
            over_core(i).start()
        for _ in range(5):
            yield
        for hop in range(wides):
            i = wides - 1 - hop
            over_core(i).wait_recv()
            total = wide(input_ref[i]) + wide(input_core[i])
            if hop > 0:
                over_x(hop - 1).wait_recv()
                total = total + wide(input_x[hop - 1])
            if i > 0:
                input_out[hop] = short(total)
                over_x(hop).start()
                for _ in range(8):
                    yield
            else:
                input_own[...] = short(total + mid_ref[...])
        yield
        part_width = result_ref.shape[2] // teams
        for hop in range(teams):
            columns = pl.ds(pl.multiple_of((team + hop) % teams * part_width, 128), part_width)
            for k, rows_ref in enumerate((result_ref, input_own)):
                stage[hop, :, :, k * part_width : (k + 1) * part_width] = rows_ref[:, :, columns]
            if hop > 0:
                over_teams(hop).start()
            else:
                back[pl.ds(team * peers, peers)] = stage[0]
            yield
        for _ in range(8):
            yield
        for i in range(wides):
            over_core(i).wait_send()
        for hop in range(wides - 1):
            over_x(hop).wait_send()
        for hop in range(1, teams):
            over_teams(hop).wait_recv()
            over_teams(hop).wait_send()

    def give(hop):
        target = (index + hop) % count
        return remote(back.at[target], given_ref.at[index], given_sems, (hop,), (target, team))

    def give_start(hop, carry):
        give(hop).start()
        return carry

    def give_wait(hop, carry):
        give(hop).wait_recv()
        give(hop).wait_send()
        return carry

    is_up, is_down = index == 4, index == 5
    is_gram = jnp.logical_or(is_up, is_down)
    size = up_ref.shape[0]
    pairs = tile_pairs(size // tile)
    share = len(pairs) // 2
    load_up = pltpu.make_async_copy(mom_up_ref, mom_up, load_sem.at[0])
    load_down = pltpu.make_async_copy(mom_down_ref, mom_down, load_sem.at[0])

    def gram_tasks():
        for ref, mom, total, low, load, mine in (
            (mom_up_ref, mom_up, up_sum_ref, up_low, load_up, is_up),
            (mom_down_ref, mom_down, down_sum_ref, down_low, load_down, is_down),
        ):

            @pl.when(mine)
            def _():
                load.wait()

            for start in range(0, ref.shape[0], 256):

                @pl.when(mine)
                def _():
                    rows = pl.ds(start, 256)
                    low[rows, :] = short(momentum_decay * mom[rows, :] + wide(total[rows, :]))

            yield

        def compute(k):
            row = pl.ds(pl.multiple_of(pick([p[0] for p in pairs], k) * tile, tile), tile)
            column = pl.ds(pl.multiple_of(pick([p[1] for p in pairs], k) * tile, tile), tile)

            @pl.when(is_up)
            def _():
                part[k] = mm_nt(up_low[row, :], up_low[column, :])

            @pl.when(is_down)
            def _():
                part[k] = mm_tn(down_low[:, row], down_low[:, column])

        def to_core(i):
            return remote(part.at[(1 - core) * share + i], core_got.at[i], core_sems, (i,), core_next)

        def to_x(i, hop):
            src = chip_sum.at[i] if hop == 0 else x_got.at[hop - 1, i]
            return remote(src, x_got.at[hop, i], x_sems, (hop, i), x_up)

        def to_back(i):
            at = tiles_ref.at[core * share + i]
            return remote(at, at, back_sems, (i,), core_next)

        for i in range(share):
            compute((1 - core) * share + i)

            @pl.when(is_gram)
            def _():
                to_core(i).start()

            yield
        for i in range(share):
            compute(core * share + i)
            yield
        for i in range(share):

            @pl.when(is_gram)
            def _():
                to_core(i).wait_recv()
                chip_sum[i] = part[core * share + i] + core_got[i]
                to_x(i, 0).start()

            yield
        for _ in range(12):
            yield
        for hop in range(wides - 1):
            for i in range(share):

                @pl.when(is_gram)
                def _():
                    to_x(i, hop).wait_recv()
                    before = chip_sum[i] if hop == 0 else tiles_ref[core * share + i]
                    tiles_ref[core * share + i] = before + x_got[hop, i]
                    if hop < wides - 2:
                        to_x(i, hop + 1).start()
                    else:
                        to_back(i).start()

                for _ in range(2):
                    yield

        @pl.when(is_gram)
        def _():
            for i in range(share):
                to_back(i).wait_recv()
                to_core(i).wait_send()
                to_back(i).wait_send()
                for hop in range(wides - 1):
                    to_x(i, hop).wait_send()

    def small_copy(hop):
        return remote(
            small_ref, small_got.at[hop], small_sems, (hop,), ((index + hop) % count, team)
        )

    def small_send(hop, carry):
        small_copy(hop).start()
        return carry

    def small_wait(hop, total):
        one = small_copy(hop)
        one.wait_send()
        one.wait_recv()
        return total + wide(small_got[hop])

    is_column, is_row = index < 3, index == 3
    is_square = index < 4
    width = square_ref.shape[2]
    load_column = pltpu.make_async_copy(
        mom_qkv_ref.at[jnp.minimum(index, 2)], mom_column, load_sem.at[0]
    )
    load_row = pltpu.make_async_copy(mom_out_ref, mom_row, load_sem.at[0])
    square_rows = square_ref.shape[1]
    block = 256
    blocks = square_rows // block

    def square_x(hop, b):
        rows = pl.ds(b * block, block)
        return remote(
            square_ref.at[hop, rows], square_ref.at[hop + 1, rows], square_x_sems, (hop, b), x_down
        )

    def square_core(hop, b):
        rows = pl.ds(b * block, block)
        return remote(
            square_ref.at[hop, rows], square_ref.at[wides + hop, rows], square_core_sems, (hop, b), core_next
        )

    def square_work():
        columns = pl.ds(pl.multiple_of(jnp.minimum(index, 3) * width, 128), width)
        for b in range(blocks):
            rows = pl.ds(b * block, block)
            fresh = wide(qkvo_sum_ref[rows, columns])

            @pl.when(is_column)
            def _():
                if b == 0:
                    load_column.wait()
                square_ref[0, rows] = short(momentum_decay * mom_column[rows, :] + fresh)

            @pl.when(is_row)
            def _():
                if b == 0:
                    load_row.wait()
                square_ref[0, rows] = short(momentum_decay * mom_row[:, rows].T + fresh)

            square_x(0, b).start()
            square_core(0, b).start()
        for hop in range(1, wides):
            for b in range(blocks):
                square_x(hop - 1, b).wait_recv()
                if hop < wides - 1:
                    square_x(hop, b).start()
                square_core(hop, b).start()
        for hop in range(wides):
            for b in range(blocks):
                square_core(hop, b).wait_recv()
        for hop in range(wides):
            for b in range(blocks):
                square_core(hop, b).wait_send()
                if hop < wides - 1:
                    square_x(hop, b).wait_send()

    next(first_ring)
    lax.fori_loop(1, count, small_send, 0)
    for one, mine in (
        (load_up, is_up),
        (load_down, is_down),
        (load_column, is_column),
        (load_row, is_row),
    ):

        @pl.when(mine)
        def _():
            one.start()

    beside = input_tasks()
    for step in first_ring:
        next(beside, None)
        if step >= 2 * count - 6:
            next(second_ring, None)
    for _ in beside:
        pass
    side = gram_tasks()
    for _ in second_ring:
        next(side, None)
    lax.fori_loop(1, count, give_start, 0)
    given_ref[index] = back[index]
    pl.when(is_square)(square_work)
    for _ in side:
        pass
    lax.fori_loop(1, count, give_wait, 0)
    small_sum_ref[...] = lax.fori_loop(1, count, small_wait, wide(small_ref[...]))
    for one in sent:
        one.wait_send()


def sums_over_dp(inner, down, up, qkvo, small, input_part, grad_mid, result, moments_old):
    groups, teams = lax.axis_size("dp"), lax.axis_size("tensor")
    wides = teams // 2
    size, width = qkvo.shape[0], qkvo.shape[1] // 4
    tile = size // 4
    pairs = len(tile_pairs(4))
    steps = 2 * (groups - 1)
    mom_qkv, mom_out, mom_up, mom_down = moments_old
    dma = pltpu.SemaphoreType.DMA
    vmem = pl.BlockSpec(memory_space=pltpu.VMEM)
    length = down.size + up.size + qkvo.size
    peers, rows, model = result.shape
    return pl.pallas_call(
        functools.partial(sum_kernel, inner, tile),
        name="sums_over_dp",
        out_shape=(
            jax.ShapeDtypeStruct(down.shape, bf16),
            jax.ShapeDtypeStruct(up.shape, bf16),
            jax.ShapeDtypeStruct(qkvo.shape, bf16),
            jax.ShapeDtypeStruct(small.shape, f32),
            jax.ShapeDtypeStruct((teams, size, width), bf16),
            jax.ShapeDtypeStruct((pairs, tile, tile), f32),
            jax.ShapeDtypeStruct((groups, rows, 2 * (model // teams)), bf16),
        ),
        in_specs=[vmem] * 7 + [pl.BlockSpec(memory_space=pl.ANY)] * 4,
        out_specs=[vmem] * 7,
        scratch_shapes=[
            pltpu.VMEM((groups - 1, down.shape[0] // groups, down.shape[1]), bf16),
            pltpu.VMEM((groups - 1, up.shape[0] // groups, up.shape[1]), bf16),
            pltpu.VMEM((groups - 1, size // 2 // groups, qkvo.shape[1]), bf16),
            pltpu.VMEM((groups - 1, size // 2 // groups, qkvo.shape[1]), bf16),
            pltpu.VMEM((groups, *small.shape), bf16),
            pltpu.VMEM(up.shape, f32),
            pltpu.VMEM(down.shape, f32),
            pltpu.VMEM((size, width), f32),
            pltpu.VMEM((width, size), f32),
            pltpu.VMEM(up.shape, bf16),
            pltpu.VMEM(down.shape, bf16),
            pltpu.VMEM((pairs, tile, tile), f32),
            pltpu.VMEM((pairs // 2, tile, tile), f32),
            pltpu.VMEM((pairs // 2, tile, tile), f32),
            pltpu.VMEM((wides - 1, pairs // 2, tile, tile), f32),
            dma((2, steps, 2, 2)),
            dma((2, steps, 2, 2)),
            dma((2, groups)),
            dma((1,)),
            dma((2, pairs // 2)),
            dma((2, wides - 1, pairs // 2)),
            dma((2, pairs // 2)),
            dma((2, wides - 1, size // 256)),
            dma((2, wides, size // 256)),
            pltpu.VMEM((wides, peers, rows, model), bf16),
            pltpu.VMEM((wides - 1, peers, rows, model), bf16),
            pltpu.VMEM((wides - 1, peers, rows, model), bf16),
            pltpu.VMEM((peers, rows, model), bf16),
            pltpu.VMEM((teams, peers, rows, 2 * (model // teams)), bf16),
            pltpu.VMEM((groups, rows, 2 * (model // teams)), bf16),
            dma((2, wides)),
            dma((2, wides - 1)),
            dma((2, teams)),
            dma((2, groups)),
        ],
        compiler_params=pltpu.CompilerParams(
            collective_id=0, has_side_effects=True, vmem_limit_bytes=52 * 2**20
        ),
        cost_estimate=pl.CostEstimate(
            flops=length, bytes_accessed=4 * length, transcendentals=0
        ),
    )(
        down, up, qkvo, small, input_part, grad_mid, result, mom_qkv, mom_out, mom_up, mom_down
    )


def dot(left, right):
    return jnp.dot(left, right, preferred_element_type=f32)

def dot_nt(left, right):
    return lax.dot_general(left, right, (((1,), (1,)), ((), ())), preferred_element_type=f32)

def middle_kernel(
    context_ref,
    x_ref,
    out_ref,
    up_ref,
    down_ref,
    bias_ref,
    vectors_ref,
    upstream_ref,
    valid_ref,
    hidden_ref,
    act_ref,
    grad_z_ref,
    grad_pre_ref,
    grad_mid_ref,
    own_grad_mid_ref,
    result_ref,
    vector_sum_ref,
    grad_down_ref,
    grad_up_ref,
    slope,
    held,
    core_out,
    core_got,
    x_out,
    x_got,
    normed_one,
    own_hidden,
    normed_two,
    own_grad_z,
    vector_own,
    vector_got,
    core_sems,
    x_sems,
    spread_x_sems,
    spread_core_sems,
    vector_sems,
):
    mesh_type = pl.DeviceIdType.MESH
    index = lax.axis_index("dp")
    team = lax.axis_index("tensor")
    teams = lax.axis_size("tensor")
    wides = teams // 2
    x_at, core = team // 2, team % 2
    core_next = (index, x_at * 2 + 1 - core)
    x_up = (index, ((x_at + 1) % wides) * 2 + core)
    x_down = (index, ((x_at + wides - 1) % wides) * 2 + core)
    barrier = pltpu.get_barrier_semaphore()
    for hop in range(1, teams):
        pl.semaphore_signal(
            barrier, inc=1, device_id=(index, (team + hop) % teams), device_id_type=mesh_type
        )
    pl.semaphore_wait(barrier, teams - 1)
    sent = []

    def remote(src, dst, sems, at, target):
        return pltpu.make_async_remote_copy(
            src_ref=src,
            dst_ref=dst,
            send_sem=sems.at[(0, *at)],
            recv_sem=sems.at[(1, *at)],
            device_id=target,
            device_id_type=mesh_type,
        )

    def start(one):
        one.start()
        sent.append(one)

    def over_core(s, i):
        return remote(core_out.at[s, i], core_got.at[s, i], core_sems, (s, i), core_next)

    def over_x(s, hop):
        return remote(x_out.at[s, hop], x_got.at[s, hop], x_sems, (s, hop), x_up)

    def finish(s, filler):
        for hop in range(wides):
            i = wides - 1 - hop
            over_core(s, i).wait_recv()
            total = held[i] + wide(core_got[s, i])
            if hop > 0:
                if filler is not None:
                    filler()
                    filler = None
                over_x(s, hop - 1).wait_recv()
                total = total + wide(x_got[s, hop - 1])
            if i > 0:
                x_out[s, hop] = short(total)
                start(over_x(s, hop))
        return total

    def along_x(s, ref, i):
        return remote(ref.at[i], ref.at[i + 1], spread_x_sems, (s, i), x_down)

    def across(s, ref, i):
        return remote(ref.at[i], ref.at[wides + i], spread_core_sems, (s, i), core_next)

    def spread(s, ref):
        start(along_x(s, ref, 0))
        start(across(s, ref, 0))

    def arrive(s, ref, i):
        if i > 0:
            along_x(s, ref, i - 1).wait_recv()
            start(across(s, ref, i))
            if i < wides - 1:
                start(along_x(s, ref, i))
        across(s, ref, i).wait_recv()

    share = x_ref.shape[0]

    def pair(ref, i):
        return jnp.concatenate([ref[i], ref[wides + i]], 0)

    def put_pair(ref, i, value):
        ref[i] = value[:share]
        ref[wides + i] = value[share:]

    def keep(s, i, partial):
        core_out[s, i] = short(partial[share:])
        start(over_core(s, i))
        held[i] = partial[:share]

    def sums(value):
        return jnp.sum(value, axis=0, keepdims=True)

    for i in range(wides - 1, -1, -1):
        keep(0, i, dot(pair(context_ref, i), out_ref[...]))
    mid = wide(x_ref[...]) + finish(0, None) + vectors_ref[0:1, :]
    normed, inverse_one, hidden = norm_forward(mid, vectors_ref[1:2, :], vectors_ref[2:3, :])
    normed_one[...] = normed
    own_hidden[...] = hidden
    hidden_ref[0] = short(hidden)
    spread(0, hidden_ref)

    units = up_ref.shape[1]
    step = min(units, 512)
    for i in range(wides):
        arrive(0, hidden_ref, i)
        rows = pair(hidden_ref, i)
        for c in range(0, units, step):
            at = slice(c, c + step)
            pre = dot(rows, up_ref[:, at]) + bias_ref[:, at]
            phi = 0.5 + 0.5 * lax.erf(pre * math.sqrt(0.5))
            act = short(pre * phi)
            bend = phi + pre * jnp.exp(-0.5 * pre * pre) * (1.0 / math.sqrt(2.0 * math.pi))
            for r, part in ((i, slice(0, share)), (wides + i, slice(share, 2 * share))):
                act_ref[r, :, at] = act[part]
                slope[r, :, at] = bend[part]
        keep(1, i, dot(pair(act_ref, i), down_ref[...]))
    summed = own_hidden[...] + finish(1, None) + vectors_ref[3:4, :]
    gain_two = vectors_ref[4:5, :]
    normed, inverse_two, result = norm_forward(summed, gain_two, vectors_ref[5:6, :])
    result_ref[...] = short(result)
    upstream = wide(upstream_ref[...]) * valid_ref[...]
    grad_z = norm_backward(upstream, normed, inverse_two, gain_two)
    own_grad_z[...] = grad_z
    grad_z_ref[0] = short(grad_z)
    spread(1, grad_z_ref)
    vector_own[...] = jnp.zeros_like(vector_own)
    vector_own[3:4, :] = sums(grad_z)
    vector_own[4:5, :] = sums(upstream * normed)
    vector_own[5:6, :] = sums(upstream)

    for i in range(wides):
        arrive(1, grad_z_ref, i)
        rows = pair(grad_z_ref, i)
        for c in range(0, units, step):
            at = slice(c, c + step)
            grad = dot_nt(rows, down_ref[at, :])
            for r, part in ((i, slice(0, share)), (wides + i, slice(share, 2 * share))):
                grad_pre_ref[r, :, at] = short(grad[part] * slope[r, :, at])
        keep(2, i, dot_nt(pair(grad_pre_ref, i), up_ref[...]))

    def every(ref, at):
        return jnp.concatenate([ref[r, :, at] for r in range(teams)], 0)

    def down_filler():
        def one(k, carry):
            at = pl.ds(pl.multiple_of(k * 128, 128), 128)
            grad_down_ref[at, :] = short(mm_tn(every(act_ref, at), every(grad_z_ref, slice(None))))
            return carry

        lax.fori_loop(0, units // 128, one, 0)

    grad_hidden = own_grad_z[...] + finish(2, down_filler)
    grad_mid = norm_backward(grad_hidden, normed_one[...], inverse_one, vectors_ref[1:2, :])
    own_grad_mid_ref[...] = grad_mid
    grad_mid_ref[0] = short(grad_mid)
    spread(2, grad_mid_ref)
    vector_own[0:1, :] = sums(grad_mid)
    vector_own[1:2, :] = sums(grad_hidden * normed_one[...])
    vector_own[2:3, :] = sums(grad_hidden)

    def to_team(hop):
        return remote(
            vector_own, vector_got.at[hop], vector_sems, (hop,), (index, (team + hop) % teams)
        )

    for hop in range(1, teams):
        start(to_team(hop))

    def up_filler(k, carry):
        at = pl.ds(pl.multiple_of(k * 128, 128), 128)
        grad_up_ref[at, :] = short(mm_tn(every(hidden_ref, at), every(grad_pre_ref, slice(None))))
        return carry

    lax.fori_loop(0, hidden_ref.shape[2] // 128, up_filler, 0)
    for i in range(wides):
        arrive(2, grad_mid_ref, i)
    total = vector_own[...]
    for hop in range(1, teams):
        to_team(hop).wait_recv()
        total = total + vector_got[hop]
    vector_sum_ref[...] = total
    for one in sent:
        one.wait_send()


def middle(context, x_own, w_out, w_up, w_down, bias_up, vectors, upstream, valid):
    teams, share, width = context.shape
    model, units = w_up.shape
    wides = teams // 2
    dma = pltpu.SemaphoreType.DMA
    vmem = pl.BlockSpec(memory_space=pltpu.VMEM)
    rows = jax.ShapeDtypeStruct((teams, share, model), bf16)
    inner = jax.ShapeDtypeStruct((teams, share, units), bf16)
    own = pltpu.VMEM((share, model), f32)
    return pl.pallas_call(
        middle_kernel,
        name="middle",
        out_shape=(
            rows,
            inner,
            rows,
            inner,
            rows,
            jax.ShapeDtypeStruct((share, model), f32),
            jax.ShapeDtypeStruct((share, model), bf16),
            jax.ShapeDtypeStruct((8, model), f32),
            jax.ShapeDtypeStruct((units, model), bf16),
            jax.ShapeDtypeStruct((model, units), bf16),
        ),
        in_specs=[vmem] * 9,
        out_specs=[vmem] * 10,
        scratch_shapes=[
            pltpu.VMEM((teams, share, units), f32),
            pltpu.VMEM((wides, share, model), f32),
            pltpu.VMEM((3, wides, share, model), bf16),
            pltpu.VMEM((3, wides, share, model), bf16),
            pltpu.VMEM((3, wides - 1, share, model), bf16),
            pltpu.VMEM((3, wides - 1, share, model), bf16),
            own,
            own,
            own,
            own,
            pltpu.VMEM((8, model), f32),
            pltpu.VMEM((teams, 8, model), f32),
            dma((2, 3, wides)),
            dma((2, 3, wides - 1)),
            dma((2, 3, wides - 1)),
            dma((2, 3, wides)),
            dma((2, teams)),
        ],
        compiler_params=pltpu.CompilerParams(
            collective_id=1, has_side_effects=True, vmem_limit_bytes=48 * 2**20
        ),
        cost_estimate=pl.CostEstimate(
            flops=12 * teams * share * model * units,
            bytes_accessed=8 * model * units,
            transcendentals=0,
        ),
    )(context, x_own, w_out, w_up, w_down, bias_up.reshape(1, units), vectors, upstream, valid)


def polar_kernel(block, m_ref, o_ref, x_ref, gram_ref, low_ref, mix_ref):
    teams, size, width = m_ref.shape
    keep = o_ref.shape[1]
    bits = 256

    def rows(i):
        return pl.ds(pl.multiple_of(i * bits, bits), bits)

    def columns(j):
        return pl.ds(pl.multiple_of(j * block, block), block)

    def norm_step(i, total):
        for r in range(teams):
            part = wide(m_ref[r, rows(i), :])
            total = total + jnp.sum(part * part, axis=0, keepdims=True)
        return total

    total = lax.fori_loop(0, size // bits, norm_step, jnp.zeros((1, width), f32))
    scale = lax.rsqrt(jnp.sum(total, axis=1, keepdims=True) + 1e-07)

    def scale_step(i, carry):
        for r in range(teams):
            x_ref[0, rows(i), r * width : (r + 1) * width] = short(wide(m_ref[r, rows(i), :]) * scale)
        return carry

    lax.fori_loop(0, size // bits, scale_step, 0)

    def sweep(k, carry):
        now = k % 2
        x = x_ref.at[now]

        def gram_step(j, carry):
            gram = dot_nt(x[...], x[columns(j), :])
            gram_ref[:, columns(j)] = gram
            low_ref[:, columns(j)] = short(gram)
            return carry

        def mix_step(j, carry):
            power = dot(low_ref[...], low_ref[:, columns(j)])
            mix_ref[:, columns(j)] = short(coef_two * gram_ref[:, columns(j)] + coef_three * power)
            return carry

        def next_step(j, carry):
            mixed = dot(mix_ref[...], x[:, columns(j)])
            x_ref[1 - now, :, columns(j)] = short(coef_one * wide(x[:, columns(j)]) + mixed)
            return carry

        lax.fori_loop(0, size // block, gram_step, 0)
        lax.fori_loop(0, size // block, mix_step, 0)
        lax.fori_loop(0, jnp.where(k < 4, size // block, -(-keep // block)), next_step, 0)
        return carry

    lax.fori_loop(0, 5, sweep, 0)
    o_ref[...] = x_ref[1, :, :keep]


def factor_kernel(block, g_ref, o_ref, current_ref, poly_ref, half_ref, factor_ref):
    size = poly_ref.shape[0]
    tile = g_ref.shape[1]
    tiles = size // tile
    keep = o_ref.shape[1]
    first = lax.axis_index("tensor") * keep
    eye = lax.broadcasted_iota(jnp.int32, (tile, tile), 0) == lax.broadcasted_iota(
        jnp.int32, (tile, tile), 1
    )
    trace = jnp.zeros((1, 1), f32)
    for k, (i, j) in enumerate(tile_pairs(tiles)):
        if i == j:
            diagonal = jnp.where(eye, g_ref[k], 0.0)
            trace = trace + jnp.sum(jnp.sum(diagonal, axis=0, keepdims=True), axis=1, keepdims=True)
    scale = lax.rsqrt(trace + 1e-07)
    scale_two = scale * scale

    def store(slot, rows, columns, value):
        high = short(value)
        current_ref[slot, 0, rows, columns] = high
        current_ref[slot, 1, rows, columns] = short(value - wide(high))

    def span(i):
        return slice(i * tile, (i + 1) * tile)

    for k, (i, j) in enumerate(tile_pairs(tiles)):
        part = g_ref[k] * scale_two
        store(0, span(i), span(j), part)
        if i != j:
            store(0, span(j), span(i), part.T)

    def cols(j):
        return pl.ds(pl.multiple_of(j * block, block), block)

    def sweep(k, exact, exact_next, last):
        now = k % 2
        high_ref, low_ref = current_ref.at[now, 0], current_ref.at[now, 1]

        def poly_step(j, carry):
            power = dot(high_ref[...], high_ref[:, cols(j)])
            if last:
                power = power + dot(high_ref[...], low_ref[:, cols(j)])
            r = lax.broadcasted_iota(jnp.int32, (size, block), 0)
            c = lax.broadcasted_iota(jnp.int32, (size, block), 1) + j * block
            present = wide(high_ref[:, cols(j)]) + wide(low_ref[:, cols(j)])
            poly = coef_two * present + coef_three * power
            poly_ref[:, cols(j)] = short(poly + jnp.where(r == c, coef_one, 0.0))
            return carry

        def half_step(j, carry):
            half = dot(poly_ref[...], high_ref[:, cols(j)])
            if exact:
                half = half + dot(poly_ref[...], low_ref[:, cols(j)])
            high = short(half)
            half_ref[0, :, cols(j)] = high
            if exact_next:
                half_ref[1, :, cols(j)] = short(half - wide(high))
            return carry

        def next_step(j, carry):
            new = dot(half_ref[0], poly_ref[:, cols(j)])
            if exact_next:
                new = new + dot(half_ref[1], poly_ref[:, cols(j)])
            store(1 - now, slice(None), cols(j), new)
            return carry

        lax.fori_loop(0, size // block, poly_step, 0)
        if not last:
            lax.fori_loop(0, size // block, half_step, 0)
            lax.fori_loop(0, size // block, next_step, 0)

    def plain_sweep(k, carry):
        sweep(k, False, False, False)
        factor_ref[...] = short(dot(poly_ref[...], factor_ref[...]))
        return carry

    sweep(0, True, True, False)
    factor_ref[...] = poly_ref[:, pl.ds(pl.multiple_of(first, 128), keep)]
    sweep(1, True, False, False)
    factor_ref[...] = short(dot(poly_ref[...], factor_ref[...]))
    lax.fori_loop(2, 4, plain_sweep, 0)
    sweep(4, False, False, True)
    o_ref[...] = short(dot(poly_ref[...], factor_ref[...]) * scale)


def step_kernel(
    block,
    square_ref,
    tiles_ref,
    o_ref,
    x_ref,
    gram_ref,
    low_ref,
    mix_ref,
    current_ref,
    poly_ref,
    half_ref,
    factor_ref,
):
    index = lax.axis_index("dp")

    @pl.when(index < 4)
    def _():
        polar_kernel(block, square_ref, o_ref, x_ref, gram_ref, low_ref, mix_ref)

    @pl.when(jnp.logical_or(index == 4, index == 5))
    def _():
        factor_kernel(block, tiles_ref, o_ref, current_ref, poly_ref, half_ref, factor_ref)

    @pl.when(index > 5)
    def _():
        o_ref[...] = jnp.zeros_like(o_ref)


def orthogonal_columns(square, tiles):
    teams, size, width = square.shape
    vmem = pl.BlockSpec(memory_space=pltpu.VMEM)
    return pl.pallas_call(
        functools.partial(step_kernel, 512),
        name="orthogonal_columns",
        out_shape=jax.ShapeDtypeStruct((size, width), bf16),
        in_specs=[vmem] * 2,
        out_specs=vmem,
        scratch_shapes=[
            pltpu.VMEM((2, size, teams * width), bf16),
            pltpu.VMEM((size, size), f32),
            pltpu.VMEM((size, size), bf16),
            pltpu.VMEM((size, size), bf16),
            pltpu.VMEM((2, 2, size, size), bf16),
            pltpu.VMEM((size, size), bf16),
            pltpu.VMEM((2, size, size), bf16),
            pltpu.VMEM((size, width), bf16),
        ],
        compiler_params=pltpu.CompilerParams(vmem_limit_bytes=48 * 2**20),
        cost_estimate=pl.CostEstimate(
            flops=40 * size**3, bytes_accessed=8 * size * size, transcendentals=0
        ),
    )(square, tiles)


def body(
    layout,
    tokens,
    cotangent,
    lengths,
    packing,
    w_qkv,
    w_out,
    w_up,
    w_down,
    bias_qv,
    bias_up,
    vectors,
    mom_qkv,
    mom_out,
    mom_up,
    mom_down,
    mom_bias_qv,
    mom_bias_up,
    mom_vectors,
):
    inner, cores = layout
    groups = lax.axis_size("dp")
    teams = lax.axis_size("tensor")
    group = lax.axis_index("dp")
    team = lax.axis_index("tensor")
    outer, wides = groups // inner, teams // cores
    count = tokens.shape[0]
    per_peer = count // groups
    share = count // teams
    width = D // teams
    all_tokens = count * groups

    outer_ring = Ring("dp", (outer, inner), 0)
    inner_ring = Ring("dp", (outer, inner), 1)
    outer_at, inner_at = outer_ring.place(group), inner_ring.place(group)
    x_ring = Ring("tensor", (wides, cores), 0)
    core_ring = Ring("tensor", (wides, cores), 1)
    x_at, core_at = x_ring.place(team), core_ring.place(team)

    def team_of(rank):
        return ((x_at + rank % wides) % wides) * cores + (core_at + rank // wides) % cores

    def to_relative(value, size, axis=0):
        return jnp.concatenate([cut(value, team_of(r), size, axis) for r in range(teams)], axis)

    def to_given(value, size, axis=0):
        parts = []
        for other in range(teams):
            rank = ((other % cores - core_at) % cores) * wides + (other // cores - x_at) % wides
            parts.append(cut(value, rank, size, axis))
        return jnp.concatenate(parts, axis)

    def spread_list(piece, ring_x=x_ring, ring_core=core_ring):
        line = [piece]
        for _ in range(wides - 1):
            line.append(ring_x.send(line[-1], -1))
        pieces = list(line)
        for hop in range(1, cores):
            pieces += [ring_core.send(p, -hop) for p in line]
        return pieces

    def spread_columns(piece):
        return to_given(jnp.concatenate(spread_list(piece), 1), piece.shape[1], 1)

    def own_rows(value):
        return cut(value, team, share, 0)

    position = jnp.arange(count, dtype=jnp.int32)
    peer = jnp.arange(groups, dtype=jnp.int32)
    packed = packing.reshape(groups, count)
    source = packed // count
    source_mine = lax.dynamic_index_in_dim(source, group, 0, keepdims=False)
    masks = jnp.concatenate([source == group, source_mine[None, :] == peer[:, None]], 0)
    before = (position[:, None] < position[None, :]).astype(bf16)
    rank = mm(masks.astype(bf16), before).astype(jnp.int32)
    key = jnp.where(masks, rank, -1)
    value = jnp.concatenate(
        [packed % count, jnp.broadcast_to(position[None, :], (groups, count))], 0
    )
    slot_in_message = jnp.arange(per_peer, dtype=jnp.int32)
    picked = jnp.sum(
        jnp.where(key[:, None, :] == slot_in_message[None, :, None], value[:, None, :], 0), axis=-1
    )
    rows_sent = picked[:groups].reshape(count)
    slots = picked[groups:].reshape(count)
    choose = (rows_sent[:, None] == position[None, :]).astype(bf16)

    length_row = lengths[0]
    end_one = length_row[0]
    end_two = end_one + length_row[1]
    end_all = end_two + length_row[2]
    segments = (
        (slots >= end_one).astype(jnp.int32)
        + (slots >= end_two).astype(jnp.int32)
        + (slots >= end_all).astype(jnp.int32)
        + jnp.maximum(slots - end_all, 0)
    )
    valid_own = own_rows((slots < end_all).astype(f32))
    segments = to_relative(segments, share)

    own_columns = jnp.concatenate([cut(tokens, team, width, 1), cut(cotangent, team, width, 1)], 1)
    sent = short(mm(choose, own_columns)).reshape(groups, per_peer, 2 * width)
    got = lax.all_to_all(sent, "dp", split_axis=0, concat_axis=0, tiled=True)
    got = got.reshape(count, 2 * width)

    packed_x = to_relative(spread_columns(got[:, :width]), share)
    turns = []
    for hop in range(teams):
        block = cut(got[:, width:], (team + hop) % teams, share, 0)
        if hop > 0:
            block = lax.ppermute(block, "tensor", [(i, (i + hop) % teams) for i in range(teams)])
        turns.append(block)
    turns = jnp.concatenate(turns, 1)
    grad_rows = jnp.concatenate(
        [cut(turns, (team - other) % teams, width, 1) for other in range(teams)], 1
    )

    wqkv_low = short(w_qkv)
    wout_low = short(w_out)
    wup_low = short(w_up)
    wdown_low = short(w_down)
    heads = width // HEAD
    score_scale = HEAD ** (-0.5)
    queries = short(mm(packed_x, wqkv_low[0]) + bias_qv[0]).reshape(count, heads, HEAD)
    keys = short(mm(packed_x, wqkv_low[1])).reshape(count, heads, HEAD)
    values = short(mm(packed_x, wqkv_low[2]) + bias_qv[1]).reshape(count, heads, HEAD)
    raw = jnp.einsum("qhd,khd->hqk", queries, keys, preferred_element_type=f32)
    same = segments[:, None] == segments[None, :]
    masked = jnp.where(same[None], raw * score_scale, masked_score)
    exponent = jnp.exp(masked - jnp.max(masked, axis=-1, keepdims=True))
    probs = exponent / jnp.sum(exponent, axis=-1, keepdims=True)
    probs_low = short(probs)
    context = short(
        jnp.einsum("hqk,khd->qhd", probs_low, values, preferred_element_type=f32)
    ).reshape(count, width)
    (
        hidden_low,
        act_low,
        grad_z_low,
        grad_pre,
        grad_mid_low,
        grad_mid,
        result,
        vector_part,
        grad_down,
        grad_up,
    ) = middle(
        context.reshape(teams, share, width),
        packed_x[:share],
        wout_low,
        wup_low,
        wdown_low,
        bias_up,
        vectors,
        grad_rows,
        valid_own[:, None],
    )
    grad_bias_up = jnp.sum(grad_pre, axis=(0, 1), dtype=f32)
    grad_mid_low = grad_mid_low.reshape(count, D)
    vector_part = vector_part[:6]
    grad_out_t = short(mm_tn(grad_mid_low, context))
    grad_context = short(mm_nt(grad_mid_low, wout_low)).reshape(count, heads, HEAD)
    grad_probs = jnp.einsum("qhd,khd->hqk", grad_context, values, preferred_element_type=f32)
    weighted = jnp.sum(probs * grad_probs, axis=-1, keepdims=True)
    grad_scores = short(probs * (grad_probs - weighted))
    grad_values = short(
        jnp.einsum("hqk,qhd->khd", probs_low, grad_context, preferred_element_type=f32)
    ).reshape(count, width)
    grad_keys = short(
        jnp.einsum("hqk,qhd->khd", grad_scores, queries, preferred_element_type=f32) * score_scale
    ).reshape(count, width)
    grad_queries = short(
        jnp.einsum("hqk,khd->qhd", grad_scores, keys, preferred_element_type=f32) * score_scale
    ).reshape(count, width)
    grad_bias_pair = jnp.stack(
        [jnp.sum(grad_queries, axis=0, dtype=f32), jnp.sum(grad_values, axis=0, dtype=f32)]
    )
    grad_qkvo = jnp.concatenate(
        [
            short(mm_tn(packed_x, jnp.concatenate([grad_queries, grad_keys, grad_values], 1))),
            grad_out_t,
        ],
        1,
    )
    input_part = (
        mm_nt(grad_queries, wqkv_low[0])
        + mm_nt(grad_keys, wqkv_low[1])
        + mm_nt(grad_values, wqkv_low[2])
    )
    columns = D
    small = jnp.concatenate(
        [vector_part.reshape(-1), grad_bias_pair.reshape(-1), grad_bias_up.reshape(-1)]
    )
    rows_small = -(-small.size // (16 * columns)) * 16
    small = jnp.pad(short(small), (0, rows_small * columns - small.size)).reshape(rows_small, columns)
    down_sum, up_sum, qkvo_sum, small_sum, square, gram_tiles, given = sums_over_dp(
        inner,
        grad_down,
        grad_up,
        grad_qkvo,
        small,
        short(input_part).reshape(teams, groups // teams, per_peer, D),
        grad_mid.reshape(groups // teams, per_peer, D),
        result.reshape(groups // teams, per_peer, D),
        (mom_qkv, mom_out, mom_up, mom_down),
    )
    pieces = spread_list(short(mm_tn(choose, given.reshape(count, 2 * width))))
    output = to_given(jnp.concatenate([p[:, :width] for p in pieces], 1), width, 1)
    grad_tokens = wide(to_given(jnp.concatenate([p[:, width:] for p in pieces], 1), width, 1))

    qkvo_sum = wide(qkvo_sum)
    small_sum = small_sum.reshape(-1)
    gradients = (
        jnp.stack([qkvo_sum[:, k * width : (k + 1) * width] for k in range(3)]),
        qkvo_sum[:, 3 * width :].T,
        wide(up_sum),
        wide(down_sum),
        small_sum[6 * D : 6 * D + 2 * width].reshape(2, width),
        small_sum[6 * D + 2 * width : 6 * D + 2 * width + bias_up.shape[0]],
        small_sum[: 6 * D].reshape(6, D),
    )
    moments_old = (mom_qkv, mom_out, mom_up, mom_down, mom_bias_qv, mom_bias_up, mom_vectors)
    moments = tuple(
        momentum_decay * old + grad for old, grad in zip(moments_old, gradients)
    )

    up_low, down_low = short(moments[2]), short(moments[3])

    stepped = orthogonal_columns(square, gram_tiles)
    dp_rows = D // groups
    steps = lax.all_to_all(
        stepped.reshape(groups, dp_rows, width), "dp", split_axis=0, concat_axis=0, tiled=True
    )
    factors = spread_columns(steps[4:6].reshape(2 * dp_rows, width))

    def mine(values_, dim):
        return lax.dynamic_slice_in_dim(values_, group * dp_rows, dp_rows, dim)

    short_rate = rate_matrix * 0.2 * math.sqrt(D)
    long_rate = rate_matrix * 0.2 * math.sqrt(w_up.shape[1] * teams)
    masters = [
        mine(w_qkv, 1) - short_rate * wide(steps[:3]),
        mine(w_out, 1) - short_rate * wide(steps[3]).T,
        mine(w_up, 0) - long_rate * mm(factors[:dp_rows], up_low),
        mine(w_down, 1) - long_rate * mm_nt(down_low, factors[dp_rows:]),
    ]
    rate_vector = 0.2 / math.sqrt(all_tokens)
    for param, moment in zip((bias_qv, bias_up, vectors), moments[4:]):
        masters.append(param - rate_vector * moment)

    return (output, grad_tokens, *gradients, *moments, *masters)


def axis_layout(mesh):
    grid = mesh.devices
    groups, teams = grid.shape
    places = [getattr(d, "coords", None) for d in grid[:, 0]]
    inner = 2 if groups % 2 == 0 else 1
    if places[0] is not None:
        moved = [k for k in range(3) if places[0][k] != places[1][k]]
        fixed = [k for k in range(3) if k not in moved]
        inner = 1
        while inner < groups and all(places[inner][k] == places[0][k] for k in fixed):
            inner += 1
        if groups % inner:
            inner = 1
    return inner, (2 if teams % 2 == 0 else 1)


def solution(mesh):
    grads = (
        P(None, None, "tensor"),
        P("tensor", None),
        P(None, "tensor"),
        P("tensor", None),
        P(None, "tensor"),
        P("tensor"),
        P(),
    )
    rows = P("dp", None)
    return jax.shard_map(
        functools.partial(body, axis_layout(mesh)),
        mesh=mesh,
        in_specs=(rows, rows, rows, P(), *grads, *grads),
        out_specs=(
            rows,
            rows,
            *grads,
            *grads,
            P(None, "dp", "tensor"),
            P("tensor", "dp"),
            P("dp", "tensor"),
            P("tensor", "dp"),
            P(None, "tensor"),
            P("tensor"),
            P(),
        ),
        check_vma=False,
    )
```

```python
import functools
import math

import jax
import jax.numpy as jnp
from jax import lax
from jax.experimental import pallas as pl
from jax.experimental.pallas import tpu as pltpu
from jax.sharding import PartitionSpec as P

D = 1024
HEAD = 64

eps_norm = 1e-05
coef_one = 3.4445
coef_two = -4.775
coef_three = 2.0315
momentum_decay = 0.9
rate_matrix = 0.1
masked_score = -1000000000.0
bf16 = jnp.bfloat16
f32 = jnp.float32


def short(value):
    return value.astype(bf16)


def wide(value):
    return value.astype(f32)


def mm(left, right):
    return jnp.dot(short(left), short(right), preferred_element_type=f32)


def mm_nt(left, right):
    return lax.dot_general(
        short(left), short(right), (((1,), (1,)), ((), ())), preferred_element_type=f32
    )


def mm_tn(left, right):
    return lax.dot_general(
        short(left), short(right), (((0,), (0,)), ((), ())), preferred_element_type=f32
    )


def norm_forward(values, gain_row, shift_row):
    average = jnp.mean(values, axis=-1, keepdims=True)
    centred = values - average
    variance = jnp.mean(centred * centred, axis=-1, keepdims=True)
    inverse = lax.rsqrt(variance + eps_norm)
    normed = centred * inverse
    return (normed, inverse, normed * gain_row + shift_row)


def norm_backward(upstream, normed, inverse, gain_row):
    scaled = upstream * gain_row
    centre_term = jnp.mean(scaled, axis=-1, keepdims=True)
    slope_term = jnp.mean(scaled * normed, axis=-1, keepdims=True)
    return inverse * (scaled - centre_term - normed * slope_term)


class Ring:
    def __init__(self, axes, sizes, digit, members=None):
        self.axes = axes
        self.count = sizes[digit]
        self.below = math.prod(sizes[digit + 1 :])
        self.total = math.prod(sizes)
        self.members = members

    def send(self, value, offset):
        count, below = self.count, self.below
        pairs = []
        for i in range(self.total):
            if self.members is not None and not self.members(i):
                continue
            at = (i // below) % count
            pairs.append((i, i + ((at + offset) % count - at) * below))
        return lax.ppermute(value, self.axes, pairs)

    def place(self, linear):
        return (linear // self.below) % self.count


def cut(value, index, size, axis):
    return lax.dynamic_slice_in_dim(value, index * size, size, axis)


def tile_pairs(tiles):
    return [(i, j) for i in range(tiles) for j in range(i, tiles)]


def pick(options, index):
    chosen = jnp.int32(options[0])
    for k in range(1, len(options)):
        chosen = jnp.where(index == k, jnp.int32(options[k]), chosen)
    return chosen


def sum_kernel(
    inner,
    tile,
    down_ref,
    up_ref,
    qkvo_ref,
    small_ref,
    input_ref,
    mid_ref,
    result_ref,
    mom_qkv_ref,
    mom_out_ref,
    mom_up_ref,
    mom_down_ref,
    down_sum_ref,
    up_sum_ref,
    qkvo_sum_ref,
    small_sum_ref,
    square_ref,
    tiles_ref,
    given_ref,
    got_down,
    got_up,
    got_low,
    got_high,
    small_got,
    mom_up,
    mom_down,
    mom_column,
    mom_row,
    up_low,
    down_low,
    part,
    core_got,
    chip_sum,
    x_got,
    ring_sems,
    late_sems,
    small_sems,
    load_sem,
    core_sems,
    x_sems,
    back_sems,
    square_x_sems,
    square_core_sems,
    input_core,
    input_x,
    input_out,
    input_own,
    stage,
    back,
    input_core_sems,
    input_x_sems,
    stage_sems,
    given_sems,
):
    mesh_type = pl.DeviceIdType.MESH
    count = lax.axis_size("dp")
    index = lax.axis_index("dp")
    team = lax.axis_index("tensor")
    wides = lax.axis_size("tensor") // 2
    x_at, core = team // 2, team % 2
    outer = count // inner
    if inner == 2:
        place = jnp.where(index % 2 == 0, index // 2, count - 1 - index // 2)

        def device(p):
            return jnp.where(p < outer, 2 * p, 2 * (count - 1 - p) + 1)
    else:
        place = index

        def device(p):
            return p

    ring_next = ((device((place + 1) % count), team), (device((place + count - 1) % count), team))
    core_next = (index, x_at * 2 + 1 - core)
    x_up = (index, ((x_at + 1) % wides) * 2 + core)
    x_down = (index, ((x_at + wides - 1) % wides) * 2 + core)

    barrier = pltpu.get_barrier_semaphore()

    def greet(hop, carry):
        pl.semaphore_signal(
            barrier, inc=1, device_id=((index + hop) % count, team), device_id_type=mesh_type
        )
        return carry

    lax.fori_loop(1, count, greet, 0)
    for hop in range(1, 2 * wides):
        pl.semaphore_signal(
            barrier,
            inc=1,
            device_id=(index, (team + hop) % (2 * wides)),
            device_id_type=mesh_type,
        )
    pl.semaphore_wait(barrier, count - 1 + 2 * wides - 1)

    def remote(src, dst, sems, at, target):
        return pltpu.make_async_remote_copy(
            src_ref=src,
            dst_ref=dst,
            send_sem=sems.at[(0, *at)],
            recv_sem=sems.at[(1, *at)],
            device_id=target,
            device_id_type=mesh_type,
        )

    sent = []

    def ring(lanes, sems):
        streams = []
        for d, (x_ref, o_ref, first, length, got) in enumerate(lanes):
            chunk = length // count
            halves = 2 if chunk % 32 == 0 else 1
            sub = chunk // halves
            for h in range(halves):
                streams.append((d, h, x_ref, o_ref, first, chunk, sub, got))
        streams.sort(key=lambda one: one[1])

        def rows(stream, hop):
            d, h, _, _, first, chunk, sub, _ = stream
            at = (place + count - hop) % count if d == 0 else (place + hop) % count
            return pl.ds(pl.multiple_of(first + at * chunk + h * sub, 16), sub)

        def copy(stream, step):
            d, h, x_ref, o_ref, _, _, sub, got = stream
            if step < count - 1:
                slot = pl.ds(h * sub, sub)
                src = x_ref.at[rows(stream, 1)] if step == 0 else got.at[step - 1, slot]
                dst = got.at[step, slot]
            else:
                src = dst = o_ref.at[rows(stream, step - (count - 1))]
            return remote(src, dst, sems, (step, d, h), ring_next[d])

        for stream in streams:
            copy(stream, 0).start()
        yield 0
        for step in range(2 * (count - 1)):
            for stream in streams:
                _, h, x_ref, o_ref, _, _, sub, got = stream
                one = copy(stream, step)
                one.wait_recv()
                sent.append(one)
                if step < count - 1:
                    slot = pl.ds(h * sub, sub)
                    total = wide(got[step, slot]) + wide(x_ref[rows(stream, step + 2)])
                    if step < count - 2:
                        got[step, slot] = short(total)
                    else:
                        o_ref[rows(stream, 0)] = short(total)
                if step < 2 * count - 3:
                    copy(stream, step + 1).start()
                yield step

    half = qkvo_ref.shape[0] // 2
    first_ring = ring(
        [
            (down_ref, down_sum_ref, 0, down_ref.shape[0], got_down),
            (up_ref, up_sum_ref, 0, up_ref.shape[0], got_up),
        ],
        ring_sems,
    )
    second_ring = ring(
        [(qkvo_ref, qkvo_sum_ref, 0, half, got_low), (qkvo_ref, qkvo_sum_ref, half, half, got_high)],
        late_sems,
    )

    teams = 2 * wides
    peers = count // teams

    def input_tasks():

        def over_core(i):
            return remote(input_ref.at[wides + i], input_core.at[i], input_core_sems, (i,), core_next)

        def over_x(hop):
            return remote(input_out.at[hop], input_x.at[hop], input_x_sems, (hop,), x_up)

        def over_teams(hop):
            target = (team + hop) % teams
            mine = back.at[pl.ds(team * peers, peers)]
            return remote(stage.at[hop], mine, stage_sems, (hop,), (index, target))

        for i in range(wides - 1, -1, -1):
            over_core(i).start()
        for _ in range(5):
            yield
        for hop in range(wides):
            i = wides - 1 - hop
            over_core(i).wait_recv()
            total = wide(input_ref[i]) + wide(input_core[i])
            if hop > 0:
                over_x(hop - 1).wait_recv()
                total = total + wide(input_x[hop - 1])
            if i > 0:
                input_out[hop] = short(total)
                over_x(hop).start()
                for _ in range(8):
                    yield
            else:
                input_own[...] = short(total + mid_ref[...])
        yield
        part_width = result_ref.shape[2] // teams
        for hop in range(teams):
            columns = pl.ds(pl.multiple_of((team + hop) % teams * part_width, 128), part_width)
            for k, rows_ref in enumerate((result_ref, input_own)):
                stage[hop, :, :, k * part_width : (k + 1) * part_width] = rows_ref[:, :, columns]
            if hop > 0:
                over_teams(hop).start()
            else:
                back[pl.ds(team * peers, peers)] = stage[0]
            yield
        for _ in range(8):
            yield
        for i in range(wides):
            over_core(i).wait_send()
        for hop in range(wides - 1):
            over_x(hop).wait_send()
        for hop in range(1, teams):
            over_teams(hop).wait_recv()
            over_teams(hop).wait_send()

    def give(hop):
        target = (index + hop) % count
        return remote(back.at[target], given_ref.at[index], given_sems, (hop,), (target, team))

    def give_start(hop, carry):
        give(hop).start()
        return carry

    def give_wait(hop, carry):
        give(hop).wait_recv()
        give(hop).wait_send()
        return carry

    is_up, is_down = index == 4, index == 5
    is_gram = jnp.logical_or(is_up, is_down)
    size = up_ref.shape[0]
    pairs = tile_pairs(size // tile)
    share = len(pairs) // 2
    load_up = pltpu.make_async_copy(mom_up_ref, mom_up, load_sem.at[0])
    load_down = pltpu.make_async_copy(mom_down_ref, mom_down, load_sem.at[0])

    def gram_tasks():
        for ref, mom, total, low, load, mine in (
            (mom_up_ref, mom_up, up_sum_ref, up_low, load_up, is_up),
            (mom_down_ref, mom_down, down_sum_ref, down_low, load_down, is_down),
        ):

            @pl.when(mine)
            def _():
                load.wait()

            for start in range(0, ref.shape[0], 256):

                @pl.when(mine)
                def _():
                    rows = pl.ds(start, 256)
                    low[rows, :] = short(momentum_decay * mom[rows, :] + wide(total[rows, :]))

            yield

        def compute(k):
            row = pl.ds(pl.multiple_of(pick([p[0] for p in pairs], k) * tile, tile), tile)
            column = pl.ds(pl.multiple_of(pick([p[1] for p in pairs], k) * tile, tile), tile)

            @pl.when(is_up)
            def _():
                part[k] = mm_nt(up_low[row, :], up_low[column, :])

            @pl.when(is_down)
            def _():
                part[k] = mm_tn(down_low[:, row], down_low[:, column])

        def to_core(i):
            return remote(part.at[(1 - core) * share + i], core_got.at[i], core_sems, (i,), core_next)

        def to_x(i, hop):
            src = chip_sum.at[i] if hop == 0 else x_got.at[hop - 1, i]
            return remote(src, x_got.at[hop, i], x_sems, (hop, i), x_up)

        def to_back(i):
            at = tiles_ref.at[core * share + i]
            return remote(at, at, back_sems, (i,), core_next)

        for i in range(share):
            compute((1 - core) * share + i)

            @pl.when(is_gram)
            def _():
                to_core(i).start()

            yield
        for i in range(share):
            compute(core * share + i)
            yield
        for i in range(share):

            @pl.when(is_gram)
            def _():
                to_core(i).wait_recv()
                chip_sum[i] = part[core * share + i] + core_got[i]
                to_x(i, 0).start()

            yield
        for _ in range(12):
            yield
        for hop in range(wides - 1):
            for i in range(share):

                @pl.when(is_gram)
                def _():
                    to_x(i, hop).wait_recv()
                    before = chip_sum[i] if hop == 0 else tiles_ref[core * share + i]
                    tiles_ref[core * share + i] = before + x_got[hop, i]
                    if hop < wides - 2:
                        to_x(i, hop + 1).start()
                    else:
                        to_back(i).start()

                for _ in range(2):
                    yield

        @pl.when(is_gram)
        def _():
            for i in range(share):
                to_back(i).wait_recv()
                to_core(i).wait_send()
                to_back(i).wait_send()
                for hop in range(wides - 1):
                    to_x(i, hop).wait_send()

    def small_copy(hop):
        return remote(
            small_ref, small_got.at[hop], small_sems, (hop,), ((index + hop) % count, team)
        )

    def small_send(hop, carry):
        small_copy(hop).start()
        return carry

    def small_wait(hop, total):
        one = small_copy(hop)
        one.wait_send()
        one.wait_recv()
        return total + wide(small_got[hop])

    is_column, is_row = index < 3, index == 3
    is_square = index < 4
    width = square_ref.shape[2]
    load_column = pltpu.make_async_copy(
        mom_qkv_ref.at[jnp.minimum(index, 2)], mom_column, load_sem.at[0]
    )
    load_row = pltpu.make_async_copy(mom_out_ref, mom_row, load_sem.at[0])
    square_rows = square_ref.shape[1]
    block = 256
    blocks = square_rows // block

    def square_x(hop, b):
        rows = pl.ds(b * block, block)
        return remote(
            square_ref.at[hop, rows], square_ref.at[hop + 1, rows], square_x_sems, (hop, b), x_down
        )

    def square_core(hop, b):
        rows = pl.ds(b * block, block)
        return remote(
            square_ref.at[hop, rows], square_ref.at[wides + hop, rows], square_core_sems, (hop, b), core_next
        )

    def square_work():
        columns = pl.ds(pl.multiple_of(jnp.minimum(index, 3) * width, 128), width)
        for b in range(blocks):
            rows = pl.ds(b * block, block)
            fresh = wide(qkvo_sum_ref[rows, columns])

            @pl.when(is_column)
            def _():
                if b == 0:
                    load_column.wait()
                square_ref[0, rows] = short(momentum_decay * mom_column[rows, :] + fresh)

            @pl.when(is_row)
            def _():
                if b == 0:
                    load_row.wait()
                square_ref[0, rows] = short(momentum_decay * mom_row[:, rows].T + fresh)

            square_x(0, b).start()
            square_core(0, b).start()
        for hop in range(1, wides):
            for b in range(blocks):
                square_x(hop - 1, b).wait_recv()
                if hop < wides - 1:
                    square_x(hop, b).start()
                square_core(hop, b).start()
        for hop in range(wides):
            for b in range(blocks):
                square_core(hop, b).wait_recv()
        for hop in range(wides):
            for b in range(blocks):
                square_core(hop, b).wait_send()
                if hop < wides - 1:
                    square_x(hop, b).wait_send()

    next(first_ring)
    lax.fori_loop(1, count, small_send, 0)
    for one, mine in (
        (load_up, is_up),
        (load_down, is_down),
        (load_column, is_column),
        (load_row, is_row),
    ):

        @pl.when(mine)
        def _():
            one.start()

    beside = input_tasks()
    for step in first_ring:
        next(beside, None)
        if step >= 2 * count - 6:
            next(second_ring, None)
    for _ in beside:
        pass
    side = gram_tasks()
    for _ in second_ring:
        next(side, None)
    lax.fori_loop(1, count, give_start, 0)
    given_ref[index] = back[index]
    pl.when(is_square)(square_work)
    for _ in side:
        pass
    lax.fori_loop(1, count, give_wait, 0)
    small_sum_ref[...] = lax.fori_loop(1, count, small_wait, wide(small_ref[...]))
    for one in sent:
        one.wait_send()


def sums_over_dp(inner, down, up, qkvo, small, input_part, grad_mid, result, moments_old):
    groups, teams = lax.axis_size("dp"), lax.axis_size("tensor")
    wides = teams // 2
    size, width = qkvo.shape[0], qkvo.shape[1] // 4
    tile = size // 4
    pairs = len(tile_pairs(4))
    steps = 2 * (groups - 1)
    mom_qkv, mom_out, mom_up, mom_down = moments_old
    dma = pltpu.SemaphoreType.DMA
    vmem = pl.BlockSpec(memory_space=pltpu.VMEM)
    length = down.size + up.size + qkvo.size
    peers, rows, model = result.shape
    return pl.pallas_call(
        functools.partial(sum_kernel, inner, tile),
        name="sums_over_dp",
        out_shape=(
            jax.ShapeDtypeStruct(down.shape, bf16),
            jax.ShapeDtypeStruct(up.shape, bf16),
            jax.ShapeDtypeStruct(qkvo.shape, bf16),
            jax.ShapeDtypeStruct(small.shape, f32),
            jax.ShapeDtypeStruct((teams, size, width), bf16),
            jax.ShapeDtypeStruct((pairs, tile, tile), f32),
            jax.ShapeDtypeStruct((groups, rows, 2 * (model // teams)), bf16),
        ),
        in_specs=[vmem] * 7 + [pl.BlockSpec(memory_space=pl.ANY)] * 4,
        out_specs=[vmem] * 7,
        scratch_shapes=[
            pltpu.VMEM((groups - 1, down.shape[0] // groups, down.shape[1]), bf16),
            pltpu.VMEM((groups - 1, up.shape[0] // groups, up.shape[1]), bf16),
            pltpu.VMEM((groups - 1, size // 2 // groups, qkvo.shape[1]), bf16),
            pltpu.VMEM((groups - 1, size // 2 // groups, qkvo.shape[1]), bf16),
            pltpu.VMEM((groups, *small.shape), bf16),
            pltpu.VMEM(up.shape, f32),
            pltpu.VMEM(down.shape, f32),
            pltpu.VMEM((size, width), f32),
            pltpu.VMEM((width, size), f32),
            pltpu.VMEM(up.shape, bf16),
            pltpu.VMEM(down.shape, bf16),
            pltpu.VMEM((pairs, tile, tile), f32),
            pltpu.VMEM((pairs // 2, tile, tile), f32),
            pltpu.VMEM((pairs // 2, tile, tile), f32),
            pltpu.VMEM((wides - 1, pairs // 2, tile, tile), f32),
            dma((2, steps, 2, 2)),
            dma((2, steps, 2, 2)),
            dma((2, groups)),
            dma((1,)),
            dma((2, pairs // 2)),
            dma((2, wides - 1, pairs // 2)),
            dma((2, pairs // 2)),
            dma((2, wides - 1, size // 256)),
            dma((2, wides, size // 256)),
            pltpu.VMEM((wides, peers, rows, model), bf16),
            pltpu.VMEM((wides - 1, peers, rows, model), bf16),
            pltpu.VMEM((wides - 1, peers, rows, model), bf16),
            pltpu.VMEM((peers, rows, model), bf16),
            pltpu.VMEM((teams, peers, rows, 2 * (model // teams)), bf16),
            pltpu.VMEM((groups, rows, 2 * (model // teams)), bf16),
            dma((2, wides)),
            dma((2, wides - 1)),
            dma((2, teams)),
            dma((2, groups)),
        ],
        compiler_params=pltpu.CompilerParams(
            collective_id=0, has_side_effects=True, vmem_limit_bytes=31 * 2**20
        ),
        cost_estimate=pl.CostEstimate(
            flops=length, bytes_accessed=4 * length, transcendentals=0
        ),
    )(
        down, up, qkvo, small, input_part, grad_mid, result, mom_qkv, mom_out, mom_up, mom_down
    )


def dot(left, right):
    return jnp.dot(left, right, preferred_element_type=f32)

def dot_nt(left, right):
    return lax.dot_general(left, right, (((1,), (1,)), ((), ())), preferred_element_type=f32)

def middle_kernel(
    context_ref,
    x_ref,
    out_ref,
    up_ref,
    down_ref,
    bias_ref,
    vectors_ref,
    upstream_ref,
    valid_ref,
    hidden_ref,
    act_ref,
    grad_z_ref,
    grad_pre_ref,
    grad_mid_ref,
    own_grad_mid_ref,
    result_ref,
    vector_sum_ref,
    grad_down_ref,
    grad_up_ref,
    slope,
    held,
    core_out,
    core_got,
    x_out,
    x_got,
    normed_one,
    own_hidden,
    normed_two,
    own_grad_z,
    vector_own,
    vector_got,
    core_sems,
    x_sems,
    spread_x_sems,
    spread_core_sems,
    vector_sems,
):
    mesh_type = pl.DeviceIdType.MESH
    index = lax.axis_index("dp")
    team = lax.axis_index("tensor")
    teams = lax.axis_size("tensor")
    wides = teams // 2
    x_at, core = team // 2, team % 2
    core_next = (index, x_at * 2 + 1 - core)
    x_up = (index, ((x_at + 1) % wides) * 2 + core)
    x_down = (index, ((x_at + wides - 1) % wides) * 2 + core)
    barrier = pltpu.get_barrier_semaphore()
    for hop in range(1, teams):
        pl.semaphore_signal(
            barrier, inc=1, device_id=(index, (team + hop) % teams), device_id_type=mesh_type
        )
    pl.semaphore_wait(barrier, teams - 1)
    sent = []

    def remote(src, dst, sems, at, target):
        return pltpu.make_async_remote_copy(
            src_ref=src,
            dst_ref=dst,
            send_sem=sems.at[(0, *at)],
            recv_sem=sems.at[(1, *at)],
            device_id=target,
            device_id_type=mesh_type,
        )

    def start(one):
        one.start()
        sent.append(one)

    def over_core(s, i):
        return remote(core_out.at[s, i], core_got.at[s, i], core_sems, (s, i), core_next)

    def over_x(s, hop):
        return remote(x_out.at[s, hop], x_got.at[s, hop], x_sems, (s, hop), x_up)

    def finish(s, filler):
        for hop in range(wides):
            i = wides - 1 - hop
            over_core(s, i).wait_recv()
            total = held[i] + wide(core_got[s, i])
            if hop > 0:
                if filler is not None:
                    filler()
                    filler = None
                over_x(s, hop - 1).wait_recv()
                total = total + wide(x_got[s, hop - 1])
            if i > 0:
                x_out[s, hop] = short(total)
                start(over_x(s, hop))
        return total

    def along_x(s, ref, i):
        return remote(ref.at[i], ref.at[i + 1], spread_x_sems, (s, i), x_down)

    def across(s, ref, i):
        return remote(ref.at[i], ref.at[wides + i], spread_core_sems, (s, i), core_next)

    def spread(s, ref):
        start(along_x(s, ref, 0))
        start(across(s, ref, 0))

    def arrive(s, ref, i):
        if i > 0:
            along_x(s, ref, i - 1).wait_recv()
            start(across(s, ref, i))
            if i < wides - 1:
                start(along_x(s, ref, i))
        across(s, ref, i).wait_recv()

    share = x_ref.shape[0]

    def pair(ref, i):
        return jnp.concatenate([ref[i], ref[wides + i]], 0)

    def put_pair(ref, i, value):
        ref[i] = value[:share]
        ref[wides + i] = value[share:]

    def keep(s, i, partial):
        core_out[s, i] = short(partial[share:])
        start(over_core(s, i))
        held[i] = partial[:share]

    def sums(value):
        return jnp.sum(value, axis=0, keepdims=True)

    for i in range(wides - 1, -1, -1):
        keep(0, i, dot(pair(context_ref, i), out_ref[...]))
    mid = wide(x_ref[...]) + finish(0, None) + vectors_ref[0:1, :]
    normed, inverse_one, hidden = norm_forward(mid, vectors_ref[1:2, :], vectors_ref[2:3, :])
    normed_one[...] = normed
    own_hidden[...] = hidden
    hidden_ref[0] = short(hidden)
    spread(0, hidden_ref)

    units = up_ref.shape[1]
    step = min(units, 512)
    for i in range(wides):
        arrive(0, hidden_ref, i)
        rows = pair(hidden_ref, i)
        for c in range(0, units, step):
            at = slice(c, c + step)
            pre = dot(rows, up_ref[:, at]) + bias_ref[:, at]
            phi = 0.5 + 0.5 * lax.erf(pre * math.sqrt(0.5))
            act = short(pre * phi)
            bend = phi + pre * jnp.exp(-0.5 * pre * pre) * (1.0 / math.sqrt(2.0 * math.pi))
            for r, part in ((i, slice(0, share)), (wides + i, slice(share, 2 * share))):
                act_ref[r, :, at] = act[part]
                slope[r, :, at] = bend[part]
        keep(1, i, dot(pair(act_ref, i), down_ref[...]))
    summed = own_hidden[...] + finish(1, None) + vectors_ref[3:4, :]
    gain_two = vectors_ref[4:5, :]
    normed, inverse_two, result = norm_forward(summed, gain_two, vectors_ref[5:6, :])
    result_ref[...] = short(result)
    upstream = wide(upstream_ref[...]) * valid_ref[...]
    grad_z = norm_backward(upstream, normed, inverse_two, gain_two)
    own_grad_z[...] = grad_z
    grad_z_ref[0] = short(grad_z)
    spread(1, grad_z_ref)
    vector_own[...] = jnp.zeros_like(vector_own)
    vector_own[3:4, :] = sums(grad_z)
    vector_own[4:5, :] = sums(upstream * normed)
    vector_own[5:6, :] = sums(upstream)

    for i in range(wides):
        arrive(1, grad_z_ref, i)
        rows = pair(grad_z_ref, i)
        for c in range(0, units, step):
            at = slice(c, c + step)
            grad = dot_nt(rows, down_ref[at, :])
            for r, part in ((i, slice(0, share)), (wides + i, slice(share, 2 * share))):
                grad_pre_ref[r, :, at] = short(grad[part] * slope[r, :, at])
        keep(2, i, dot_nt(pair(grad_pre_ref, i), up_ref[...]))

    def every(ref, at):
        return jnp.concatenate([ref[r, :, at] for r in range(teams)], 0)

    def down_filler():
        def one(k, carry):
            at = pl.ds(pl.multiple_of(k * 128, 128), 128)
            grad_down_ref[at, :] = short(mm_tn(every(act_ref, at), every(grad_z_ref, slice(None))))
            return carry

        lax.fori_loop(0, units // 128, one, 0)

    grad_hidden = own_grad_z[...] + finish(2, down_filler)
    grad_mid = norm_backward(grad_hidden, normed_one[...], inverse_one, vectors_ref[1:2, :])
    own_grad_mid_ref[...] = grad_mid
    grad_mid_ref[0] = short(grad_mid)
    spread(2, grad_mid_ref)
    vector_own[0:1, :] = sums(grad_mid)
    vector_own[1:2, :] = sums(grad_hidden * normed_one[...])
    vector_own[2:3, :] = sums(grad_hidden)

    def to_team(hop):
        return remote(
            vector_own, vector_got.at[hop], vector_sems, (hop,), (index, (team + hop) % teams)
        )

    for hop in range(1, teams):
        start(to_team(hop))

    def up_filler(k, carry):
        at = pl.ds(pl.multiple_of(k * 128, 128), 128)
        grad_up_ref[at, :] = short(mm_tn(every(hidden_ref, at), every(grad_pre_ref, slice(None))))
        return carry

    lax.fori_loop(0, hidden_ref.shape[2] // 128, up_filler, 0)
    for i in range(wides):
        arrive(2, grad_mid_ref, i)
    total = vector_own[...]
    for hop in range(1, teams):
        to_team(hop).wait_recv()
        total = total + vector_got[hop]
    vector_sum_ref[...] = total
    for one in sent:
        one.wait_send()


def middle(context, x_own, w_out, w_up, w_down, bias_up, vectors, upstream, valid):
    teams, share, width = context.shape
    model, units = w_up.shape
    wides = teams // 2
    dma = pltpu.SemaphoreType.DMA
    vmem = pl.BlockSpec(memory_space=pltpu.VMEM)
    rows = jax.ShapeDtypeStruct((teams, share, model), bf16)
    inner = jax.ShapeDtypeStruct((teams, share, units), bf16)
    own = pltpu.VMEM((share, model), f32)
    return pl.pallas_call(
        middle_kernel,
        name="middle",
        out_shape=(
            rows,
            inner,
            rows,
            inner,
            rows,
            jax.ShapeDtypeStruct((share, model), f32),
            jax.ShapeDtypeStruct((share, model), bf16),
            jax.ShapeDtypeStruct((8, model), f32),
            jax.ShapeDtypeStruct((units, model), bf16),
            jax.ShapeDtypeStruct((model, units), bf16),
        ),
        in_specs=[vmem] * 9,
        out_specs=[vmem] * 10,
        scratch_shapes=[
            pltpu.VMEM((teams, share, units), f32),
            pltpu.VMEM((wides, share, model), f32),
            pltpu.VMEM((3, wides, share, model), bf16),
            pltpu.VMEM((3, wides, share, model), bf16),
            pltpu.VMEM((3, wides - 1, share, model), bf16),
            pltpu.VMEM((3, wides - 1, share, model), bf16),
            own,
            own,
            own,
            own,
            pltpu.VMEM((8, model), f32),
            pltpu.VMEM((teams, 8, model), f32),
            dma((2, 3, wides)),
            dma((2, 3, wides - 1)),
            dma((2, 3, wides - 1)),
            dma((2, 3, wides)),
            dma((2, teams)),
        ],
        compiler_params=pltpu.CompilerParams(
            collective_id=1, has_side_effects=True, vmem_limit_bytes=48 * 2**20
        ),
        cost_estimate=pl.CostEstimate(
            flops=12 * teams * share * model * units,
            bytes_accessed=8 * model * units,
            transcendentals=0,
        ),
    )(context, x_own, w_out, w_up, w_down, bias_up.reshape(1, units), vectors, upstream, valid)


def polar_kernel(block, m_ref, o_ref, x_ref, gram_ref, low_ref, mix_ref):
    teams, size, width = m_ref.shape
    keep = o_ref.shape[1]
    bits = 256

    def rows(i):
        return pl.ds(pl.multiple_of(i * bits, bits), bits)

    def columns(j):
        return pl.ds(pl.multiple_of(j * block, block), block)

    def norm_step(i, total):
        for r in range(teams):
            part = wide(m_ref[r, rows(i), :])
            total = total + jnp.sum(part * part, axis=0, keepdims=True)
        return total

    total = lax.fori_loop(0, size // bits, norm_step, jnp.zeros((1, width), f32))
    scale = lax.rsqrt(jnp.sum(total, axis=1, keepdims=True) + 1e-07)

    def scale_step(i, carry):
        for r in range(teams):
            x_ref[0, rows(i), r * width : (r + 1) * width] = short(wide(m_ref[r, rows(i), :]) * scale)
        return carry

    lax.fori_loop(0, size // bits, scale_step, 0)

    def sweep(k, carry):
        now = k % 2
        x = x_ref.at[now]

        def gram_step(j, carry):
            gram = dot_nt(x[...], x[columns(j), :])
            gram_ref[:, columns(j)] = gram
            low_ref[:, columns(j)] = short(gram)
            return carry

        def mix_step(j, carry):
            power = dot(low_ref[...], low_ref[:, columns(j)])
            mix_ref[:, columns(j)] = short(coef_two * gram_ref[:, columns(j)] + coef_three * power)
            return carry

        def next_step(j, carry):
            mixed = dot(mix_ref[...], x[:, columns(j)])
            x_ref[1 - now, :, columns(j)] = short(coef_one * wide(x[:, columns(j)]) + mixed)
            return carry

        lax.fori_loop(0, size // block, gram_step, 0)
        lax.fori_loop(0, size // block, mix_step, 0)
        lax.fori_loop(0, jnp.where(k < 4, size // block, -(-keep // block)), next_step, 0)
        return carry

    lax.fori_loop(0, 5, sweep, 0)
    o_ref[...] = x_ref[1, :, :keep]


def factor_kernel(block, g_ref, o_ref, current_ref, poly_ref, half_ref, factor_ref):
    size = poly_ref.shape[0]
    tile = g_ref.shape[1]
    tiles = size // tile
    keep = o_ref.shape[1]
    first = lax.axis_index("tensor") * keep
    eye = lax.broadcasted_iota(jnp.int32, (tile, tile), 0) == lax.broadcasted_iota(
        jnp.int32, (tile, tile), 1
    )
    trace = jnp.zeros((1, 1), f32)
    for k, (i, j) in enumerate(tile_pairs(tiles)):
        if i == j:
            diagonal = jnp.where(eye, g_ref[k], 0.0)
            trace = trace + jnp.sum(jnp.sum(diagonal, axis=0, keepdims=True), axis=1, keepdims=True)
    scale = lax.rsqrt(trace + 1e-07)
    scale_two = scale * scale

    def store(slot, rows, columns, value):
        high = short(value)
        current_ref[slot, 0, rows, columns] = high
        current_ref[slot, 1, rows, columns] = short(value - wide(high))

    def span(i):
        return slice(i * tile, (i + 1) * tile)

    for k, (i, j) in enumerate(tile_pairs(tiles)):
        part = g_ref[k] * scale_two
        store(0, span(i), span(j), part)
        if i != j:
            store(0, span(j), span(i), part.T)

    def cols(j):
        return pl.ds(pl.multiple_of(j * block, block), block)

    def sweep(k, exact, exact_next, last):
        now = k % 2
        high_ref, low_ref = current_ref.at[now, 0], current_ref.at[now, 1]

        def poly_step(j, carry):
            power = dot(high_ref[...], high_ref[:, cols(j)])
            if last:
                power = power + dot(high_ref[...], low_ref[:, cols(j)])
            r = lax.broadcasted_iota(jnp.int32, (size, block), 0)
            c = lax.broadcasted_iota(jnp.int32, (size, block), 1) + j * block
            present = wide(high_ref[:, cols(j)]) + wide(low_ref[:, cols(j)])
            poly = coef_two * present + coef_three * power
            poly_ref[:, cols(j)] = short(poly + jnp.where(r == c, coef_one, 0.0))
            return carry

        def half_step(j, carry):
            half = dot(poly_ref[...], high_ref[:, cols(j)])
            if exact:
                half = half + dot(poly_ref[...], low_ref[:, cols(j)])
            high = short(half)
            half_ref[0, :, cols(j)] = high
            if exact_next:
                half_ref[1, :, cols(j)] = short(half - wide(high))
            return carry

        def next_step(j, carry):
            new = dot(half_ref[0], poly_ref[:, cols(j)])
            if exact_next:
                new = new + dot(half_ref[1], poly_ref[:, cols(j)])
            store(1 - now, slice(None), cols(j), new)
            return carry

        lax.fori_loop(0, size // block, poly_step, 0)
        if not last:
            lax.fori_loop(0, size // block, half_step, 0)
            lax.fori_loop(0, size // block, next_step, 0)

    def plain_sweep(k, carry):
        sweep(k, False, False, False)
        factor_ref[...] = short(dot(poly_ref[...], factor_ref[...]))
        return carry

    sweep(0, True, True, False)
    factor_ref[...] = poly_ref[:, pl.ds(pl.multiple_of(first, 128), keep)]
    sweep(1, True, False, False)
    factor_ref[...] = short(dot(poly_ref[...], factor_ref[...]))
    lax.fori_loop(2, 4, plain_sweep, 0)
    sweep(4, False, False, True)
    o_ref[...] = short(dot(poly_ref[...], factor_ref[...]) * scale)


def step_kernel(
    block,
    square_ref,
    tiles_ref,
    o_ref,
    x_ref,
    gram_ref,
    low_ref,
    mix_ref,
    current_ref,
    poly_ref,
    half_ref,
    factor_ref,
):
    index = lax.axis_index("dp")

    @pl.when(index < 4)
    def _():
        polar_kernel(block, square_ref, o_ref, x_ref, gram_ref, low_ref, mix_ref)

    @pl.when(jnp.logical_or(index == 4, index == 5))
    def _():
        factor_kernel(block, tiles_ref, o_ref, current_ref, poly_ref, half_ref, factor_ref)

    @pl.when(index > 5)
    def _():
        o_ref[...] = jnp.zeros_like(o_ref)


def orthogonal_columns(square, tiles):
    teams, size, width = square.shape
    vmem = pl.BlockSpec(memory_space=pltpu.VMEM)
    return pl.pallas_call(
        functools.partial(step_kernel, 512),
        name="orthogonal_columns",
        out_shape=jax.ShapeDtypeStruct((size, width), bf16),
        in_specs=[vmem] * 2,
        out_specs=vmem,
        scratch_shapes=[
            pltpu.VMEM((2, size, teams * width), bf16),
            pltpu.VMEM((size, size), f32),
            pltpu.VMEM((size, size), bf16),
            pltpu.VMEM((size, size), bf16),
            pltpu.VMEM((2, 2, size, size), bf16),
            pltpu.VMEM((size, size), bf16),
            pltpu.VMEM((2, size, size), bf16),
            pltpu.VMEM((size, width), bf16),
        ],
        compiler_params=pltpu.CompilerParams(vmem_limit_bytes=48 * 2**20),
        cost_estimate=pl.CostEstimate(
            flops=40 * size**3, bytes_accessed=8 * size * size, transcendentals=0
        ),
    )(square, tiles)


def body(
    layout,
    tokens,
    cotangent,
    lengths,
    packing,
    w_qkv,
    w_out,
    w_up,
    w_down,
    bias_qv,
    bias_up,
    vectors,
    mom_qkv,
    mom_out,
    mom_up,
    mom_down,
    mom_bias_qv,
    mom_bias_up,
    mom_vectors,
):
    inner, cores = layout
    groups = lax.axis_size("dp")
    teams = lax.axis_size("tensor")
    group = lax.axis_index("dp")
    team = lax.axis_index("tensor")
    outer, wides = groups // inner, teams // cores
    count = tokens.shape[0]
    per_peer = count // groups
    share = count // teams
    width = D // teams
    all_tokens = count * groups

    outer_ring = Ring("dp", (outer, inner), 0)
    inner_ring = Ring("dp", (outer, inner), 1)
    outer_at, inner_at = outer_ring.place(group), inner_ring.place(group)
    x_ring = Ring("tensor", (wides, cores), 0)
    core_ring = Ring("tensor", (wides, cores), 1)
    x_at, core_at = x_ring.place(team), core_ring.place(team)

    def team_of(rank):
        return ((x_at + rank % wides) % wides) * cores + (core_at + rank // wides) % cores

    def to_relative(value, size, axis=0):
        return jnp.concatenate([cut(value, team_of(r), size, axis) for r in range(teams)], axis)

    def to_given(value, size, axis=0):
        parts = []
        for other in range(teams):
            rank = ((other % cores - core_at) % cores) * wides + (other // cores - x_at) % wides
            parts.append(cut(value, rank, size, axis))
        return jnp.concatenate(parts, axis)

    def spread_list(piece, ring_x=x_ring, ring_core=core_ring):
        line = [piece]
        for _ in range(wides - 1):
            line.append(ring_x.send(line[-1], -1))
        pieces = list(line)
        for hop in range(1, cores):
            pieces += [ring_core.send(p, -hop) for p in line]
        return pieces

    def spread_columns(piece):
        return to_given(jnp.concatenate(spread_list(piece), 1), piece.shape[1], 1)

    def own_rows(value):
        return cut(value, team, share, 0)

    position = jnp.arange(count, dtype=jnp.int32)
    peer = jnp.arange(groups, dtype=jnp.int32)
    packed = packing.reshape(groups, count)
    source = packed // count
    source_mine = lax.dynamic_index_in_dim(source, group, 0, keepdims=False)
    masks = jnp.concatenate([source == group, source_mine[None, :] == peer[:, None]], 0)
    before = (position[:, None] < position[None, :]).astype(bf16)
    rank = mm(masks.astype(bf16), before).astype(jnp.int32)
    key = jnp.where(masks, rank, -1)
    value = jnp.concatenate(
        [packed % count, jnp.broadcast_to(position[None, :], (groups, count))], 0
    )
    slot_in_message = jnp.arange(per_peer, dtype=jnp.int32)
    picked = jnp.sum(
        jnp.where(key[:, None, :] == slot_in_message[None, :, None], value[:, None, :], 0), axis=-1
    )
    rows_sent = picked[:groups].reshape(count)
    slots = picked[groups:].reshape(count)
    choose = (rows_sent[:, None] == position[None, :]).astype(bf16)

    length_row = lengths[0]
    end_one = length_row[0]
    end_two = end_one + length_row[1]
    end_all = end_two + length_row[2]
    segments = (
        (slots >= end_one).astype(jnp.int32)
        + (slots >= end_two).astype(jnp.int32)
        + (slots >= end_all).astype(jnp.int32)
        + jnp.maximum(slots - end_all, 0)
    )
    valid_own = own_rows((slots < end_all).astype(f32))
    segments = to_relative(segments, share)

    own_columns = jnp.concatenate([cut(tokens, team, width, 1), cut(cotangent, team, width, 1)], 1)
    sent = short(mm(choose, own_columns)).reshape(groups, per_peer, 2 * width)
    got = lax.all_to_all(sent, "dp", split_axis=0, concat_axis=0, tiled=True)
    got = got.reshape(count, 2 * width)

    packed_x = to_relative(spread_columns(got[:, :width]), share)
    turns = []
    for hop in range(teams):
        block = cut(got[:, width:], (team + hop) % teams, share, 0)
        if hop > 0:
            block = lax.ppermute(block, "tensor", [(i, (i + hop) % teams) for i in range(teams)])
        turns.append(block)
    turns = jnp.concatenate(turns, 1)
    grad_rows = jnp.concatenate(
        [cut(turns, (team - other) % teams, width, 1) for other in range(teams)], 1
    )

    wqkv_low = short(w_qkv)
    wout_low = short(w_out)
    wup_low = short(w_up)
    wdown_low = short(w_down)
    heads = width // HEAD
    score_scale = HEAD ** (-0.5)
    queries = short(mm(packed_x, wqkv_low[0]) + bias_qv[0]).reshape(count, heads, HEAD)
    keys = short(mm(packed_x, wqkv_low[1])).reshape(count, heads, HEAD)
    values = short(mm(packed_x, wqkv_low[2]) + bias_qv[1]).reshape(count, heads, HEAD)
    raw = jnp.einsum("qhd,khd->hqk", queries, keys, preferred_element_type=f32)
    same = segments[:, None] == segments[None, :]
    masked = jnp.where(same[None], raw * score_scale, masked_score)
    exponent = jnp.exp(masked - jnp.max(masked, axis=-1, keepdims=True))
    probs = exponent / jnp.sum(exponent, axis=-1, keepdims=True)
    probs_low = short(probs)
    context = short(
        jnp.einsum("hqk,khd->qhd", probs_low, values, preferred_element_type=f32)
    ).reshape(count, width)
    (
        hidden_low,
        act_low,
        grad_z_low,
        grad_pre,
        grad_mid_low,
        grad_mid,
        result,
        vector_part,
        grad_down,
        grad_up,
    ) = middle(
        context.reshape(teams, share, width),
        packed_x[:share],
        wout_low,
        wup_low,
        wdown_low,
        bias_up,
        vectors,
        grad_rows,
        valid_own[:, None],
    )
    grad_bias_up = jnp.sum(grad_pre, axis=(0, 1), dtype=f32)
    grad_mid_low = grad_mid_low.reshape(count, D)
    vector_part = vector_part[:6]
    grad_out_t = short(mm_tn(grad_mid_low, context))
    grad_context = short(mm_nt(grad_mid_low, wout_low)).reshape(count, heads, HEAD)
    grad_probs = jnp.einsum("qhd,khd->hqk", grad_context, values, preferred_element_type=f32)
    weighted = jnp.sum(probs * grad_probs, axis=-1, keepdims=True)
    grad_scores = short(probs * (grad_probs - weighted))
    grad_values = short(
        jnp.einsum("hqk,qhd->khd", probs_low, grad_context, preferred_element_type=f32)
    ).reshape(count, width)
    grad_keys = short(
        jnp.einsum("hqk,qhd->khd", grad_scores, queries, preferred_element_type=f32) * score_scale
    ).reshape(count, width)
    grad_queries = short(
        jnp.einsum("hqk,khd->qhd", grad_scores, keys, preferred_element_type=f32) * score_scale
    ).reshape(count, width)
    grad_bias_pair = jnp.stack(
        [jnp.sum(grad_queries, axis=0, dtype=f32), jnp.sum(grad_values, axis=0, dtype=f32)]
    )
    grad_qkvo = jnp.concatenate(
        [
            short(mm_tn(packed_x, jnp.concatenate([grad_queries, grad_keys, grad_values], 1))),
            grad_out_t,
        ],
        1,
    )
    input_part = (
        mm_nt(grad_queries, wqkv_low[0])
        + mm_nt(grad_keys, wqkv_low[1])
        + mm_nt(grad_values, wqkv_low[2])
    )
    columns = D
    small = jnp.concatenate(
        [vector_part.reshape(-1), grad_bias_pair.reshape(-1), grad_bias_up.reshape(-1)]
    )
    rows_small = -(-small.size // (16 * columns)) * 16
    small = jnp.pad(short(small), (0, rows_small * columns - small.size)).reshape(rows_small, columns)
    down_sum, up_sum, qkvo_sum, small_sum, square, gram_tiles, given = sums_over_dp(
        inner,
        grad_down,
        grad_up,
        grad_qkvo,
        small,
        short(input_part).reshape(teams, groups // teams, per_peer, D),
        grad_mid.reshape(groups // teams, per_peer, D),
        result.reshape(groups // teams, per_peer, D),
        (mom_qkv, mom_out, mom_up, mom_down),
    )
    pieces = spread_list(short(mm_tn(choose, given.reshape(count, 2 * width))))
    output = to_given(jnp.concatenate([p[:, :width] for p in pieces], 1), width, 1)
    grad_tokens = wide(to_given(jnp.concatenate([p[:, width:] for p in pieces], 1), width, 1))

    qkvo_sum = wide(qkvo_sum)
    small_sum = small_sum.reshape(-1)
    gradients = (
        jnp.stack([qkvo_sum[:, k * width : (k + 1) * width] for k in range(3)]),
        qkvo_sum[:, 3 * width :].T,
        wide(up_sum),
        wide(down_sum),
        small_sum[6 * D : 6 * D + 2 * width].reshape(2, width),
        small_sum[6 * D + 2 * width : 6 * D + 2 * width + bias_up.shape[0]],
        small_sum[: 6 * D].reshape(6, D),
    )
    moments_old = (mom_qkv, mom_out, mom_up, mom_down, mom_bias_qv, mom_bias_up, mom_vectors)
    moments = tuple(
        momentum_decay * old + grad for old, grad in zip(moments_old, gradients)
    )

    up_low, down_low = short(moments[2]), short(moments[3])

    stepped = orthogonal_columns(square, gram_tiles)
    dp_rows = D // groups
    steps = lax.all_to_all(
        stepped.reshape(groups, dp_rows, width), "dp", split_axis=0, concat_axis=0, tiled=True
    )
    factors = spread_columns(steps[4:6].reshape(2 * dp_rows, width))

    def mine(values_, dim):
        return lax.dynamic_slice_in_dim(values_, group * dp_rows, dp_rows, dim)

    short_rate = rate_matrix * 0.2 * math.sqrt(D)
    long_rate = rate_matrix * 0.2 * math.sqrt(w_up.shape[1] * teams)
    masters = [
        mine(w_qkv, 1) - short_rate * wide(steps[:3]),
        mine(w_out, 1) - short_rate * wide(steps[3]).T,
        mine(w_up, 0) - long_rate * mm(factors[:dp_rows], up_low),
        mine(w_down, 1) - long_rate * mm_nt(down_low, factors[dp_rows:]),
    ]
    rate_vector = 0.2 / math.sqrt(all_tokens)
    for param, moment in zip((bias_qv, bias_up, vectors), moments[4:]):
        masters.append(param - rate_vector * moment)

    return (output, grad_tokens, *gradients, *moments, *masters)


def axis_layout(mesh):
    grid = mesh.devices
    groups, teams = grid.shape
    places = [getattr(d, "coords", None) for d in grid[:, 0]]
    inner = 2 if groups % 2 == 0 else 1
    if places[0] is not None:
        moved = [k for k in range(3) if places[0][k] != places[1][k]]
        fixed = [k for k in range(3) if k not in moved]
        inner = 1
        while inner < groups and all(places[inner][k] == places[0][k] for k in fixed):
            inner += 1
        if groups % inner:
            inner = 1
    return inner, (2 if teams % 2 == 0 else 1)


def solution(mesh):
    grads = (
        P(None, None, "tensor"),
        P("tensor", None),
        P(None, "tensor"),
        P("tensor", None),
        P(None, "tensor"),
        P("tensor"),
        P(),
    )
    rows = P("dp", None)
    return jax.shard_map(
        functools.partial(body, axis_layout(mesh)),
        mesh=mesh,
        in_specs=(rows, rows, rows, P(), *grads, *grads),
        out_specs=(
            rows,
            rows,
            *grads,
            *grads,
            P(None, "dp", "tensor"),
            P("tensor", "dp"),
            P("dp", "tensor"),
            P("tensor", "dp"),
            P(None, "tensor"),
            P("tensor"),
            P(),
        ),
        check_vma=False,
    )
```

```python
import functools
import math

import jax
import jax.numpy as jnp
from jax import lax
from jax.experimental import pallas as pl
from jax.experimental.pallas import tpu as pltpu
from jax.sharding import PartitionSpec as P

D = 1024
HEAD = 64

eps_norm = 1e-05
coef_one = 3.4445
coef_two = -4.775
coef_three = 2.0315
momentum_decay = 0.9
rate_matrix = 0.1
masked_score = -1000000000.0
bf16 = jnp.bfloat16
f32 = jnp.float32


def short(value):
    return value.astype(bf16)


def wide(value):
    return value.astype(f32)


def mm(left, right):
    return jnp.dot(short(left), short(right), preferred_element_type=f32)


def mm_nt(left, right):
    return lax.dot_general(
        short(left), short(right), (((1,), (1,)), ((), ())), preferred_element_type=f32
    )


def mm_tn(left, right):
    return lax.dot_general(
        short(left), short(right), (((0,), (0,)), ((), ())), preferred_element_type=f32
    )


def norm_forward(values, gain_row, shift_row):
    average = jnp.mean(values, axis=-1, keepdims=True)
    centred = values - average
    variance = jnp.mean(centred * centred, axis=-1, keepdims=True)
    inverse = lax.rsqrt(variance + eps_norm)
    normed = centred * inverse
    return (normed, inverse, normed * gain_row + shift_row)


def norm_backward(upstream, normed, inverse, gain_row):
    scaled = upstream * gain_row
    centre_term = jnp.mean(scaled, axis=-1, keepdims=True)
    slope_term = jnp.mean(scaled * normed, axis=-1, keepdims=True)
    return inverse * (scaled - centre_term - normed * slope_term)


class Ring:
    def __init__(self, axes, sizes, digit, members=None):
        self.axes = axes
        self.count = sizes[digit]
        self.below = math.prod(sizes[digit + 1 :])
        self.total = math.prod(sizes)
        self.members = members

    def send(self, value, offset):
        count, below = self.count, self.below
        pairs = []
        for i in range(self.total):
            if self.members is not None and not self.members(i):
                continue
            at = (i // below) % count
            pairs.append((i, i + ((at + offset) % count - at) * below))
        return lax.ppermute(value, self.axes, pairs)

    def place(self, linear):
        return (linear // self.below) % self.count


def cut(value, index, size, axis):
    return lax.dynamic_slice_in_dim(value, index * size, size, axis)


def tile_pairs(tiles):
    return [(i, j) for i in range(tiles) for j in range(i, tiles)]


def pick(options, index):
    chosen = jnp.int32(options[0])
    for k in range(1, len(options)):
        chosen = jnp.where(index == k, jnp.int32(options[k]), chosen)
    return chosen


def sum_kernel(
    inner,
    tile,
    down_ref,
    up_ref,
    qkvo_ref,
    small_ref,
    input_ref,
    mid_ref,
    result_ref,
    mom_qkv_ref,
    mom_out_ref,
    mom_up_ref,
    mom_down_ref,
    down_sum_ref,
    up_sum_ref,
    qkvo_sum_ref,
    small_sum_ref,
    square_ref,
    tiles_ref,
    given_ref,
    got_down,
    got_up,
    got_low,
    got_high,
    small_got,
    mom_up,
    mom_down,
    mom_column,
    mom_row,
    up_low,
    down_low,
    part,
    core_got,
    chip_sum,
    x_got,
    ring_sems,
    late_sems,
    small_sems,
    load_sem,
    core_sems,
    x_sems,
    back_sems,
    square_x_sems,
    square_core_sems,
    input_core,
    input_x,
    input_out,
    input_own,
    stage,
    back,
    input_core_sems,
    input_x_sems,
    stage_sems,
    given_sems,
):
    mesh_type = pl.DeviceIdType.MESH
    count = lax.axis_size("dp")
    index = lax.axis_index("dp")
    team = lax.axis_index("tensor")
    wides = lax.axis_size("tensor") // 2
    x_at, core = team // 2, team % 2
    outer = count // inner
    if inner == 2:
        place = jnp.where(index % 2 == 0, index // 2, count - 1 - index // 2)

        def device(p):
            return jnp.where(p < outer, 2 * p, 2 * (count - 1 - p) + 1)
    else:
        place = index

        def device(p):
            return p

    ring_next = ((device((place + 1) % count), team), (device((place + count - 1) % count), team))
    core_next = (index, x_at * 2 + 1 - core)
    x_up = (index, ((x_at + 1) % wides) * 2 + core)
    x_down = (index, ((x_at + wides - 1) % wides) * 2 + core)

    barrier = pltpu.get_barrier_semaphore()

    def greet(hop, carry):
        pl.semaphore_signal(
            barrier, inc=1, device_id=((index + hop) % count, team), device_id_type=mesh_type
        )
        return carry

    lax.fori_loop(1, count, greet, 0)
    for hop in range(1, 2 * wides):
        pl.semaphore_signal(
            barrier,
            inc=1,
            device_id=(index, (team + hop) % (2 * wides)),
            device_id_type=mesh_type,
        )
    pl.semaphore_wait(barrier, count - 1 + 2 * wides - 1)

    def remote(src, dst, sems, at, target):
        return pltpu.make_async_remote_copy(
            src_ref=src,
            dst_ref=dst,
            send_sem=sems.at[(0, *at)],
            recv_sem=sems.at[(1, *at)],
            device_id=target,
            device_id_type=mesh_type,
        )

    sent = []

    def ring(lanes, sems):
        streams = []
        for d, (x_ref, o_ref, first, length, got) in enumerate(lanes):
            chunk = length // count
            halves = 2 if chunk % 32 == 0 else 1
            sub = chunk // halves
            for h in range(halves):
                streams.append((d, h, x_ref, o_ref, first, chunk, sub, got))
        streams.sort(key=lambda one: one[1])

        def rows(stream, hop):
            d, h, _, _, first, chunk, sub, _ = stream
            at = (place + count - hop) % count if d == 0 else (place + hop) % count
            return pl.ds(pl.multiple_of(first + at * chunk + h * sub, 16), sub)

        def copy(stream, step):
            d, h, x_ref, o_ref, _, _, sub, got = stream
            if step < count - 1:
                slot = pl.ds(h * sub, sub)
                src = x_ref.at[rows(stream, 1)] if step == 0 else got.at[step - 1, slot]
                dst = got.at[step, slot]
            else:
                src = dst = o_ref.at[rows(stream, step - (count - 1))]
            return remote(src, dst, sems, (step, d, h), ring_next[d])

        for stream in streams:
            copy(stream, 0).start()
        yield 0
        for step in range(2 * (count - 1)):
            for stream in streams:
                _, h, x_ref, o_ref, _, _, sub, got = stream
                one = copy(stream, step)
                one.wait_recv()
                sent.append(one)
                if step < count - 1:
                    slot = pl.ds(h * sub, sub)
                    total = wide(got[step, slot]) + wide(x_ref[rows(stream, step + 2)])
                    if step < count - 2:
                        got[step, slot] = short(total)
                    else:
                        o_ref[rows(stream, 0)] = short(total)
                if step < 2 * count - 3:
                    copy(stream, step + 1).start()
                yield step

    half = qkvo_ref.shape[0] // 2
    first_ring = ring(
        [
            (down_ref, down_sum_ref, 0, down_ref.shape[0], got_down),
            (up_ref, up_sum_ref, 0, up_ref.shape[0], got_up),
        ],
        ring_sems,
    )
    second_ring = ring(
        [(qkvo_ref, qkvo_sum_ref, 0, half, got_low), (qkvo_ref, qkvo_sum_ref, half, half, got_high)],
        late_sems,
    )

    teams = 2 * wides
    peers = count // teams

    def input_tasks():

        def over_core(i):
            return remote(input_ref.at[wides + i], input_core.at[i], input_core_sems, (i,), core_next)

        def over_x(hop):
            return remote(input_out.at[hop], input_x.at[hop], input_x_sems, (hop,), x_up)

        def over_teams(hop):
            target = (team + hop) % teams
            mine = back.at[pl.ds(team * peers, peers)]
            return remote(stage.at[hop], mine, stage_sems, (hop,), (index, target))

        for i in range(wides - 1, -1, -1):
            over_core(i).start()
        for _ in range(5):
            yield
        for hop in range(wides):
            i = wides - 1 - hop
            over_core(i).wait_recv()
            total = wide(input_ref[i]) + wide(input_core[i])
            if hop > 0:
                over_x(hop - 1).wait_recv()
                total = total + wide(input_x[hop - 1])
            if i > 0:
                input_out[hop] = short(total)
                over_x(hop).start()
                for _ in range(8):
                    yield
            else:
                input_own[...] = short(total + mid_ref[...])
        yield
        part_width = result_ref.shape[2] // teams
        for hop in range(teams):
            columns = pl.ds(pl.multiple_of((team + hop) % teams * part_width, 128), part_width)
            for k, rows_ref in enumerate((result_ref, input_own)):
                stage[hop, :, :, k * part_width : (k + 1) * part_width] = rows_ref[:, :, columns]
            if hop > 0:
                over_teams(hop).start()
            else:
                back[pl.ds(team * peers, peers)] = stage[0]
            yield
        for _ in range(8):
            yield
        for i in range(wides):
            over_core(i).wait_send()
        for hop in range(wides - 1):
            over_x(hop).wait_send()
        for hop in range(1, teams):
            over_teams(hop).wait_recv()
            over_teams(hop).wait_send()

    def give(hop):
        target = (index + hop) % count
        return remote(back.at[target], given_ref.at[index], given_sems, (hop,), (target, team))

    def give_start(hop, carry):
        give(hop).start()
        return carry

    def give_wait(hop, carry):
        give(hop).wait_recv()
        give(hop).wait_send()
        return carry

    is_up, is_down = index == 4, index == 5
    is_gram = jnp.logical_or(is_up, is_down)
    size = up_ref.shape[0]
    pairs = tile_pairs(size // tile)
    share = len(pairs) // 2
    load_up = pltpu.make_async_copy(mom_up_ref, mom_up, load_sem.at[0])
    load_down = pltpu.make_async_copy(mom_down_ref, mom_down, load_sem.at[0])

    def gram_tasks():
        for ref, mom, total, low, load, mine in (
            (mom_up_ref, mom_up, up_sum_ref, up_low, load_up, is_up),
            (mom_down_ref, mom_down, down_sum_ref, down_low, load_down, is_down),
        ):

            @pl.when(mine)
            def _():
                load.wait()

            for start in range(0, ref.shape[0], 256):

                @pl.when(mine)
                def _():
                    rows = pl.ds(start, 256)
                    low[rows, :] = short(momentum_decay * mom[rows, :] + wide(total[rows, :]))

            yield

        def compute(k):
            row = pl.ds(pl.multiple_of(pick([p[0] for p in pairs], k) * tile, tile), tile)
            column = pl.ds(pl.multiple_of(pick([p[1] for p in pairs], k) * tile, tile), tile)

            @pl.when(is_up)
            def _():
                part[k] = mm_nt(up_low[row, :], up_low[column, :])

            @pl.when(is_down)
            def _():
                part[k] = mm_tn(down_low[:, row], down_low[:, column])

        def to_core(i):
            return remote(part.at[(1 - core) * share + i], core_got.at[i], core_sems, (i,), core_next)

        def to_x(i, hop):
            src = chip_sum.at[i] if hop == 0 else x_got.at[hop - 1, i]
            return remote(src, x_got.at[hop, i], x_sems, (hop, i), x_up)

        def to_back(i):
            at = tiles_ref.at[core * share + i]
            return remote(at, at, back_sems, (i,), core_next)

        for i in range(share):
            compute((1 - core) * share + i)

            @pl.when(is_gram)
            def _():
                to_core(i).start()

            yield
        for i in range(share):
            compute(core * share + i)
            yield
        for i in range(share):

            @pl.when(is_gram)
            def _():
                to_core(i).wait_recv()
                chip_sum[i] = part[core * share + i] + core_got[i]
                to_x(i, 0).start()

            yield
        for _ in range(12):
            yield
        for hop in range(wides - 1):
            for i in range(share):

                @pl.when(is_gram)
                def _():
                    to_x(i, hop).wait_recv()
                    before = chip_sum[i] if hop == 0 else tiles_ref[core * share + i]
                    tiles_ref[core * share + i] = before + x_got[hop, i]
                    if hop < wides - 2:
                        to_x(i, hop + 1).start()
                    else:
                        to_back(i).start()

                for _ in range(2):
                    yield

        @pl.when(is_gram)
        def _():
            for i in range(share):
                to_back(i).wait_recv()
                to_core(i).wait_send()
                to_back(i).wait_send()
                for hop in range(wides - 1):
                    to_x(i, hop).wait_send()

    def small_copy(hop):
        return remote(
            small_ref, small_got.at[hop], small_sems, (hop,), ((index + hop) % count, team)
        )

    def small_send(hop, carry):
        small_copy(hop).start()
        return carry

    def small_wait(hop, total):
        one = small_copy(hop)
        one.wait_send()
        one.wait_recv()
        return total + wide(small_got[hop])

    is_column, is_row = index < 3, index == 3
    is_square = index < 4
    width = square_ref.shape[2]
    load_column = pltpu.make_async_copy(
        mom_qkv_ref.at[jnp.minimum(index, 2)], mom_column, load_sem.at[0]
    )
    load_row = pltpu.make_async_copy(mom_out_ref, mom_row, load_sem.at[0])
    square_rows = square_ref.shape[1]
    block = 256
    blocks = square_rows // block

    def square_x(hop, b):
        rows = pl.ds(b * block, block)
        return remote(
            square_ref.at[hop, rows], square_ref.at[hop + 1, rows], square_x_sems, (hop, b), x_down
        )

    def square_core(hop, b):
        rows = pl.ds(b * block, block)
        return remote(
            square_ref.at[hop, rows], square_ref.at[wides + hop, rows], square_core_sems, (hop, b), core_next
        )

    def square_work():
        columns = pl.ds(pl.multiple_of(jnp.minimum(index, 3) * width, 128), width)
        for b in range(blocks):
            rows = pl.ds(b * block, block)
            fresh = wide(qkvo_sum_ref[rows, columns])

            @pl.when(is_column)
            def _():
                if b == 0:
                    load_column.wait()
                square_ref[0, rows] = short(momentum_decay * mom_column[rows, :] + fresh)

            @pl.when(is_row)
            def _():
                if b == 0:
                    load_row.wait()
                square_ref[0, rows] = short(momentum_decay * mom_row[:, rows].T + fresh)

            square_x(0, b).start()
            square_core(0, b).start()
        for hop in range(1, wides):
            for b in range(blocks):
                square_x(hop - 1, b).wait_recv()
                if hop < wides - 1:
                    square_x(hop, b).start()
                square_core(hop, b).start()
        for hop in range(wides):
            for b in range(blocks):
                square_core(hop, b).wait_recv()
        for hop in range(wides):
            for b in range(blocks):
                square_core(hop, b).wait_send()
                if hop < wides - 1:
                    square_x(hop, b).wait_send()

    next(first_ring)
    lax.fori_loop(1, count, small_send, 0)
    for one, mine in (
        (load_up, is_up),
        (load_down, is_down),
        (load_column, is_column),
        (load_row, is_row),
    ):

        @pl.when(mine)
        def _():
            one.start()

    beside = input_tasks()
    for step in first_ring:
        next(beside, None)
        if step >= 2 * count - 6:
            next(second_ring, None)
    for _ in beside:
        pass
    side = gram_tasks()
    for _ in second_ring:
        next(side, None)
    lax.fori_loop(1, count, give_start, 0)
    given_ref[index] = back[index]
    pl.when(is_square)(square_work)
    for _ in side:
        pass
    lax.fori_loop(1, count, give_wait, 0)
    small_sum_ref[...] = lax.fori_loop(1, count, small_wait, wide(small_ref[...]))
    for one in sent:
        one.wait_send()


def sums_over_dp(inner, down, up, qkvo, small, input_part, grad_mid, result, moments_old):
    groups, teams = lax.axis_size("dp"), lax.axis_size("tensor")
    wides = teams // 2
    size, width = qkvo.shape[0], qkvo.shape[1] // 4
    tile = size // 4
    pairs = len(tile_pairs(4))
    steps = 2 * (groups - 1)
    mom_qkv, mom_out, mom_up, mom_down = moments_old
    dma = pltpu.SemaphoreType.DMA
    vmem = pl.BlockSpec(memory_space=pltpu.VMEM)
    length = down.size + up.size + qkvo.size
    peers, rows, model = result.shape
    return pl.pallas_call(
        functools.partial(sum_kernel, inner, tile),
        name="sums_over_dp",
        out_shape=(
            jax.ShapeDtypeStruct(down.shape, bf16),
            jax.ShapeDtypeStruct(up.shape, bf16),
            jax.ShapeDtypeStruct(qkvo.shape, bf16),
            jax.ShapeDtypeStruct(small.shape, f32),
            jax.ShapeDtypeStruct((teams, size, width), bf16),
            jax.ShapeDtypeStruct((pairs, tile, tile), f32),
            jax.ShapeDtypeStruct((groups, rows, 2 * (model // teams)), bf16),
        ),
        in_specs=[vmem] * 7 + [pl.BlockSpec(memory_space=pl.ANY)] * 4,
        out_specs=[vmem] * 7,
        scratch_shapes=[
            pltpu.VMEM((groups - 1, down.shape[0] // groups, down.shape[1]), bf16),
            pltpu.VMEM((groups - 1, up.shape[0] // groups, up.shape[1]), bf16),
            pltpu.VMEM((groups - 1, size // 2 // groups, qkvo.shape[1]), bf16),
            pltpu.VMEM((groups - 1, size // 2 // groups, qkvo.shape[1]), bf16),
            pltpu.VMEM((groups, *small.shape), bf16),
            pltpu.VMEM(up.shape, f32),
            pltpu.VMEM(down.shape, f32),
            pltpu.VMEM((size, width), f32),
            pltpu.VMEM((width, size), f32),
            pltpu.VMEM(up.shape, bf16),
            pltpu.VMEM(down.shape, bf16),
            pltpu.VMEM((pairs, tile, tile), f32),
            pltpu.VMEM((pairs // 2, tile, tile), f32),
            pltpu.VMEM((pairs // 2, tile, tile), f32),
            pltpu.VMEM((wides - 1, pairs // 2, tile, tile), f32),
            dma((2, steps, 2, 2)),
            dma((2, steps, 2, 2)),
            dma((2, groups)),
            dma((1,)),
            dma((2, pairs // 2)),
            dma((2, wides - 1, pairs // 2)),
            dma((2, pairs // 2)),
            dma((2, wides - 1, size // 256)),
            dma((2, wides, size // 256)),
            pltpu.VMEM((wides, peers, rows, model), bf16),
            pltpu.VMEM((wides - 1, peers, rows, model), bf16),
            pltpu.VMEM((wides - 1, peers, rows, model), bf16),
            pltpu.VMEM((peers, rows, model), bf16),
            pltpu.VMEM((teams, peers, rows, 2 * (model // teams)), bf16),
            pltpu.VMEM((groups, rows, 2 * (model // teams)), bf16),
            dma((2, wides)),
            dma((2, wides - 1)),
            dma((2, teams)),
            dma((2, groups)),
        ],
        compiler_params=pltpu.CompilerParams(
            collective_id=0, has_side_effects=True, vmem_limit_bytes=52 * 2**20
        ),
        cost_estimate=pl.CostEstimate(
            flops=length, bytes_accessed=4 * length, transcendentals=0
        ),
    )(
        down, up, qkvo, small, input_part, grad_mid, result, mom_qkv, mom_out, mom_up, mom_down
    )


def dot(left, right):
    return jnp.dot(left, right, preferred_element_type=f32)

def dot_nt(left, right):
    return lax.dot_general(left, right, (((1,), (1,)), ((), ())), preferred_element_type=f32)

def middle_kernel(
    context_ref,
    x_ref,
    out_ref,
    up_ref,
    down_ref,
    bias_ref,
    vectors_ref,
    upstream_ref,
    valid_ref,
    hidden_ref,
    act_ref,
    grad_z_ref,
    grad_pre_ref,
    grad_mid_ref,
    own_grad_mid_ref,
    result_ref,
    vector_sum_ref,
    grad_down_ref,
    grad_up_ref,
    bias_sum_ref,
    slope,
    held,
    core_out,
    core_got,
    x_out,
    x_got,
    normed_one,
    own_hidden,
    normed_two,
    own_grad_z,
    vector_own,
    vector_got,
    core_sems,
    x_sems,
    spread_x_sems,
    spread_core_sems,
    vector_sems,
):
    mesh_type = pl.DeviceIdType.MESH
    index = lax.axis_index("dp")
    team = lax.axis_index("tensor")
    teams = lax.axis_size("tensor")
    wides = teams // 2
    x_at, core = team // 2, team % 2
    core_next = (index, x_at * 2 + 1 - core)
    x_up = (index, ((x_at + 1) % wides) * 2 + core)
    x_down = (index, ((x_at + wides - 1) % wides) * 2 + core)
    barrier = pltpu.get_barrier_semaphore()
    for hop in range(1, teams):
        pl.semaphore_signal(
            barrier, inc=1, device_id=(index, (team + hop) % teams), device_id_type=mesh_type
        )
    pl.semaphore_wait(barrier, teams - 1)
    sent = []

    def remote(src, dst, sems, at, target):
        return pltpu.make_async_remote_copy(
            src_ref=src,
            dst_ref=dst,
            send_sem=sems.at[(0, *at)],
            recv_sem=sems.at[(1, *at)],
            device_id=target,
            device_id_type=mesh_type,
        )

    def start(one):
        one.start()
        sent.append(one)

    def over_core(s, i):
        return remote(core_out.at[s, i], core_got.at[s, i], core_sems, (s, i), core_next)

    def over_x(s, hop):
        return remote(x_out.at[s, hop], x_got.at[s, hop], x_sems, (s, hop), x_up)

    def finish(s, filler):
        for hop in range(wides):
            i = wides - 1 - hop
            over_core(s, i).wait_recv()
            total = held[i] + wide(core_got[s, i])
            if hop > 0:
                if filler is not None:
                    filler()
                    filler = None
                over_x(s, hop - 1).wait_recv()
                total = total + wide(x_got[s, hop - 1])
            if i > 0:
                x_out[s, hop] = short(total)
                start(over_x(s, hop))
        return total

    def along_x(s, ref, i):
        return remote(ref.at[i], ref.at[i + 1], spread_x_sems, (s, i), x_down)

    def across(s, ref, i):
        return remote(ref.at[i], ref.at[wides + i], spread_core_sems, (s, i), core_next)

    def spread(s, ref):
        start(along_x(s, ref, 0))
        start(across(s, ref, 0))

    def arrive(s, ref, i):
        if i > 0:
            along_x(s, ref, i - 1).wait_recv()
            start(across(s, ref, i))
            if i < wides - 1:
                start(along_x(s, ref, i))
        across(s, ref, i).wait_recv()

    share = x_ref.shape[0]

    def pair(ref, i):
        return jnp.concatenate([ref[i], ref[wides + i]], 0)

    def put_pair(ref, i, value):
        ref[i] = value[:share]
        ref[wides + i] = value[share:]

    def keep(s, i, partial):
        core_out[s, i] = short(partial[share:])
        start(over_core(s, i))
        held[i] = partial[:share]

    def sums(value):
        return jnp.sum(value, axis=0, keepdims=True)

    for i in range(wides - 1, -1, -1):
        keep(0, i, dot(pair(context_ref, i), out_ref[...]))
    mid = wide(x_ref[...]) + finish(0, None) + vectors_ref[0:1, :]
    normed, inverse_one, hidden = norm_forward(mid, vectors_ref[1:2, :], vectors_ref[2:3, :])
    normed_one[...] = normed
    own_hidden[...] = hidden
    hidden_ref[0] = short(hidden)
    spread(0, hidden_ref)

    units = up_ref.shape[1]
    step = min(units, 512)
    for i in range(wides):
        arrive(0, hidden_ref, i)
        rows = pair(hidden_ref, i)
        for c in range(0, units, step):
            at = slice(c, c + step)
            pre = dot(rows, up_ref[:, at]) + bias_ref[:, at]
            phi = 0.5 + 0.5 * lax.erf(pre * math.sqrt(0.5))
            act = short(pre * phi)
            bend = phi + pre * jnp.exp(-0.5 * pre * pre) * (1.0 / math.sqrt(2.0 * math.pi))
            for r, part in ((i, slice(0, share)), (wides + i, slice(share, 2 * share))):
                act_ref[r, :, at] = act[part]
                slope[r, :, at] = bend[part]
        keep(1, i, dot(pair(act_ref, i), down_ref[...]))
    summed = own_hidden[...] + finish(1, None) + vectors_ref[3:4, :]
    gain_two = vectors_ref[4:5, :]
    normed, inverse_two, result = norm_forward(summed, gain_two, vectors_ref[5:6, :])
    result_ref[...] = short(result)
    upstream = wide(upstream_ref[...]) * valid_ref[...]
    grad_z = norm_backward(upstream, normed, inverse_two, gain_two)
    own_grad_z[...] = grad_z
    grad_z_ref[0] = short(grad_z)
    spread(1, grad_z_ref)
    vector_own[...] = jnp.zeros_like(vector_own)
    vector_own[3:4, :] = sums(grad_z)
    vector_own[4:5, :] = sums(upstream * normed)
    vector_own[5:6, :] = sums(upstream)

    for i in range(wides):
        arrive(1, grad_z_ref, i)
        rows = pair(grad_z_ref, i)
        for c in range(0, units, step):
            at = slice(c, c + step)
            grad = dot_nt(rows, down_ref[at, :])
            total = jnp.zeros((1, at.stop - at.start), f32)
            for r, part in ((i, slice(0, share)), (wides + i, slice(share, 2 * share))):
                low = short(grad[part] * slope[r, :, at])
                grad_pre_ref[r, :, at] = low
                total = total + sums(wide(low))
            bias_sum_ref[:, at] = total if i == 0 else bias_sum_ref[:, at] + total
        keep(2, i, dot_nt(pair(grad_pre_ref, i), up_ref[...]))

    def every(ref, at):
        return jnp.concatenate([ref[r, :, at] for r in range(teams)], 0)

    def down_filler():
        def one(k, carry):
            at = pl.ds(pl.multiple_of(k * 128, 128), 128)
            grad_down_ref[at, :] = short(mm_tn(every(act_ref, at), every(grad_z_ref, slice(None))))
            return carry

        lax.fori_loop(0, units // 128, one, 0)

    grad_hidden = own_grad_z[...] + finish(2, down_filler)
    grad_mid = norm_backward(grad_hidden, normed_one[...], inverse_one, vectors_ref[1:2, :])
    own_grad_mid_ref[...] = grad_mid
    grad_mid_ref[0] = short(grad_mid)
    spread(2, grad_mid_ref)
    vector_own[0:1, :] = sums(grad_mid)
    vector_own[1:2, :] = sums(grad_hidden * normed_one[...])
    vector_own[2:3, :] = sums(grad_hidden)

    def to_team(hop):
        return remote(
            vector_own, vector_got.at[hop], vector_sems, (hop,), (index, (team + hop) % teams)
        )

    for hop in range(1, teams):
        start(to_team(hop))

    def up_filler(k, carry):
        at = pl.ds(pl.multiple_of(k * 128, 128), 128)
        grad_up_ref[at, :] = short(mm_tn(every(hidden_ref, at), every(grad_pre_ref, slice(None))))
        return carry

    lax.fori_loop(0, hidden_ref.shape[2] // 128, up_filler, 0)
    for i in range(wides):
        arrive(2, grad_mid_ref, i)
    total = vector_own[...]
    for hop in range(1, teams):
        to_team(hop).wait_recv()
        total = total + vector_got[hop]
    vector_sum_ref[...] = total
    for one in sent:
        one.wait_send()


def middle(context, x_own, w_out, w_up, w_down, bias_up, vectors, upstream, valid):
    teams, share, width = context.shape
    model, units = w_up.shape
    wides = teams // 2
    dma = pltpu.SemaphoreType.DMA
    vmem = pl.BlockSpec(memory_space=pltpu.VMEM)
    rows = jax.ShapeDtypeStruct((teams, share, model), bf16)
    inner = jax.ShapeDtypeStruct((teams, share, units), bf16)
    own = pltpu.VMEM((share, model), f32)
    return pl.pallas_call(
        middle_kernel,
        name="middle",
        out_shape=(
            rows,
            inner,
            rows,
            inner,
            rows,
            jax.ShapeDtypeStruct((share, model), f32),
            jax.ShapeDtypeStruct((share, model), bf16),
            jax.ShapeDtypeStruct((8, model), f32),
            jax.ShapeDtypeStruct((units, model), bf16),
            jax.ShapeDtypeStruct((model, units), bf16),
            jax.ShapeDtypeStruct((1, units), f32),
        ),
        in_specs=[vmem] * 9,
        out_specs=[vmem] * 11,
        scratch_shapes=[
            pltpu.VMEM((teams, share, units), f32),
            pltpu.VMEM((wides, share, model), f32),
            pltpu.VMEM((3, wides, share, model), bf16),
            pltpu.VMEM((3, wides, share, model), bf16),
            pltpu.VMEM((3, wides - 1, share, model), bf16),
            pltpu.VMEM((3, wides - 1, share, model), bf16),
            own,
            own,
            own,
            own,
            pltpu.VMEM((8, model), f32),
            pltpu.VMEM((teams, 8, model), f32),
            dma((2, 3, wides)),
            dma((2, 3, wides - 1)),
            dma((2, 3, wides - 1)),
            dma((2, 3, wides)),
            dma((2, teams)),
        ],
        compiler_params=pltpu.CompilerParams(
            collective_id=1, has_side_effects=True, vmem_limit_bytes=48 * 2**20
        ),
        cost_estimate=pl.CostEstimate(
            flops=12 * teams * share * model * units,
            bytes_accessed=8 * model * units,
            transcendentals=0,
        ),
    )(context, x_own, w_out, w_up, w_down, bias_up.reshape(1, units), vectors, upstream, valid)


def polar_kernel(block, m_ref, o_ref, x_ref, gram_ref, low_ref, mix_ref):
    teams, size, width = m_ref.shape
    keep = o_ref.shape[1]
    bits = 256

    def rows(i):
        return pl.ds(pl.multiple_of(i * bits, bits), bits)

    def columns(j):
        return pl.ds(pl.multiple_of(j * block, block), block)

    def norm_step(i, total):
        for r in range(teams):
            part = wide(m_ref[r, rows(i), :])
            total = total + jnp.sum(part * part, axis=0, keepdims=True)
        return total

    total = lax.fori_loop(0, size // bits, norm_step, jnp.zeros((1, width), f32))
    scale = lax.rsqrt(jnp.sum(total, axis=1, keepdims=True) + 1e-07)

    def scale_step(i, carry):
        for r in range(teams):
            x_ref[0, rows(i), r * width : (r + 1) * width] = short(wide(m_ref[r, rows(i), :]) * scale)
        return carry

    lax.fori_loop(0, size // bits, scale_step, 0)

    def sweep(k, carry):
        now = k % 2
        x = x_ref.at[now]

        def gram_step(j, carry):
            gram = dot_nt(x[...], x[columns(j), :])
            gram_ref[:, columns(j)] = gram
            low_ref[:, columns(j)] = short(gram)
            return carry

        def mix_step(j, carry):
            power = dot(low_ref[...], low_ref[:, columns(j)])
            mix_ref[:, columns(j)] = short(coef_two * gram_ref[:, columns(j)] + coef_three * power)
            return carry

        def next_step(j, carry):
            mixed = dot(mix_ref[...], x[:, columns(j)])
            x_ref[1 - now, :, columns(j)] = short(coef_one * wide(x[:, columns(j)]) + mixed)
            return carry

        lax.fori_loop(0, size // block, gram_step, 0)
        lax.fori_loop(0, size // block, mix_step, 0)
        lax.fori_loop(0, jnp.where(k < 4, size // block, -(-keep // block)), next_step, 0)
        return carry

    lax.fori_loop(0, 5, sweep, 0)
    o_ref[...] = x_ref[1, :, :keep]


def factor_kernel(block, g_ref, o_ref, current_ref, poly_ref, half_ref, factor_ref):
    size = poly_ref.shape[0]
    tile = g_ref.shape[1]
    tiles = size // tile
    keep = o_ref.shape[1]
    first = lax.axis_index("tensor") * keep
    eye = lax.broadcasted_iota(jnp.int32, (tile, tile), 0) == lax.broadcasted_iota(
        jnp.int32, (tile, tile), 1
    )
    trace = jnp.zeros((1, 1), f32)
    for k, (i, j) in enumerate(tile_pairs(tiles)):
        if i == j:
            diagonal = jnp.where(eye, g_ref[k], 0.0)
            trace = trace + jnp.sum(jnp.sum(diagonal, axis=0, keepdims=True), axis=1, keepdims=True)
    scale = lax.rsqrt(trace + 1e-07)
    scale_two = scale * scale

    def store(slot, rows, columns, value):
        high = short(value)
        current_ref[slot, 0, rows, columns] = high
        current_ref[slot, 1, rows, columns] = short(value - wide(high))

    def span(i):
        return slice(i * tile, (i + 1) * tile)

    for k, (i, j) in enumerate(tile_pairs(tiles)):
        part = g_ref[k] * scale_two
        store(0, span(i), span(j), part)
        if i != j:
            store(0, span(j), span(i), part.T)

    def cols(j):
        return pl.ds(pl.multiple_of(j * block, block), block)

    def sweep(k, exact, exact_next, last):
        now = k % 2
        high_ref, low_ref = current_ref.at[now, 0], current_ref.at[now, 1]

        def poly_step(j, carry):
            power = dot(high_ref[...], high_ref[:, cols(j)])
            if last:
                power = power + dot(high_ref[...], low_ref[:, cols(j)])
            r = lax.broadcasted_iota(jnp.int32, (size, block), 0)
            c = lax.broadcasted_iota(jnp.int32, (size, block), 1) + j * block
            present = wide(high_ref[:, cols(j)]) + wide(low_ref[:, cols(j)])
            poly = coef_two * present + coef_three * power
            poly_ref[:, cols(j)] = short(poly + jnp.where(r == c, coef_one, 0.0))
            return carry

        def half_step(j, carry):
            half = dot(poly_ref[...], high_ref[:, cols(j)])
            if exact:
                half = half + dot(poly_ref[...], low_ref[:, cols(j)])
            high = short(half)
            half_ref[0, :, cols(j)] = high
            if exact_next:
                half_ref[1, :, cols(j)] = short(half - wide(high))
            return carry

        def next_step(j, carry):
            new = dot(half_ref[0], poly_ref[:, cols(j)])
            if exact_next:
                new = new + dot(half_ref[1], poly_ref[:, cols(j)])
            store(1 - now, slice(None), cols(j), new)
            return carry

        lax.fori_loop(0, size // block, poly_step, 0)
        if not last:
            lax.fori_loop(0, size // block, half_step, 0)
            lax.fori_loop(0, size // block, next_step, 0)

    def plain_sweep(k, carry):
        sweep(k, False, False, False)
        factor_ref[...] = short(dot(poly_ref[...], factor_ref[...]))
        return carry

    sweep(0, True, True, False)
    factor_ref[...] = poly_ref[:, pl.ds(pl.multiple_of(first, 128), keep)]
    sweep(1, True, False, False)
    factor_ref[...] = short(dot(poly_ref[...], factor_ref[...]))
    lax.fori_loop(2, 4, plain_sweep, 0)
    sweep(4, False, False, True)
    o_ref[...] = short(dot(poly_ref[...], factor_ref[...]) * scale)


def step_kernel(
    block,
    square_ref,
    tiles_ref,
    o_ref,
    x_ref,
    gram_ref,
    low_ref,
    mix_ref,
    current_ref,
    poly_ref,
    half_ref,
    factor_ref,
):
    index = lax.axis_index("dp")

    @pl.when(index < 4)
    def _():
        polar_kernel(block, square_ref, o_ref, x_ref, gram_ref, low_ref, mix_ref)

    @pl.when(jnp.logical_or(index == 4, index == 5))
    def _():
        factor_kernel(block, tiles_ref, o_ref, current_ref, poly_ref, half_ref, factor_ref)

    @pl.when(index > 5)
    def _():
        o_ref[...] = jnp.zeros_like(o_ref)


def orthogonal_columns(square, tiles):
    teams, size, width = square.shape
    vmem = pl.BlockSpec(memory_space=pltpu.VMEM)
    return pl.pallas_call(
        functools.partial(step_kernel, 512),
        name="orthogonal_columns",
        out_shape=jax.ShapeDtypeStruct((size, width), bf16),
        in_specs=[vmem] * 2,
        out_specs=vmem,
        scratch_shapes=[
            pltpu.VMEM((2, size, teams * width), bf16),
            pltpu.VMEM((size, size), f32),
            pltpu.VMEM((size, size), bf16),
            pltpu.VMEM((size, size), bf16),
            pltpu.VMEM((2, 2, size, size), bf16),
            pltpu.VMEM((size, size), bf16),
            pltpu.VMEM((2, size, size), bf16),
            pltpu.VMEM((size, width), bf16),
        ],
        compiler_params=pltpu.CompilerParams(vmem_limit_bytes=48 * 2**20),
        cost_estimate=pl.CostEstimate(
            flops=40 * size**3, bytes_accessed=8 * size * size, transcendentals=0
        ),
    )(square, tiles)


def body(
    layout,
    tokens,
    cotangent,
    lengths,
    packing,
    w_qkv,
    w_out,
    w_up,
    w_down,
    bias_qv,
    bias_up,
    vectors,
    mom_qkv,
    mom_out,
    mom_up,
    mom_down,
    mom_bias_qv,
    mom_bias_up,
    mom_vectors,
):
    inner, cores = layout
    groups = lax.axis_size("dp")
    teams = lax.axis_size("tensor")
    group = lax.axis_index("dp")
    team = lax.axis_index("tensor")
    outer, wides = groups // inner, teams // cores
    count = tokens.shape[0]
    per_peer = count // groups
    share = count // teams
    width = D // teams
    all_tokens = count * groups

    outer_ring = Ring("dp", (outer, inner), 0)
    inner_ring = Ring("dp", (outer, inner), 1)
    outer_at, inner_at = outer_ring.place(group), inner_ring.place(group)
    x_ring = Ring("tensor", (wides, cores), 0)
    core_ring = Ring("tensor", (wides, cores), 1)
    x_at, core_at = x_ring.place(team), core_ring.place(team)

    def team_of(rank):
        return ((x_at + rank % wides) % wides) * cores + (core_at + rank // wides) % cores

    def to_relative(value, size, axis=0):
        return jnp.concatenate([cut(value, team_of(r), size, axis) for r in range(teams)], axis)

    def to_given(value, size, axis=0):
        parts = []
        for other in range(teams):
            rank = ((other % cores - core_at) % cores) * wides + (other // cores - x_at) % wides
            parts.append(cut(value, rank, size, axis))
        return jnp.concatenate(parts, axis)

    def spread_list(piece, ring_x=x_ring, ring_core=core_ring):
        line = [piece]
        for _ in range(wides - 1):
            line.append(ring_x.send(line[-1], -1))
        pieces = list(line)
        for hop in range(1, cores):
            pieces += [ring_core.send(p, -hop) for p in line]
        return pieces

    def spread_columns(piece):
        return to_given(jnp.concatenate(spread_list(piece), 1), piece.shape[1], 1)

    def own_rows(value):
        return cut(value, team, share, 0)

    position = jnp.arange(count, dtype=jnp.int32)
    peer = jnp.arange(groups, dtype=jnp.int32)
    packed = packing.reshape(groups, count)
    mine_packed = lax.dynamic_index_in_dim(packed, group, 0, keepdims=False)
    offset = packed - group * count
    offset_mine = mine_packed[None, :] - peer[:, None] * count
    masks = jnp.concatenate(
        [
            jnp.logical_and(offset >= 0, offset < count),
            jnp.logical_and(offset_mine >= 0, offset_mine < count),
        ],
        0,
    )
    before = (position[:, None] < position[None, :]).astype(bf16)
    rank = mm(masks.astype(bf16), before).astype(jnp.int32)
    key = jnp.where(masks, rank, -1)
    value = jnp.concatenate(
        [offset, jnp.broadcast_to(position[None, :], (groups, count))], 0
    )
    slot_in_message = jnp.arange(per_peer, dtype=jnp.int32)
    picked = jnp.sum(
        jnp.where(key[:, None, :] == slot_in_message[None, :, None], value[:, None, :], 0), axis=-1
    )
    rows_sent = picked[:groups].reshape(count)
    slots = picked[groups:].reshape(count)
    choose = (rows_sent[:, None] == position[None, :]).astype(bf16)

    length_row = lengths[0]
    end_one = length_row[0]
    end_two = end_one + length_row[1]
    end_all = end_two + length_row[2]
    segments = (
        (slots >= end_one).astype(jnp.int32)
        + (slots >= end_two).astype(jnp.int32)
        + (slots >= end_all).astype(jnp.int32)
        + jnp.maximum(slots - end_all, 0)
    )
    valid_own = own_rows((slots < end_all).astype(f32))
    segments = to_relative(segments, share)

    own_columns = jnp.concatenate([cut(tokens, team, width, 1), cut(cotangent, team, width, 1)], 1)
    sent = short(mm(choose, own_columns)).reshape(groups, per_peer, 2 * width)
    got = lax.all_to_all(sent, "dp", split_axis=0, concat_axis=0, tiled=True)
    got = got.reshape(count, 2 * width)

    packed_x = to_relative(spread_columns(got[:, :width]), share)
    turns = []
    for hop in range(teams):
        block = cut(got[:, width:], (team + hop) % teams, share, 0)
        if hop > 0:
            block = lax.ppermute(block, "tensor", [(i, (i + hop) % teams) for i in range(teams)])
        turns.append(block)
    turns = jnp.concatenate(turns, 1)
    grad_rows = jnp.concatenate(
        [cut(turns, (team - other) % teams, width, 1) for other in range(teams)], 1
    )

    wqkv_low = short(w_qkv)
    wout_low = short(w_out)
    wup_low = short(w_up)
    wdown_low = short(w_down)
    heads = width // HEAD
    score_scale = HEAD ** (-0.5)
    queries = short(mm(packed_x, wqkv_low[0]) + bias_qv[0]).reshape(count, heads, HEAD)
    keys = short(mm(packed_x, wqkv_low[1])).reshape(count, heads, HEAD)
    values = short(mm(packed_x, wqkv_low[2]) + bias_qv[1]).reshape(count, heads, HEAD)
    raw = jnp.einsum("qhd,khd->hqk", queries, keys, preferred_element_type=f32)
    same = segments[:, None] == segments[None, :]
    masked = jnp.where(same[None], raw * score_scale, masked_score)
    exponent = jnp.exp(masked - jnp.max(masked, axis=-1, keepdims=True))
    probs = exponent / jnp.sum(exponent, axis=-1, keepdims=True)
    probs_low = short(probs)
    context = short(
        jnp.einsum("hqk,khd->qhd", probs_low, values, preferred_element_type=f32)
    ).reshape(count, width)
    (
        hidden_low,
        act_low,
        grad_z_low,
        grad_pre,
        grad_mid_low,
        grad_mid,
        result,
        vector_part,
        grad_down,
        grad_up,
        grad_bias_up,
    ) = middle(
        context.reshape(teams, share, width),
        packed_x[:share],
        wout_low,
        wup_low,
        wdown_low,
        bias_up,
        vectors,
        grad_rows,
        valid_own[:, None],
    )
    grad_bias_up = grad_bias_up[0]
    grad_mid_low = grad_mid_low.reshape(count, D)
    vector_part = vector_part[:6]
    grad_out_t = short(mm_tn(grad_mid_low, context))
    grad_context = short(mm_nt(grad_mid_low, wout_low)).reshape(count, heads, HEAD)
    grad_probs = jnp.einsum("qhd,khd->hqk", grad_context, values, preferred_element_type=f32)
    weighted = jnp.sum(probs * grad_probs, axis=-1, keepdims=True)
    grad_scores = short(probs * (grad_probs - weighted))
    grad_values = short(
        jnp.einsum("hqk,qhd->khd", probs_low, grad_context, preferred_element_type=f32)
    ).reshape(count, width)
    grad_keys = short(
        jnp.einsum("hqk,qhd->khd", grad_scores, queries, preferred_element_type=f32) * score_scale
    ).reshape(count, width)
    grad_queries = short(
        jnp.einsum("hqk,khd->qhd", grad_scores, keys, preferred_element_type=f32) * score_scale
    ).reshape(count, width)
    grad_bias_pair = jnp.stack(
        [jnp.sum(grad_queries, axis=0, dtype=f32), jnp.sum(grad_values, axis=0, dtype=f32)]
    )
    grad_projected = jnp.concatenate([grad_queries, grad_keys, grad_values], 1)
    grad_qkvo = jnp.concatenate(
        [
            short(mm_tn(packed_x, grad_projected)),
            grad_out_t,
        ],
        1,
    )
    input_part = mm_nt(grad_projected, jnp.concatenate([wqkv_low[k] for k in range(3)], 1))
    columns = D
    small = jnp.concatenate(
        [vector_part.reshape(-1), grad_bias_pair.reshape(-1), grad_bias_up.reshape(-1)]
    )
    rows_small = -(-small.size // (16 * columns)) * 16
    small = jnp.pad(short(small), (0, rows_small * columns - small.size)).reshape(rows_small, columns)
    down_sum, up_sum, qkvo_sum, small_sum, square, gram_tiles, given = sums_over_dp(
        inner,
        grad_down,
        grad_up,
        grad_qkvo,
        small,
        short(input_part).reshape(teams, groups // teams, per_peer, D),
        grad_mid.reshape(groups // teams, per_peer, D),
        result.reshape(groups // teams, per_peer, D),
        (mom_qkv, mom_out, mom_up, mom_down),
    )
    pieces = spread_list(short(mm_tn(choose, given.reshape(count, 2 * width))))
    output = to_given(jnp.concatenate([p[:, :width] for p in pieces], 1), width, 1)
    grad_tokens = wide(to_given(jnp.concatenate([p[:, width:] for p in pieces], 1), width, 1))

    qkvo_sum = wide(qkvo_sum)
    small_sum = small_sum.reshape(-1)
    gradients = (
        jnp.stack([qkvo_sum[:, k * width : (k + 1) * width] for k in range(3)]),
        qkvo_sum[:, 3 * width :].T,
        wide(up_sum),
        wide(down_sum),
        small_sum[6 * D : 6 * D + 2 * width].reshape(2, width),
        small_sum[6 * D + 2 * width : 6 * D + 2 * width + bias_up.shape[0]],
        small_sum[: 6 * D].reshape(6, D),
    )
    moments_old = (mom_qkv, mom_out, mom_up, mom_down, mom_bias_qv, mom_bias_up, mom_vectors)
    moments = tuple(
        momentum_decay * old + grad for old, grad in zip(moments_old, gradients)
    )

    up_low, down_low = short(moments[2]), short(moments[3])

    stepped = orthogonal_columns(square, gram_tiles)
    dp_rows = D // groups
    steps = lax.all_to_all(
        stepped.reshape(groups, dp_rows, width), "dp", split_axis=0, concat_axis=0, tiled=True
    )
    factors = spread_columns(steps[4:6].reshape(2 * dp_rows, width))

    def mine(values_, dim):
        return lax.dynamic_slice_in_dim(values_, group * dp_rows, dp_rows, dim)

    short_rate = rate_matrix * 0.2 * math.sqrt(D)
    long_rate = rate_matrix * 0.2 * math.sqrt(w_up.shape[1] * teams)
    masters = [
        mine(w_qkv, 1) - short_rate * wide(steps[:3]),
        mine(w_out, 1) - short_rate * wide(steps[3]).T,
        mine(w_up, 0) - long_rate * mm(factors[:dp_rows], up_low),
        mine(w_down, 1) - long_rate * mm_nt(down_low, factors[dp_rows:]),
    ]
    rate_vector = 0.2 / math.sqrt(all_tokens)
    for param, moment in zip((bias_qv, bias_up, vectors), moments[4:]):
        masters.append(param - rate_vector * moment)

    return (output, grad_tokens, *gradients, *moments, *masters)


def axis_layout(mesh):
    grid = mesh.devices
    groups, teams = grid.shape
    places = [getattr(d, "coords", None) for d in grid[:, 0]]
    inner = 2 if groups % 2 == 0 else 1
    if places[0] is not None:
        moved = [k for k in range(3) if places[0][k] != places[1][k]]
        fixed = [k for k in range(3) if k not in moved]
        inner = 1
        while inner < groups and all(places[inner][k] == places[0][k] for k in fixed):
            inner += 1
        if groups % inner:
            inner = 1
    return inner, (2 if teams % 2 == 0 else 1)


def solution(mesh):
    grads = (
        P(None, None, "tensor"),
        P("tensor", None),
        P(None, "tensor"),
        P("tensor", None),
        P(None, "tensor"),
        P("tensor"),
        P(),
    )
    rows = P("dp", None)
    return jax.shard_map(
        functools.partial(body, axis_layout(mesh)),
        mesh=mesh,
        in_specs=(rows, rows, rows, P(), *grads, *grads),
        out_specs=(
            rows,
            rows,
            *grads,
            *grads,
            P(None, "dp", "tensor"),
            P("tensor", "dp"),
            P("dp", "tensor"),
            P("tensor", "dp"),
            P(None, "tensor"),
            P("tensor"),
            P(),
        ),
        check_vma=False,
    )
```

```python
import functools
import math

import jax
import jax.numpy as jnp
from jax import lax
from jax.experimental import pallas as pl
from jax.experimental.pallas import tpu as pltpu
from jax.sharding import PartitionSpec as P

D = 1024
HEAD = 64

eps_norm = 1e-05
coef_one = 3.4445
coef_two = -4.775
coef_three = 2.0315
momentum_decay = 0.9
rate_matrix = 0.1
masked_score = -1000000000.0
bf16 = jnp.bfloat16
f32 = jnp.float32


def short(value):
    return value.astype(bf16)


def wide(value):
    return value.astype(f32)


def mm(left, right):
    return jnp.dot(short(left), short(right), preferred_element_type=f32)


def mm_nt(left, right):
    return lax.dot_general(
        short(left), short(right), (((1,), (1,)), ((), ())), preferred_element_type=f32
    )


def mm_tn(left, right):
    return lax.dot_general(
        short(left), short(right), (((0,), (0,)), ((), ())), preferred_element_type=f32
    )


def norm_forward(values, gain_row, shift_row):
    average = jnp.mean(values, axis=-1, keepdims=True)
    centred = values - average
    variance = jnp.mean(centred * centred, axis=-1, keepdims=True)
    inverse = lax.rsqrt(variance + eps_norm)
    normed = centred * inverse
    return (normed, inverse, normed * gain_row + shift_row)


def norm_backward(upstream, normed, inverse, gain_row):
    scaled = upstream * gain_row
    centre_term = jnp.mean(scaled, axis=-1, keepdims=True)
    slope_term = jnp.mean(scaled * normed, axis=-1, keepdims=True)
    return inverse * (scaled - centre_term - normed * slope_term)


class Ring:
    def __init__(self, axes, sizes, digit, members=None):
        self.axes = axes
        self.count = sizes[digit]
        self.below = math.prod(sizes[digit + 1 :])
        self.total = math.prod(sizes)
        self.members = members

    def send(self, value, offset):
        count, below = self.count, self.below
        pairs = []
        for i in range(self.total):
            if self.members is not None and not self.members(i):
                continue
            at = (i // below) % count
            pairs.append((i, i + ((at + offset) % count - at) * below))
        return lax.ppermute(value, self.axes, pairs)

    def place(self, linear):
        return (linear // self.below) % self.count


def cut(value, index, size, axis):
    return lax.dynamic_slice_in_dim(value, index * size, size, axis)


def tile_pairs(tiles):
    return [(i, j) for i in range(tiles) for j in range(i, tiles)]


def pick(options, index):
    chosen = jnp.int32(options[0])
    for k in range(1, len(options)):
        chosen = jnp.where(index == k, jnp.int32(options[k]), chosen)
    return chosen


def sum_kernel(
    inner,
    tile,
    down_ref,
    up_ref,
    qkvo_ref,
    small_ref,
    input_ref,
    mid_ref,
    result_ref,
    mom_qkv_ref,
    mom_out_ref,
    mom_up_ref,
    mom_down_ref,
    down_sum_ref,
    up_sum_ref,
    qkvo_sum_ref,
    small_sum_ref,
    square_ref,
    tiles_ref,
    given_ref,
    got_down,
    got_up,
    got_low,
    got_high,
    small_got,
    mom_up,
    mom_down,
    mom_column,
    mom_row,
    up_low,
    down_low,
    part,
    core_got,
    chip_sum,
    x_got,
    ring_sems,
    late_sems,
    small_sems,
    load_sem,
    core_sems,
    x_sems,
    back_sems,
    square_x_sems,
    square_core_sems,
    input_core,
    input_x,
    input_out,
    input_own,
    stage,
    back,
    input_core_sems,
    input_x_sems,
    stage_sems,
    given_sems,
):
    mesh_type = pl.DeviceIdType.MESH
    count = lax.axis_size("dp")
    index = lax.axis_index("dp")
    team = lax.axis_index("tensor")
    wides = lax.axis_size("tensor") // 2
    x_at, core = team // 2, team % 2
    outer = count // inner
    if inner == 2:
        place = jnp.where(index % 2 == 0, index // 2, count - 1 - index // 2)

        def device(p):
            return jnp.where(p < outer, 2 * p, 2 * (count - 1 - p) + 1)
    else:
        place = index

        def device(p):
            return p

    ring_next = ((device((place + 1) % count), team), (device((place + count - 1) % count), team))
    core_next = (index, x_at * 2 + 1 - core)
    x_up = (index, ((x_at + 1) % wides) * 2 + core)
    x_down = (index, ((x_at + wides - 1) % wides) * 2 + core)

    barrier = pltpu.get_barrier_semaphore()

    def greet(hop, carry):
        pl.semaphore_signal(
            barrier, inc=1, device_id=((index + hop) % count, team), device_id_type=mesh_type
        )
        return carry

    lax.fori_loop(1, count, greet, 0)
    for hop in range(1, 2 * wides):
        pl.semaphore_signal(
            barrier,
            inc=1,
            device_id=(index, (team + hop) % (2 * wides)),
            device_id_type=mesh_type,
        )
    pl.semaphore_wait(barrier, count - 1 + 2 * wides - 1)

    def remote(src, dst, sems, at, target):
        return pltpu.make_async_remote_copy(
            src_ref=src,
            dst_ref=dst,
            send_sem=sems.at[(0, *at)],
            recv_sem=sems.at[(1, *at)],
            device_id=target,
            device_id_type=mesh_type,
        )

    sent = []

    def ring(lanes, sems):
        streams = []
        for d, (x_ref, o_ref, first, length, got) in enumerate(lanes):
            chunk = length // count
            halves = 2 if chunk % 32 == 0 else 1
            sub = chunk // halves
            for h in range(halves):
                streams.append((d, h, x_ref, o_ref, first, chunk, sub, got))
        streams.sort(key=lambda one: one[1])

        def rows(stream, hop):
            d, h, _, _, first, chunk, sub, _ = stream
            at = (place + count - hop) % count if d == 0 else (place + hop) % count
            return pl.ds(pl.multiple_of(first + at * chunk + h * sub, 16), sub)

        def copy(stream, step):
            d, h, x_ref, o_ref, _, _, sub, got = stream
            if step < count - 1:
                slot = pl.ds(h * sub, sub)
                src = x_ref.at[rows(stream, 1)] if step == 0 else got.at[step - 1, slot]
                dst = got.at[step, slot]
            else:
                src = dst = o_ref.at[rows(stream, step - (count - 1))]
            return remote(src, dst, sems, (step, d, h), ring_next[d])

        for stream in streams:
            copy(stream, 0).start()
        yield 0
        for step in range(2 * (count - 1)):
            for stream in streams:
                _, h, x_ref, o_ref, _, _, sub, got = stream
                one = copy(stream, step)
                one.wait_recv()
                sent.append(one)
                if step < count - 1:
                    slot = pl.ds(h * sub, sub)
                    total = wide(got[step, slot]) + wide(x_ref[rows(stream, step + 2)])
                    if step < count - 2:
                        got[step, slot] = short(total)
                    else:
                        o_ref[rows(stream, 0)] = short(total)
                if step < 2 * count - 3:
                    copy(stream, step + 1).start()
                yield step

    half = qkvo_ref.shape[0] // 2
    first_ring = ring(
        [
            (down_ref, down_sum_ref, 0, down_ref.shape[0], got_down),
            (up_ref, up_sum_ref, 0, up_ref.shape[0], got_up),
        ],
        ring_sems,
    )
    second_ring = ring(
        [(qkvo_ref, qkvo_sum_ref, 0, half, got_low), (qkvo_ref, qkvo_sum_ref, half, half, got_high)],
        late_sems,
    )

    teams = 2 * wides
    peers = count // teams

    def input_tasks():

        def over_core(i):
            return remote(input_ref.at[wides + i], input_core.at[i], input_core_sems, (i,), core_next)

        def over_x(hop):
            return remote(input_out.at[hop], input_x.at[hop], input_x_sems, (hop,), x_up)

        def over_teams(hop):
            target = (team + hop) % teams
            mine = back.at[pl.ds(team * peers, peers)]
            return remote(stage.at[hop], mine, stage_sems, (hop,), (index, target))

        for i in range(wides - 1, -1, -1):
            over_core(i).start()
        for _ in range(5):
            yield
        for hop in range(wides):
            i = wides - 1 - hop
            over_core(i).wait_recv()
            total = wide(input_ref[i]) + wide(input_core[i])
            if hop > 0:
                over_x(hop - 1).wait_recv()
                total = total + wide(input_x[hop - 1])
            if i > 0:
                input_out[hop] = short(total)
                over_x(hop).start()
                for _ in range(8):
                    yield
            else:
                input_own[...] = short(total + mid_ref[...])
        yield
        part_width = result_ref.shape[2] // teams
        for hop in range(teams):
            columns = pl.ds(pl.multiple_of((team + hop) % teams * part_width, 128), part_width)
            for k, rows_ref in enumerate((result_ref, input_own)):
                stage[hop, :, :, k * part_width : (k + 1) * part_width] = rows_ref[:, :, columns]
            if hop > 0:
                over_teams(hop).start()
            else:
                back[pl.ds(team * peers, peers)] = stage[0]
            yield
        for _ in range(8):
            yield
        for i in range(wides):
            over_core(i).wait_send()
        for hop in range(wides - 1):
            over_x(hop).wait_send()
        for hop in range(1, teams):
            over_teams(hop).wait_recv()
            over_teams(hop).wait_send()

    def give(hop):
        target = (index + hop) % count
        return remote(back.at[target], given_ref.at[index], given_sems, (hop,), (target, team))

    def give_start(hop, carry):
        give(hop).start()
        return carry

    def give_wait(hop, carry):
        give(hop).wait_recv()
        give(hop).wait_send()
        return carry

    is_up, is_down = index == 4, index == 5
    is_gram = jnp.logical_or(is_up, is_down)
    size = up_ref.shape[0]
    pairs = tile_pairs(size // tile)
    share = len(pairs) // 2
    load_up = pltpu.make_async_copy(mom_up_ref, mom_up, load_sem.at[0])
    load_down = pltpu.make_async_copy(mom_down_ref, mom_down, load_sem.at[0])

    def gram_tasks():
        for ref, mom, total, low, load, mine in (
            (mom_up_ref, mom_up, up_sum_ref, up_low, load_up, is_up),
            (mom_down_ref, mom_down, down_sum_ref, down_low, load_down, is_down),
        ):

            @pl.when(mine)
            def _():
                load.wait()

            for start in range(0, ref.shape[0], 256):

                @pl.when(mine)
                def _():
                    rows = pl.ds(start, 256)
                    low[rows, :] = short(momentum_decay * mom[rows, :] + wide(total[rows, :]))

            yield

        def compute(k):
            row = pl.ds(pl.multiple_of(pick([p[0] for p in pairs], k) * tile, tile), tile)
            column = pl.ds(pl.multiple_of(pick([p[1] for p in pairs], k) * tile, tile), tile)

            @pl.when(is_up)
            def _():
                part[k] = mm_nt(up_low[row, :], up_low[column, :])

            @pl.when(is_down)
            def _():
                part[k] = mm_tn(down_low[:, row], down_low[:, column])

        def to_core(i):
            return remote(part.at[(1 - core) * share + i], core_got.at[i], core_sems, (i,), core_next)

        def to_x(i, hop):
            src = chip_sum.at[i] if hop == 0 else x_got.at[hop - 1, i]
            return remote(src, x_got.at[hop, i], x_sems, (hop, i), x_up)

        def to_back(i):
            at = tiles_ref.at[core * share + i]
            return remote(at, at, back_sems, (i,), core_next)

        for i in range(share):
            compute((1 - core) * share + i)

            @pl.when(is_gram)
            def _():
                to_core(i).start()

            yield
        for i in range(share):
            compute(core * share + i)
            yield
        for i in range(share):

            @pl.when(is_gram)
            def _():
                to_core(i).wait_recv()
                chip_sum[i] = part[core * share + i] + core_got[i]
                to_x(i, 0).start()

            yield
        for _ in range(12):
            yield
        for hop in range(wides - 1):
            for i in range(share):

                @pl.when(is_gram)
                def _():
                    to_x(i, hop).wait_recv()
                    before = chip_sum[i] if hop == 0 else tiles_ref[core * share + i]
                    tiles_ref[core * share + i] = before + x_got[hop, i]
                    if hop < wides - 2:
                        to_x(i, hop + 1).start()
                    else:
                        to_back(i).start()

                for _ in range(2):
                    yield

        @pl.when(is_gram)
        def _():
            for i in range(share):
                to_back(i).wait_recv()
                to_core(i).wait_send()
                to_back(i).wait_send()
                for hop in range(wides - 1):
                    to_x(i, hop).wait_send()

    def small_copy(hop):
        return remote(
            small_ref, small_got.at[hop], small_sems, (hop,), ((index + hop) % count, team)
        )

    def small_send(hop, carry):
        small_copy(hop).start()
        return carry

    def small_wait(hop, total):
        one = small_copy(hop)
        one.wait_send()
        one.wait_recv()
        return total + wide(small_got[hop])

    is_column, is_row = index < 3, index == 3
    is_square = index < 4
    width = square_ref.shape[2]
    load_column = pltpu.make_async_copy(
        mom_qkv_ref.at[jnp.minimum(index, 2)], mom_column, load_sem.at[0]
    )
    load_row = pltpu.make_async_copy(mom_out_ref, mom_row, load_sem.at[0])
    square_rows = square_ref.shape[1]
    block = 256
    blocks = square_rows // block

    def square_x(hop, b):
        rows = pl.ds(b * block, block)
        return remote(
            square_ref.at[hop, rows], square_ref.at[hop + 1, rows], square_x_sems, (hop, b), x_down
        )

    def square_core(hop, b):
        rows = pl.ds(b * block, block)
        return remote(
            square_ref.at[hop, rows], square_ref.at[wides + hop, rows], square_core_sems, (hop, b), core_next
        )

    def square_work():
        columns = pl.ds(pl.multiple_of(jnp.minimum(index, 3) * width, 128), width)
        for b in range(blocks):
            rows = pl.ds(b * block, block)
            fresh = wide(qkvo_sum_ref[rows, columns])

            @pl.when(is_column)
            def _():
                if b == 0:
                    load_column.wait()
                square_ref[0, rows] = short(momentum_decay * mom_column[rows, :] + fresh)

            @pl.when(is_row)
            def _():
                if b == 0:
                    load_row.wait()
                square_ref[0, rows] = short(momentum_decay * mom_row[:, rows].T + fresh)

            square_x(0, b).start()
            square_core(0, b).start()
        for hop in range(1, wides):
            for b in range(blocks):
                square_x(hop - 1, b).wait_recv()
                if hop < wides - 1:
                    square_x(hop, b).start()
                square_core(hop, b).start()
        for hop in range(wides):
            for b in range(blocks):
                square_core(hop, b).wait_recv()
        for hop in range(wides):
            for b in range(blocks):
                square_core(hop, b).wait_send()
                if hop < wides - 1:
                    square_x(hop, b).wait_send()

    next(first_ring)
    lax.fori_loop(1, count, small_send, 0)
    for one, mine in (
        (load_up, is_up),
        (load_down, is_down),
        (load_column, is_column),
        (load_row, is_row),
    ):

        @pl.when(mine)
        def _():
            one.start()

    beside = input_tasks()
    for step in first_ring:
        next(beside, None)
        if step >= 2 * count - 6:
            next(second_ring, None)
    for _ in beside:
        pass
    side = gram_tasks()
    for _ in second_ring:
        next(side, None)
    lax.fori_loop(1, count, give_start, 0)
    given_ref[index] = back[index]
    pl.when(is_square)(square_work)
    for _ in side:
        pass
    lax.fori_loop(1, count, give_wait, 0)
    small_sum_ref[...] = lax.fori_loop(1, count, small_wait, wide(small_ref[...]))
    for one in sent:
        one.wait_send()


def sums_over_dp(inner, down, up, qkvo, small, input_part, grad_mid, result, moments_old):
    groups, teams = lax.axis_size("dp"), lax.axis_size("tensor")
    wides = teams // 2
    size, width = qkvo.shape[0], qkvo.shape[1] // 4
    tile = size // 4
    pairs = len(tile_pairs(4))
    steps = 2 * (groups - 1)
    mom_qkv, mom_out, mom_up, mom_down = moments_old
    dma = pltpu.SemaphoreType.DMA
    vmem = pl.BlockSpec(memory_space=pltpu.VMEM)
    length = down.size + up.size + qkvo.size
    peers, rows, model = result.shape
    return pl.pallas_call(
        functools.partial(sum_kernel, inner, tile),
        name="sums_over_dp",
        out_shape=(
            jax.ShapeDtypeStruct(down.shape, bf16),
            jax.ShapeDtypeStruct(up.shape, bf16),
            jax.ShapeDtypeStruct(qkvo.shape, bf16),
            jax.ShapeDtypeStruct(small.shape, f32),
            jax.ShapeDtypeStruct((teams, size, width), bf16),
            jax.ShapeDtypeStruct((pairs, tile, tile), f32),
            jax.ShapeDtypeStruct((groups, rows, 2 * (model // teams)), bf16),
        ),
        in_specs=[vmem] * 7 + [pl.BlockSpec(memory_space=pl.ANY)] * 4,
        out_specs=[vmem] * 7,
        scratch_shapes=[
            pltpu.VMEM((groups - 1, down.shape[0] // groups, down.shape[1]), bf16),
            pltpu.VMEM((groups - 1, up.shape[0] // groups, up.shape[1]), bf16),
            pltpu.VMEM((groups - 1, size // 2 // groups, qkvo.shape[1]), bf16),
            pltpu.VMEM((groups - 1, size // 2 // groups, qkvo.shape[1]), bf16),
            pltpu.VMEM((groups, *small.shape), bf16),
            pltpu.VMEM(up.shape, f32),
            pltpu.VMEM(down.shape, f32),
            pltpu.VMEM((size, width), f32),
            pltpu.VMEM((width, size), f32),
            pltpu.VMEM(up.shape, bf16),
            pltpu.VMEM(down.shape, bf16),
            pltpu.VMEM((pairs, tile, tile), f32),
            pltpu.VMEM((pairs // 2, tile, tile), f32),
            pltpu.VMEM((pairs // 2, tile, tile), f32),
            pltpu.VMEM((wides - 1, pairs // 2, tile, tile), f32),
            dma((2, steps, 2, 2)),
            dma((2, steps, 2, 2)),
            dma((2, groups)),
            dma((1,)),
            dma((2, pairs // 2)),
            dma((2, wides - 1, pairs // 2)),
            dma((2, pairs // 2)),
            dma((2, wides - 1, size // 256)),
            dma((2, wides, size // 256)),
            pltpu.VMEM((wides, peers, rows, model), bf16),
            pltpu.VMEM((wides - 1, peers, rows, model), bf16),
            pltpu.VMEM((wides - 1, peers, rows, model), bf16),
            pltpu.VMEM((peers, rows, model), bf16),
            pltpu.VMEM((teams, peers, rows, 2 * (model // teams)), bf16),
            pltpu.VMEM((groups, rows, 2 * (model // teams)), bf16),
            dma((2, wides)),
            dma((2, wides - 1)),
            dma((2, teams)),
            dma((2, groups)),
        ],
        compiler_params=pltpu.CompilerParams(
            collective_id=0, has_side_effects=True, vmem_limit_bytes=52 * 2**20
        ),
        cost_estimate=pl.CostEstimate(
            flops=length, bytes_accessed=4 * length, transcendentals=0
        ),
    )(
        down, up, qkvo, small, input_part, grad_mid, result, mom_qkv, mom_out, mom_up, mom_down
    )


def dot(left, right):
    return jnp.dot(left, right, preferred_element_type=f32)

def dot_nt(left, right):
    return lax.dot_general(left, right, (((1,), (1,)), ((), ())), preferred_element_type=f32)

def middle_kernel(
    context_ref,
    x_ref,
    out_ref,
    up_ref,
    down_ref,
    bias_ref,
    vectors_ref,
    upstream_ref,
    valid_ref,
    hidden_ref,
    act_ref,
    grad_z_ref,
    grad_pre_ref,
    grad_mid_ref,
    own_grad_mid_ref,
    result_ref,
    vector_sum_ref,
    grad_down_ref,
    grad_up_ref,
    bias_sum_ref,
    slope,
    held,
    core_out,
    core_got,
    x_out,
    x_got,
    normed_one,
    own_hidden,
    normed_two,
    own_grad_z,
    vector_own,
    vector_got,
    core_sems,
    x_sems,
    spread_x_sems,
    spread_core_sems,
    vector_sems,
):
    mesh_type = pl.DeviceIdType.MESH
    index = lax.axis_index("dp")
    team = lax.axis_index("tensor")
    teams = lax.axis_size("tensor")
    wides = teams // 2
    x_at, core = team // 2, team % 2
    core_next = (index, x_at * 2 + 1 - core)
    x_up = (index, ((x_at + 1) % wides) * 2 + core)
    x_down = (index, ((x_at + wides - 1) % wides) * 2 + core)
    barrier = pltpu.get_barrier_semaphore()
    for hop in range(1, teams):
        pl.semaphore_signal(
            barrier, inc=1, device_id=(index, (team + hop) % teams), device_id_type=mesh_type
        )
    pl.semaphore_wait(barrier, teams - 1)
    sent = []

    def remote(src, dst, sems, at, target):
        return pltpu.make_async_remote_copy(
            src_ref=src,
            dst_ref=dst,
            send_sem=sems.at[(0, *at)],
            recv_sem=sems.at[(1, *at)],
            device_id=target,
            device_id_type=mesh_type,
        )

    def start(one):
        one.start()
        sent.append(one)

    def over_core(s, i):
        return remote(core_out.at[s, i], core_got.at[s, i], core_sems, (s, i), core_next)

    def over_x(s, hop):
        return remote(x_out.at[s, hop], x_got.at[s, hop], x_sems, (s, hop), x_up)

    def finish(s, filler):
        for hop in range(wides):
            i = wides - 1 - hop
            over_core(s, i).wait_recv()
            total = held[i] + wide(core_got[s, i])
            if hop > 0:
                if filler is not None:
                    filler()
                    filler = None
                over_x(s, hop - 1).wait_recv()
                total = total + wide(x_got[s, hop - 1])
            if i > 0:
                x_out[s, hop] = short(total)
                start(over_x(s, hop))
        return total

    def along_x(s, ref, i):
        return remote(ref.at[i], ref.at[i + 1], spread_x_sems, (s, i), x_down)

    def across(s, ref, i):
        return remote(ref.at[i], ref.at[wides + i], spread_core_sems, (s, i), core_next)

    def spread(s, ref):
        start(along_x(s, ref, 0))
        start(across(s, ref, 0))

    def arrive(s, ref, i):
        if i > 0:
            along_x(s, ref, i - 1).wait_recv()
            start(across(s, ref, i))
            if i < wides - 1:
                start(along_x(s, ref, i))
        across(s, ref, i).wait_recv()

    share = x_ref.shape[0]

    def pair(ref, i):
        return jnp.concatenate([ref[i], ref[wides + i]], 0)

    def put_pair(ref, i, value):
        ref[i] = value[:share]
        ref[wides + i] = value[share:]

    def keep(s, i, partial):
        core_out[s, i] = short(partial[share:])
        start(over_core(s, i))
        held[i] = partial[:share]

    def sums(value):
        return jnp.sum(value, axis=0, keepdims=True)

    for i in range(wides - 1, -1, -1):
        keep(0, i, dot(pair(context_ref, i), out_ref[...]))
    mid = wide(x_ref[...]) + finish(0, None) + vectors_ref[0:1, :]
    normed, inverse_one, hidden = norm_forward(mid, vectors_ref[1:2, :], vectors_ref[2:3, :])
    normed_one[...] = normed
    own_hidden[...] = hidden
    hidden_ref[0] = short(hidden)
    spread(0, hidden_ref)

    units = up_ref.shape[1]
    step = min(units, 512)
    for i in range(wides):
        arrive(0, hidden_ref, i)
        rows = pair(hidden_ref, i)
        for c in range(0, units, step):
            at = slice(c, c + step)
            pre = dot(rows, up_ref[:, at]) + bias_ref[:, at]
            phi = 0.5 + 0.5 * lax.erf(pre * math.sqrt(0.5))
            act = short(pre * phi)
            bend = phi + pre * jnp.exp(-0.5 * pre * pre) * (1.0 / math.sqrt(2.0 * math.pi))
            for r, part in ((i, slice(0, share)), (wides + i, slice(share, 2 * share))):
                act_ref[r, :, at] = act[part]
                slope[r, :, at] = bend[part]
        keep(1, i, dot(pair(act_ref, i), down_ref[...]))
    summed = own_hidden[...] + finish(1, None) + vectors_ref[3:4, :]
    gain_two = vectors_ref[4:5, :]
    normed, inverse_two, result = norm_forward(summed, gain_two, vectors_ref[5:6, :])
    result_ref[...] = short(result)
    upstream = wide(upstream_ref[...]) * valid_ref[...]
    grad_z = norm_backward(upstream, normed, inverse_two, gain_two)
    own_grad_z[...] = grad_z
    grad_z_ref[0] = short(grad_z)
    spread(1, grad_z_ref)
    vector_own[...] = jnp.zeros_like(vector_own)
    vector_own[3:4, :] = sums(grad_z)
    vector_own[4:5, :] = sums(upstream * normed)
    vector_own[5:6, :] = sums(upstream)

    for i in range(wides):
        arrive(1, grad_z_ref, i)
        rows = pair(grad_z_ref, i)
        for c in range(0, units, step):
            at = slice(c, c + step)
            grad = dot_nt(rows, down_ref[at, :])
            total = jnp.zeros((1, at.stop - at.start), f32)
            for r, part in ((i, slice(0, share)), (wides + i, slice(share, 2 * share))):
                low = short(grad[part] * slope[r, :, at])
                grad_pre_ref[r, :, at] = low
                total = total + sums(wide(low))
            bias_sum_ref[:, at] = total if i == 0 else bias_sum_ref[:, at] + total
        keep(2, i, dot_nt(pair(grad_pre_ref, i), up_ref[...]))

    def every(ref, at):
        return jnp.concatenate([ref[r, :, at] for r in range(teams)], 0)

    def down_filler():
        def one(k, carry):
            at = pl.ds(pl.multiple_of(k * 128, 128), 128)
            grad_down_ref[at, :] = short(mm_tn(every(act_ref, at), every(grad_z_ref, slice(None))))
            return carry

        lax.fori_loop(0, units // 128, one, 0)

    grad_hidden = own_grad_z[...] + finish(2, down_filler)
    grad_mid = norm_backward(grad_hidden, normed_one[...], inverse_one, vectors_ref[1:2, :])
    own_grad_mid_ref[...] = grad_mid
    grad_mid_ref[0] = short(grad_mid)
    spread(2, grad_mid_ref)
    vector_own[0:1, :] = sums(grad_mid)
    vector_own[1:2, :] = sums(grad_hidden * normed_one[...])
    vector_own[2:3, :] = sums(grad_hidden)

    def to_team(hop):
        return remote(
            vector_own, vector_got.at[hop], vector_sems, (hop,), (index, (team + hop) % teams)
        )

    for hop in range(1, teams):
        start(to_team(hop))

    def up_filler(k, carry):
        at = pl.ds(pl.multiple_of(k * 128, 128), 128)
        grad_up_ref[at, :] = short(mm_tn(every(hidden_ref, at), every(grad_pre_ref, slice(None))))
        return carry

    lax.fori_loop(0, hidden_ref.shape[2] // 128, up_filler, 0)
    for i in range(wides):
        arrive(2, grad_mid_ref, i)
    total = vector_own[...]
    for hop in range(1, teams):
        to_team(hop).wait_recv()
        total = total + vector_got[hop]
    vector_sum_ref[...] = total
    for one in sent:
        one.wait_send()


def middle(context, x_own, w_out, w_up, w_down, bias_up, vectors, upstream, valid):
    teams, share, width = context.shape
    model, units = w_up.shape
    wides = teams // 2
    dma = pltpu.SemaphoreType.DMA
    vmem = pl.BlockSpec(memory_space=pltpu.VMEM)
    rows = jax.ShapeDtypeStruct((teams, share, model), bf16)
    inner = jax.ShapeDtypeStruct((teams, share, units), bf16)
    own = pltpu.VMEM((share, model), f32)
    return pl.pallas_call(
        middle_kernel,
        name="middle",
        out_shape=(
            rows,
            inner,
            rows,
            inner,
            rows,
            jax.ShapeDtypeStruct((share, model), f32),
            jax.ShapeDtypeStruct((share, model), bf16),
            jax.ShapeDtypeStruct((8, model), f32),
            jax.ShapeDtypeStruct((units, model), bf16),
            jax.ShapeDtypeStruct((model, units), bf16),
            jax.ShapeDtypeStruct((1, units), f32),
        ),
        in_specs=[vmem] * 9,
        out_specs=[vmem] * 11,
        scratch_shapes=[
            pltpu.VMEM((teams, share, units), f32),
            pltpu.VMEM((wides, share, model), f32),
            pltpu.VMEM((3, wides, share, model), bf16),
            pltpu.VMEM((3, wides, share, model), bf16),
            pltpu.VMEM((3, wides - 1, share, model), bf16),
            pltpu.VMEM((3, wides - 1, share, model), bf16),
            own,
            own,
            own,
            own,
            pltpu.VMEM((8, model), f32),
            pltpu.VMEM((teams, 8, model), f32),
            dma((2, 3, wides)),
            dma((2, 3, wides - 1)),
            dma((2, 3, wides - 1)),
            dma((2, 3, wides)),
            dma((2, teams)),
        ],
        compiler_params=pltpu.CompilerParams(
            collective_id=1, has_side_effects=True, vmem_limit_bytes=48 * 2**20
        ),
        cost_estimate=pl.CostEstimate(
            flops=12 * teams * share * model * units,
            bytes_accessed=8 * model * units,
            transcendentals=0,
        ),
    )(context, x_own, w_out, w_up, w_down, bias_up.reshape(1, units), vectors, upstream, valid)


def polar_kernel(block, m_ref, o_ref, x_ref, gram_ref, low_ref, mix_ref):
    teams, size, width = m_ref.shape
    keep = o_ref.shape[1]
    bits = 256

    def rows(i):
        return pl.ds(pl.multiple_of(i * bits, bits), bits)

    def columns(j):
        return pl.ds(pl.multiple_of(j * block, block), block)

    def norm_step(i, total):
        for r in range(teams):
            part = wide(m_ref[r, rows(i), :])
            total = total + jnp.sum(part * part, axis=0, keepdims=True)
        return total

    total = lax.fori_loop(0, size // bits, norm_step, jnp.zeros((1, width), f32))
    scale = lax.rsqrt(jnp.sum(total, axis=1, keepdims=True) + 1e-07)

    def scale_step(i, carry):
        for r in range(teams):
            x_ref[0, rows(i), r * width : (r + 1) * width] = short(wide(m_ref[r, rows(i), :]) * scale)
        return carry

    lax.fori_loop(0, size // bits, scale_step, 0)

    def sweep(k, carry):
        now = k % 2
        x = x_ref.at[now]

        def gram_step(j, carry):
            gram = dot_nt(x[...], x[columns(j), :])
            gram_ref[:, columns(j)] = gram
            low_ref[:, columns(j)] = short(gram)
            return carry

        def mix_step(j, carry):
            power = dot(low_ref[...], low_ref[:, columns(j)])
            mix_ref[:, columns(j)] = short(coef_two * gram_ref[:, columns(j)] + coef_three * power)
            return carry

        def next_step(j, carry):
            mixed = dot(mix_ref[...], x[:, columns(j)])
            x_ref[1 - now, :, columns(j)] = short(coef_one * wide(x[:, columns(j)]) + mixed)
            return carry

        lax.fori_loop(0, size // block, gram_step, 0)
        lax.fori_loop(0, size // block, mix_step, 0)
        lax.fori_loop(0, jnp.where(k < 4, size // block, -(-keep // block)), next_step, 0)
        return carry

    lax.fori_loop(0, 5, sweep, 0)
    o_ref[...] = x_ref[1, :, :keep]


def factor_kernel(block, g_ref, o_ref, current_ref, poly_ref, half_ref, factor_ref):
    size = poly_ref.shape[0]
    tile = g_ref.shape[1]
    tiles = size // tile
    keep = o_ref.shape[1]
    first = lax.axis_index("tensor") * keep
    eye = lax.broadcasted_iota(jnp.int32, (tile, tile), 0) == lax.broadcasted_iota(
        jnp.int32, (tile, tile), 1
    )
    trace = jnp.zeros((1, 1), f32)
    for k, (i, j) in enumerate(tile_pairs(tiles)):
        if i == j:
            diagonal = jnp.where(eye, g_ref[k], 0.0)
            trace = trace + jnp.sum(jnp.sum(diagonal, axis=0, keepdims=True), axis=1, keepdims=True)
    scale = lax.rsqrt(trace + 1e-07)
    scale_two = scale * scale

    def store(slot, rows, columns, value):
        high = short(value)
        current_ref[slot, 0, rows, columns] = high
        current_ref[slot, 1, rows, columns] = short(value - wide(high))

    def span(i):
        return slice(i * tile, (i + 1) * tile)

    for k, (i, j) in enumerate(tile_pairs(tiles)):
        part = g_ref[k] * scale_two
        store(0, span(i), span(j), part)
        if i != j:
            store(0, span(j), span(i), part.T)

    def cols(j):
        return pl.ds(pl.multiple_of(j * block, block), block)

    def sweep(k, exact, exact_next, last):
        now = k % 2
        high_ref, low_ref = current_ref.at[now, 0], current_ref.at[now, 1]

        def poly_step(j, carry):
            power = dot(high_ref[...], high_ref[:, cols(j)])
            if last:
                power = power + dot(high_ref[...], low_ref[:, cols(j)])
            r = lax.broadcasted_iota(jnp.int32, (size, block), 0)
            c = lax.broadcasted_iota(jnp.int32, (size, block), 1) + j * block
            present = wide(high_ref[:, cols(j)]) + wide(low_ref[:, cols(j)])
            poly = coef_two * present + coef_three * power
            poly_ref[:, cols(j)] = short(poly + jnp.where(r == c, coef_one, 0.0))
            return carry

        def half_step(j, carry):
            half = dot(poly_ref[...], high_ref[:, cols(j)])
            if exact:
                half = half + dot(poly_ref[...], low_ref[:, cols(j)])
            high = short(half)
            half_ref[0, :, cols(j)] = high
            if exact_next:
                half_ref[1, :, cols(j)] = short(half - wide(high))
            return carry

        def next_step(j, carry):
            new = dot(half_ref[0], poly_ref[:, cols(j)])
            if exact_next:
                new = new + dot(half_ref[1], poly_ref[:, cols(j)])
            store(1 - now, slice(None), cols(j), new)
            return carry

        lax.fori_loop(0, size // block, poly_step, 0)
        if not last:
            lax.fori_loop(0, size // block, half_step, 0)
            lax.fori_loop(0, size // block, next_step, 0)

    def plain_sweep(k, carry):
        sweep(k, False, False, False)
        factor_ref[...] = short(dot(poly_ref[...], factor_ref[...]))
        return carry

    sweep(0, True, True, False)
    factor_ref[...] = poly_ref[:, pl.ds(pl.multiple_of(first, 128), keep)]
    sweep(1, True, False, False)
    factor_ref[...] = short(dot(poly_ref[...], factor_ref[...]))
    lax.fori_loop(2, 4, plain_sweep, 0)
    sweep(4, False, False, True)
    o_ref[...] = short(dot(poly_ref[...], factor_ref[...]) * scale)


def step_kernel(
    block,
    square_ref,
    tiles_ref,
    o_ref,
    x_ref,
    gram_ref,
    low_ref,
    mix_ref,
    current_ref,
    poly_ref,
    half_ref,
    factor_ref,
):
    index = lax.axis_index("dp")

    @pl.when(index < 4)
    def _():
        polar_kernel(block, square_ref, o_ref, x_ref, gram_ref, low_ref, mix_ref)

    @pl.when(jnp.logical_or(index == 4, index == 5))
    def _():
        factor_kernel(block, tiles_ref, o_ref, current_ref, poly_ref, half_ref, factor_ref)

    @pl.when(index > 5)
    def _():
        o_ref[...] = jnp.zeros_like(o_ref)


def orthogonal_columns(square, tiles):
    teams, size, width = square.shape
    vmem = pl.BlockSpec(memory_space=pltpu.VMEM)
    return pl.pallas_call(
        functools.partial(step_kernel, 512),
        name="orthogonal_columns",
        out_shape=jax.ShapeDtypeStruct((size, width), bf16),
        in_specs=[vmem] * 2,
        out_specs=vmem,
        scratch_shapes=[
            pltpu.VMEM((2, size, teams * width), bf16),
            pltpu.VMEM((size, size), f32),
            pltpu.VMEM((size, size), bf16),
            pltpu.VMEM((size, size), bf16),
            pltpu.VMEM((2, 2, size, size), bf16),
            pltpu.VMEM((size, size), bf16),
            pltpu.VMEM((2, size, size), bf16),
            pltpu.VMEM((size, width), bf16),
        ],
        compiler_params=pltpu.CompilerParams(vmem_limit_bytes=48 * 2**20),
        cost_estimate=pl.CostEstimate(
            flops=40 * size**3, bytes_accessed=8 * size * size, transcendentals=0
        ),
    )(square, tiles)


def body(
    layout,
    tokens,
    cotangent,
    lengths,
    packing,
    w_qkv,
    w_out,
    w_up,
    w_down,
    bias_qv,
    bias_up,
    vectors,
    mom_qkv,
    mom_out,
    mom_up,
    mom_down,
    mom_bias_qv,
    mom_bias_up,
    mom_vectors,
):
    inner, cores = layout
    groups = lax.axis_size("dp")
    teams = lax.axis_size("tensor")
    group = lax.axis_index("dp")
    team = lax.axis_index("tensor")
    outer, wides = groups // inner, teams // cores
    count = tokens.shape[0]
    per_peer = count // groups
    share = count // teams
    width = D // teams
    all_tokens = count * groups

    outer_ring = Ring("dp", (outer, inner), 0)
    inner_ring = Ring("dp", (outer, inner), 1)
    outer_at, inner_at = outer_ring.place(group), inner_ring.place(group)
    x_ring = Ring("tensor", (wides, cores), 0)
    core_ring = Ring("tensor", (wides, cores), 1)
    x_at, core_at = x_ring.place(team), core_ring.place(team)

    def team_of(rank):
        return ((x_at + rank % wides) % wides) * cores + (core_at + rank // wides) % cores

    def to_relative(value, size, axis=0):
        return jnp.concatenate([cut(value, team_of(r), size, axis) for r in range(teams)], axis)

    def to_given(value, size, axis=0):
        parts = []
        for other in range(teams):
            rank = ((other % cores - core_at) % cores) * wides + (other // cores - x_at) % wides
            parts.append(cut(value, rank, size, axis))
        return jnp.concatenate(parts, axis)

    def spread_list(piece, ring_x=x_ring, ring_core=core_ring):
        line = [piece]
        for _ in range(wides - 1):
            line.append(ring_x.send(line[-1], -1))
        pieces = list(line)
        for hop in range(1, cores):
            pieces += [ring_core.send(p, -hop) for p in line]
        return pieces

    def spread_columns(piece):
        return to_given(jnp.concatenate(spread_list(piece), 1), piece.shape[1], 1)

    def own_rows(value):
        return cut(value, team, share, 0)

    position = jnp.arange(count, dtype=jnp.int32)
    peer = jnp.arange(groups, dtype=jnp.int32)
    packed = packing.reshape(groups, count)
    mine_packed = lax.dynamic_index_in_dim(packed, group, 0, keepdims=False)
    offset = packed - group * count
    offset_mine = mine_packed[None, :] - peer[:, None] * count
    masks = jnp.concatenate(
        [
            jnp.logical_and(offset >= 0, offset < count),
            jnp.logical_and(offset_mine >= 0, offset_mine < count),
        ],
        0,
    )
    before = (position[:, None] < position[None, :]).astype(bf16)
    rank = mm(masks.astype(bf16), before).astype(jnp.int32)
    key = jnp.where(masks, rank, -1)
    value = jnp.concatenate(
        [offset, jnp.broadcast_to(position[None, :], (groups, count))], 0
    )
    slot_in_message = jnp.arange(per_peer, dtype=jnp.int32)
    picked = jnp.sum(
        jnp.where(key[:, None, :] == slot_in_message[None, :, None], value[:, None, :], 0), axis=-1
    )
    rows_sent = picked[:groups].reshape(count)
    slots = picked[groups:].reshape(count)
    choose = (rows_sent[:, None] == position[None, :]).astype(bf16)

    length_row = lengths[0]
    end_one = length_row[0]
    end_two = end_one + length_row[1]
    end_all = end_two + length_row[2]
    segments = (
        (slots >= end_one).astype(jnp.int32)
        + (slots >= end_two).astype(jnp.int32)
        + (slots >= end_all).astype(jnp.int32)
        + jnp.maximum(slots - end_all, 0)
    )
    valid_own = own_rows((slots < end_all).astype(f32))
    segments = to_relative(segments, share)

    own_columns = jnp.concatenate([cut(tokens, team, width, 1), cut(cotangent, team, width, 1)], 1)
    sent = short(mm(choose, own_columns)).reshape(groups, per_peer, 2 * width)
    got = lax.all_to_all(sent, "dp", split_axis=0, concat_axis=0, tiled=True)
    got = got.reshape(count, 2 * width)

    packed_x = to_relative(spread_columns(got[:, :width]), share)
    turns = []
    for hop in range(teams):
        block = cut(got[:, width:], (team + hop) % teams, share, 0)
        if hop > 0:
            block = lax.ppermute(block, "tensor", [(i, (i + hop) % teams) for i in range(teams)])
        turns.append(block)
    turns = jnp.concatenate(turns, 1)
    grad_rows = jnp.concatenate(
        [cut(turns, (team - other) % teams, width, 1) for other in range(teams)], 1
    )

    wqkv_low = short(w_qkv)
    wout_low = short(w_out)
    wup_low = short(w_up)
    wdown_low = short(w_down)
    heads = width // HEAD
    score_scale = HEAD ** (-0.5)
    wqkv_wide = jnp.concatenate([wqkv_low[k] for k in range(3)], 1)
    bias_wide = jnp.concatenate([bias_qv[0], jnp.zeros((width,), f32), bias_qv[1]])
    projected = short(mm(packed_x, wqkv_wide) + bias_wide)
    queries, keys, values = (
        projected[:, k * width : (k + 1) * width].reshape(count, heads, HEAD) for k in range(3)
    )
    raw = jnp.einsum("qhd,khd->hqk", queries, keys, preferred_element_type=f32)
    same = segments[:, None] == segments[None, :]
    masked = jnp.where(same[None], raw * score_scale, masked_score)
    exponent = jnp.exp(masked - jnp.max(masked, axis=-1, keepdims=True))
    probs = exponent / jnp.sum(exponent, axis=-1, keepdims=True)
    probs_low = short(probs)
    context = short(
        jnp.einsum("hqk,khd->qhd", probs_low, values, preferred_element_type=f32)
    ).reshape(count, width)
    (
        hidden_low,
        act_low,
        grad_z_low,
        grad_pre,
        grad_mid_low,
        grad_mid,
        result,
        vector_part,
        grad_down,
        grad_up,
        grad_bias_up,
    ) = middle(
        context.reshape(teams, share, width),
        packed_x[:share],
        wout_low,
        wup_low,
        wdown_low,
        bias_up,
        vectors,
        grad_rows,
        valid_own[:, None],
    )
    grad_bias_up = grad_bias_up[0]
    grad_mid_low = grad_mid_low.reshape(count, D)
    vector_part = vector_part[:6]
    grad_out_t = short(mm_tn(grad_mid_low, context))
    grad_context = short(mm_nt(grad_mid_low, wout_low)).reshape(count, heads, HEAD)
    grad_probs = jnp.einsum("qhd,khd->hqk", grad_context, values, preferred_element_type=f32)
    weighted = jnp.sum(probs * grad_probs, axis=-1, keepdims=True)
    grad_scores = short(probs * (grad_probs - weighted))
    grad_values = short(
        jnp.einsum("hqk,qhd->khd", probs_low, grad_context, preferred_element_type=f32)
    ).reshape(count, width)
    grad_keys = short(
        jnp.einsum("hqk,qhd->khd", grad_scores, queries, preferred_element_type=f32) * score_scale
    ).reshape(count, width)
    grad_queries = short(
        jnp.einsum("hqk,khd->qhd", grad_scores, keys, preferred_element_type=f32) * score_scale
    ).reshape(count, width)
    grad_bias_pair = jnp.stack(
        [jnp.sum(grad_queries, axis=0, dtype=f32), jnp.sum(grad_values, axis=0, dtype=f32)]
    )
    grad_projected = jnp.concatenate([grad_queries, grad_keys, grad_values], 1)
    grad_qkvo = jnp.concatenate(
        [
            short(mm_tn(packed_x, grad_projected)),
            grad_out_t,
        ],
        1,
    )
    input_part = mm_nt(grad_projected, wqkv_wide)
    columns = D
    small = jnp.concatenate(
        [vector_part.reshape(-1), grad_bias_pair.reshape(-1), grad_bias_up.reshape(-1)]
    )
    rows_small = -(-small.size // (16 * columns)) * 16
    small = jnp.pad(short(small), (0, rows_small * columns - small.size)).reshape(rows_small, columns)
    down_sum, up_sum, qkvo_sum, small_sum, square, gram_tiles, given = sums_over_dp(
        inner,
        grad_down,
        grad_up,
        grad_qkvo,
        small,
        short(input_part).reshape(teams, groups // teams, per_peer, D),
        grad_mid.reshape(groups // teams, per_peer, D),
        result.reshape(groups // teams, per_peer, D),
        (mom_qkv, mom_out, mom_up, mom_down),
    )
    pieces = spread_list(short(mm_tn(choose, given.reshape(count, 2 * width))))
    output = to_given(jnp.concatenate([p[:, :width] for p in pieces], 1), width, 1)
    grad_tokens = wide(to_given(jnp.concatenate([p[:, width:] for p in pieces], 1), width, 1))

    qkvo_sum = wide(qkvo_sum)
    small_sum = small_sum.reshape(-1)
    gradients = (
        jnp.stack([qkvo_sum[:, k * width : (k + 1) * width] for k in range(3)]),
        qkvo_sum[:, 3 * width :].T,
        wide(up_sum),
        wide(down_sum),
        small_sum[6 * D : 6 * D + 2 * width].reshape(2, width),
        small_sum[6 * D + 2 * width : 6 * D + 2 * width + bias_up.shape[0]],
        small_sum[: 6 * D].reshape(6, D),
    )
    moments_old = (mom_qkv, mom_out, mom_up, mom_down, mom_bias_qv, mom_bias_up, mom_vectors)
    moments = tuple(
        momentum_decay * old + grad for old, grad in zip(moments_old, gradients)
    )

    up_low, down_low = short(moments[2]), short(moments[3])

    stepped = orthogonal_columns(square, gram_tiles)
    dp_rows = D // groups
    steps = lax.all_to_all(
        stepped.reshape(groups, dp_rows, width), "dp", split_axis=0, concat_axis=0, tiled=True
    )
    factors = spread_columns(steps[4:6].reshape(2 * dp_rows, width))

    def mine(values_, dim):
        return lax.dynamic_slice_in_dim(values_, group * dp_rows, dp_rows, dim)

    short_rate = rate_matrix * 0.2 * math.sqrt(D)
    long_rate = rate_matrix * 0.2 * math.sqrt(w_up.shape[1] * teams)
    masters = [
        mine(w_qkv, 1) - short_rate * wide(steps[:3]),
        mine(w_out, 1) - short_rate * wide(steps[3]).T,
        mine(w_up, 0) - long_rate * mm(factors[:dp_rows], up_low),
        mine(w_down, 1) - long_rate * mm_nt(down_low, factors[dp_rows:]),
    ]
    rate_vector = 0.2 / math.sqrt(all_tokens)
    for param, moment in zip((bias_qv, bias_up, vectors), moments[4:]):
        masters.append(param - rate_vector * moment)

    return (output, grad_tokens, *gradients, *moments, *masters)


def axis_layout(mesh):
    grid = mesh.devices
    groups, teams = grid.shape
    places = [getattr(d, "coords", None) for d in grid[:, 0]]
    inner = 2 if groups % 2 == 0 else 1
    if places[0] is not None:
        moved = [k for k in range(3) if places[0][k] != places[1][k]]
        fixed = [k for k in range(3) if k not in moved]
        inner = 1
        while inner < groups and all(places[inner][k] == places[0][k] for k in fixed):
            inner += 1
        if groups % inner:
            inner = 1
    return inner, (2 if teams % 2 == 0 else 1)


def solution(mesh):
    grads = (
        P(None, None, "tensor"),
        P("tensor", None),
        P(None, "tensor"),
        P("tensor", None),
        P(None, "tensor"),
        P("tensor"),
        P(),
    )
    rows = P("dp", None)
    return jax.shard_map(
        functools.partial(body, axis_layout(mesh)),
        mesh=mesh,
        in_specs=(rows, rows, rows, P(), *grads, *grads),
        out_specs=(
            rows,
            rows,
            *grads,
            *grads,
            P(None, "dp", "tensor"),
            P("tensor", "dp"),
            P("dp", "tensor"),
            P("tensor", "dp"),
            P(None, "tensor"),
            P("tensor"),
            P(),
        ),
        check_vma=False,
    )
```
